128 devices in a mesh: row: 16 (over z_hi, y, core), col: 8 (over z_lo, x).
Axes of the slice: x: 4, y: 4, z: 4 (z_hi: 2, z_lo: 2; z = z_hi * 2 + z_lo), core: 2. Of those that a mesh axis runs over, the one named last changes fastest.
Arguments:
- tiles: bfloat16 [128, 128, 1536], P('row', 'col'), may hold values from -6 to 6
- tissue: int32 [128, 128], P('row', 'col'), may hold values from 0 to 1, as said below
- project_in: bfloat16 [1536, 2304], P(('row', 'col')), as said below
- project_out: bfloat16 [768, 1536], P(('row', 'col')), may hold values from -0.21875 to 0.21875
- grad_layer: bfloat16 [128, 128, 1536], P('row', 'col'), may hold values from -6 to 6
Outputs:
- layer_out: bfloat16 [128, 128, 1536], P('row', 'col')
- grad_tiles: bfloat16 [128, 128, 1536], P('row', 'col')
- grad_project_in: float32 [1536, 2304], P(('row', 'col'))
- grad_project_out: float32 [768, 1536], P(('row', 'col'))
The draws below stay inside these ranges and needn't reach their ends.
Inputs may be any that keep to these rules, and one draw needn't show every extreme that they name: 1 marks a tissue tile, 0 a background tile; tissue lies in patches. `project_in`: query, key and value projections side by side along the second dimension.
All inputs are finite; a program needn't handle non-finite values.
Results may differ from the reference program's by a relative error of at most 0.009.
Values may be sent and summed in bfloat16 or wider, within the bound.
No kernel may reach another device: no remote copies, remote signals or barrier semaphores. Data moves between devices by JAX's collectives and lax.ppermute only.
A program may use at most 128 MiB of HBM per device.

```python
import jax
import jax.numpy as jnp
from jax import lax

D = 1536
HEADS = 12
HEAD_DIM = 64
WINDOW = 7
DH = 768
ROWS = 128
COLS = 128


def draw_tissue(key, part):
    key = jax.random.fold_in(key, 11)
    coarse_key, fine_key = jax.random.split(key)
    levels = jax.random.randint(coarse_key, (ROWS // 4 + 1, COLS // 4 + 1), 0, 5)
    levels = jnp.repeat(jnp.repeat(levels, 4, axis=0), 4, axis=1)[:ROWS, :COLS]
    rolls = jax.random.randint(fine_key, (ROWS, COLS), 0, 4)
    return (rolls < levels).astype(jnp.int32)


def draw_project_in(key, part):
    key = jax.random.fold_in(key, 23)
    base_key = jax.random.fold_in(key, 0)
    weights = jax.random.normal(base_key, (D, 3 * DH), jnp.float32) * D ** (-0.5)
    return weights.astype(jnp.bfloat16)


def spiked(entries, key, source, target, shards_of, factor):
    def block_of(dim):
        return (jnp.arange(entries.shape[dim]) // (entries.shape[dim] // shards_of)).reshape((-1,) + (1,) * (entries.ndim - 1 - dim))

    one_side = jax.random.permutation(key, shards_of)[block_of(target)]
    other_side = (block_of(target) + shards_of // 2) % shards_of
    return jnp.where((block_of(source) == one_side) | (block_of(source) == other_side), factor * entries, entries)


def block_scale(key, shape, pieces, smallest, top_value):
    factor_of = 1.0
    for position, parts in pieces:
        steps = jax.random.uniform(jax.random.fold_in(jax.random.fold_in(key, 6), position), (parts,), jnp.float32, smallest / len(pieces), top_value / len(pieces))
        factor_of = factor_of * jnp.repeat(jnp.exp(steps), shape[position] // parts).reshape((-1,) + (1,) * (len(shape) - 1 - position))
    return factor_of


def noise(key, extent, spread, reach, pieces=(), kind=jnp.bfloat16):
    entries = jax.random.normal(key, extent, jnp.float32) * spread
    if len(pieces) > 0:
        entries = block_scale(key, extent, pieces, -0.22, 0.18) * entries
    return jnp.clip(entries, min=-reach, max=reach).astype(kind)


def gaussian_with(rng, dims, scale, reach, cuts, heavy, kind=jnp.bfloat16):
    drawn = scale * jax.random.normal(rng, dims, jnp.float32)
    if cuts:
        drawn = drawn * block_scale(rng, dims, cuts, -0.22, 0.18)
    return jnp.clip(spiked(drawn, jax.random.fold_in(rng, 3), *heavy), -reach, reach).astype(kind)


def setup_inputs(seed: int = 0) -> dict:
    arg_keys = jax.random.split(jax.random.key(seed), 6)
    return {
        "tiles": gaussian_with(arg_keys[0], (ROWS, COLS, D), 1.0, 6.0, ((0, 16), (1, 8)), (0, 2, 16, 2.0)),
        "tissue": draw_tissue(jax.random.fold_in(arg_keys[5], 71), 0),
        "project_in": draw_project_in(jax.random.fold_in(arg_keys[5], 71), 0),
        "project_out": noise(arg_keys[3], (DH, D), DH ** -0.5, 0.21875, ((0, 128),)),
        "grad_layer": noise(arg_keys[4], (ROWS, COLS, D), 1.0, 6.0, ((0, 16), (1, 8))),
    }


epsilon = 1e-05
masked_score = -1e+30

def normalize(values):
    center = values - lax.optimization_barrier(jnp.mean(values, axis=-1, keepdims=True))
    inverse = lax.rsqrt(lax.optimization_barrier(jnp.mean(center * center, axis=-1, keepdims=True)) + epsilon)
    return (center * inverse, inverse)

def reference(tiles, tissue, project_in, project_out, grad_layer):
    tokens = ROWS * COLS
    scale = HEAD_DIM ** (-0.5)
    flat_tiles = tiles.reshape(tokens, D).astype(jnp.float32)
    normed, inverse = normalize(flat_tiles)
    hidden = normed.astype(jnp.bfloat16)
    packed = jnp.dot(hidden, project_in, preferred_element_type=jnp.float32).astype(jnp.bfloat16)
    packed = packed.reshape(ROWS, COLS, 3, HEADS, HEAD_DIM)
    query = packed[:, :, 0].astype(jnp.float32)
    key_all = packed[:, :, 1]
    value_all = packed[:, :, 2]
    row_start = jnp.clip(jnp.arange(ROWS, dtype=jnp.int32) - WINDOW // 2, 0, ROWS - WINDOW)
    col_start = jnp.clip(jnp.arange(COLS, dtype=jnp.int32) - WINDOW // 2, 0, COLS - WINDOW)

    def neighbours(offset):
        row_index = (row_start + offset // WINDOW)[:, None]
        col_index = (col_start + offset % WINDOW)[None, :]
        return (key_all[row_index, col_index], value_all[row_index, col_index], tissue[row_index, col_index], row_index, col_index)
    score_list = []
    for offset in range(WINDOW * WINDOW):
        keys, values, alive, row_index, col_index = neighbours(offset)
        raw = jnp.einsum('ijhd,ijhd->ijh', query, keys.astype(jnp.float32)) * scale
        score_list.append(jnp.where(alive[:, :, None] > 0, raw, masked_score))
    scores = jnp.stack(score_list, axis=0)
    highest = lax.optimization_barrier(jnp.max(scores, axis=0, keepdims=True))
    expon = jnp.exp(scores - highest)
    prob = expon / lax.optimization_barrier(jnp.sum(expon, axis=0, keepdims=True))
    weights = prob.astype(jnp.bfloat16)
    mixed = jnp.zeros((ROWS, COLS, HEADS, HEAD_DIM), jnp.float32)
    for offset in range(WINDOW * WINDOW):
        keys, values, alive, row_index, col_index = neighbours(offset)
        mixed = mixed + weights[offset][..., None].astype(jnp.float32) * values.astype(jnp.float32)
    attention = mixed.astype(jnp.bfloat16).reshape(tokens, DH)
    projected = jnp.dot(attention, project_out, preferred_element_type=jnp.float32)
    live = tissue.reshape(tokens, 1).astype(jnp.float32)
    layer_out = (flat_tiles + projected * live).astype(jnp.bfloat16).reshape(ROWS, COLS, D)
    grad_flat = grad_layer.reshape(tokens, D).astype(jnp.float32)
    grad_proj = (grad_flat * live).astype(jnp.bfloat16)
    grad_project_out = jnp.dot(attention.T, grad_proj, preferred_element_type=jnp.float32)
    grad_attention = jnp.dot(grad_proj, project_out.T, preferred_element_type=jnp.float32).astype(jnp.bfloat16)
    grad_attn4 = grad_attention.reshape(ROWS, COLS, HEADS, HEAD_DIM).astype(jnp.float32)
    attn4 = attention.reshape(ROWS, COLS, HEADS, HEAD_DIM).astype(jnp.float32)
    delta = jnp.einsum('ijhd,ijhd->ijh', grad_attn4, attn4)
    grad_query = jnp.zeros((ROWS, COLS, HEADS, HEAD_DIM), jnp.float32)
    grad_key = jnp.zeros((ROWS, COLS, HEADS, HEAD_DIM), jnp.float32)
    grad_value = jnp.zeros((ROWS, COLS, HEADS, HEAD_DIM), jnp.float32)
    for offset in range(WINDOW * WINDOW):
        keys, values, alive, row_index, col_index = neighbours(offset)
        grad_prob = jnp.einsum('ijhd,ijhd->ijh', grad_attn4, values.astype(jnp.float32))
        grad_score = prob[offset] * (grad_prob - delta) * scale
        grad_query = grad_query + grad_score[..., None] * keys.astype(jnp.float32)
        grad_key = grad_key.at[row_index, col_index].add(grad_score[..., None] * query)
        grad_value = grad_value.at[row_index, col_index].add(weights[offset][..., None].astype(jnp.float32) * grad_attn4)
    grad_packed = jnp.stack([grad_query, grad_key, grad_value], axis=2).reshape(tokens, 3 * DH).astype(jnp.bfloat16)
    grad_project_in = jnp.dot(hidden.T, grad_packed, preferred_element_type=jnp.float32)
    grad_hidden = jnp.dot(grad_packed, project_in.T, preferred_element_type=jnp.float32)
    grad_norm = inverse * (grad_hidden - lax.optimization_barrier(jnp.mean(grad_hidden, axis=-1, keepdims=True)) - normed * lax.optimization_barrier(jnp.mean(grad_hidden * normed, axis=-1, keepdims=True)))
    grad_tiles = (grad_flat + grad_norm).astype(jnp.bfloat16).reshape(ROWS, COLS, D)
    return (layer_out, grad_tiles, grad_project_in, grad_project_out)
```

```python
import jax
import jax.numpy as jnp
from jax import lax
from jax.experimental import pallas as pl
from jax.experimental.pallas import tpu as pltpu
from jax.sharding import Mesh, PartitionSpec as P

HEAD_DIM = 64
WINDOW = 7
D = 1536
DH = 768
HALF = DH // 2
GRID = 128
SIDE = 16
KEY_ROWS = 28
KEY_COLS = 32
QUERY_ROWS = 22
QUERY_COLS = 24
LANE = 128

AXES = ("zh", "y", "c", "zl", "x")
STAGES = (("z", "y", "x"), ("x", "z", "y"))

epsilon = 1e-05
masked_score = -1e30
outside_score = -3e30
open_score = 3e38

f32 = jnp.float32
bf16 = jnp.bfloat16


def device(x, y, z, c):
    return (((z // 2 * 4 + y) * 2 + c) * 2 + z % 2) * 4 + x


def stage_pairs(stage, shift):
    pairs = []
    for x in range(4):
        for y in range(4):
            for z in range(4):
                for c in range(2):
                    place = {"x": x, "y": y, "z": z}
                    axis = STAGES[c][stage]
                    place[axis] = (place[axis] + shift) % 4
                    pairs.append((device(x, y, z, c), device(place["x"], place["y"], place["z"], c)))
    return pairs


def shifted(value, stage, shift):
    return lax.ppermute(value, AXES, stage_pairs(stage, shift))


def swap_cores(value):
    return lax.ppermute(value, "c", [(0, 1), (1, 0)])


def row_neighbour(value):
    pairs = [(r, r + 1 if r % 2 else r - 1) for r in range(16)]
    return lax.ppermute(value, ("zh", "y", "c"), [(a, b) for a, b in pairs if 0 <= b < 16])


def col_neighbour(value, step):
    pairs = [(i, i + step) for i in range(8)]
    return lax.ppermute(value, ("zl", "x"), [(a, b) for a, b in pairs if 0 <= b < 8])


def gather_stage(block, stage):
    far = shifted(block, stage, 2)
    near = shifted(block, stage, 1)
    back = shifted(block, stage, 3)
    return [block, near, far, back]


def scatter_stage(chunks, stage):
    far = shifted(chunks[2], stage, 2)
    near = shifted(chunks[1], stage, 3)
    back = shifted(chunks[3], stage, 1)
    return (chunks[0].astype(f32) + near.astype(f32)) + (far.astype(f32) + back.astype(f32))


def by_core(core, mine, other, axis):
    return jnp.where(
        core == 0,
        jnp.concatenate([mine, other], axis=axis),
        jnp.concatenate([other, mine], axis=axis),
    )


def normalize(values):
    center = values - jnp.mean(values, axis=-1, keepdims=True)
    inverse = lax.rsqrt(jnp.mean(center * center, axis=-1, keepdims=True) + epsilon)
    return (center * inverse, inverse)


def attention_kernel(base_ref, packed_ref, grad_ref, alive_ref, col_ref, attn_out, grads_out, dk, dv, attn, dq):
    base = base_ref[0]
    width = 2 * QUERY_COLS
    span = 8 * KEY_COLS
    dk[...] = jnp.zeros_like(dk)
    dv[...] = jnp.zeros_like(dv)
    key_line = lax.broadcasted_iota(jnp.int32, (1, span), 1) // KEY_COLS
    low = lax.broadcasted_iota(jnp.int32, (width, LANE), 1) < HEAD_DIM
    low2 = jnp.concatenate([low, jnp.logical_not(low)], axis=0)

    def block(i, carry):
        row = base - 3 + 2 * i
        start = jnp.clip(row - 3, 0, GRID - 8)
        local = start - (base - 6)
        alive = alive_ref[pl.ds(local, 1), :]
        key_row = key_line + start
        caps = []
        for step in range(2):
            first = jnp.clip(row + step - 3, 0, GRID - WINDOW)
            inside = jnp.logical_and(key_row >= first, key_row < first + WINDOW)
            caps.append(jnp.minimum(col_ref[...], jnp.where(inside, alive, outside_score)))
        cap = jnp.concatenate(caps + caps, axis=0)
        keys_at = pl.ds(pl.multiple_of(local * KEY_COLS, KEY_COLS), span)
        query_at = pl.multiple_of((3 + 2 * i) * KEY_COLS, KEY_COLS)
        block_at = pl.ds(pl.multiple_of(i * width, width), width)
        for g in range(3):
            q_lanes = pl.ds(g * LANE, LANE)
            k_lanes = pl.ds(HALF + g * LANE, LANE)
            v_lanes = pl.ds(2 * HALF + g * LANE, LANE)
            key = packed_ref[keys_at, k_lanes]
            value = packed_ref[keys_at, v_lanes]
            lines = packed_ref[pl.ds(query_at, 2 * KEY_COLS), q_lanes].astype(f32) * HEAD_DIM ** (-0.5)
            query = jnp.concatenate([lines[:QUERY_COLS], lines[KEY_COLS : KEY_COLS + QUERY_COLS]], axis=0)
            grad = grad_ref[block_at, q_lanes].astype(f32)
            query2 = jnp.where(low2, jnp.concatenate([query, query], axis=0), 0.0).astype(bf16)
            grad2f = jnp.where(low2, jnp.concatenate([grad, grad], axis=0), 0.0)
            grad2 = grad2f.astype(bf16)
            contract = (((1,), (1,)), ((), ()))
            raw = lax.dot_general(query2, key, contract, preferred_element_type=f32)
            scores = jnp.minimum(raw, cap)
            expon = jnp.exp(scores - jnp.max(scores, axis=1, keepdims=True))
            prob = expon * (1.0 / jnp.sum(expon, axis=1, keepdims=True))
            weights = prob.astype(bf16)
            mixed2 = jnp.dot(weights, value, preferred_element_type=f32).astype(bf16).astype(f32)
            attn[block_at, q_lanes] = jnp.where(low, mixed2[:width], mixed2[width:])
            delta = jnp.sum(grad2f * mixed2, axis=1, keepdims=True)
            grad_prob = lax.dot_general(grad2, value, contract, preferred_element_type=f32)
            grad_score = (prob * (grad_prob - delta)).astype(bf16)
            grad_q = jnp.dot(grad_score, key, preferred_element_type=f32)
            dq[block_at, q_lanes] = jnp.where(low, grad_q[:width], grad_q[width:])
            over = (((0,), (0,)), ((), ()))
            dk[keys_at, q_lanes] += lax.dot_general(grad_score, query2, over, preferred_element_type=f32)
            dv[keys_at, q_lanes] += lax.dot_general(weights, grad2, over, preferred_element_type=f32)
        return carry

    lax.fori_loop(0, QUERY_ROWS // 2, block, 0)
    for r in range(SIDE):
        own = pl.ds(r * SIDE, SIDE)
        at_query = pl.ds((r + 3) * QUERY_COLS, SIDE)
        at_key = pl.ds((r + 6) * KEY_COLS, SIDE)
        attn_out[own, :] = attn[at_query, :].astype(bf16)
        grads_out[own, :HALF] = (dq[at_query, :] * HEAD_DIM ** (-0.5)).astype(bf16)
        grads_out[own, HALF : 2 * HALF] = dk[at_key, :].astype(bf16)
        grads_out[own, 2 * HALF :] = dv[at_key, :].astype(bf16)


def attend(base, packed, grad_attention, alive, columns):
    vmem = pl.BlockSpec(memory_space=pltpu.VMEM)
    return pl.pallas_call(
        attention_kernel,
        out_shape=(
            jax.ShapeDtypeStruct((SIDE * SIDE, HALF), bf16),
            jax.ShapeDtypeStruct((SIDE * SIDE, 3 * HALF), bf16),
        ),
        in_specs=[pl.BlockSpec(memory_space=pltpu.SMEM), vmem, vmem, vmem, vmem],
        out_specs=(vmem, vmem),
        scratch_shapes=[
            pltpu.VMEM((KEY_ROWS * KEY_COLS, HALF), f32),
            pltpu.VMEM((KEY_ROWS * KEY_COLS, HALF), f32),
            pltpu.VMEM((QUERY_ROWS * QUERY_COLS, HALF), f32),
            pltpu.VMEM((QUERY_ROWS * QUERY_COLS, HALF), f32),
        ],
        compiler_params=pltpu.CompilerParams(vmem_limit_bytes=32 * 1024 * 1024),
        cost_estimate=pl.CostEstimate(flops=2 * 10**9, bytes_accessed=4 * 10**6, transcendentals=10**6),
    )(base, packed, grad_attention, alive, columns)


def feature_places(core, x, y, z):
    place = jnp.arange(D, dtype=jnp.int32)
    step = [(place // 24) % 4, (place // 96) % 4, place // 384]
    here = {"x": x, "y": y, "z": z}
    found = {}
    for name in ("x", "y", "z"):
        mine = [lax.rem(here[name] - step[STAGES[c].index(name)] + 4, 4) for c in range(2)]
        found[name] = jnp.where(core == 0, mine[0], mine[1])
    inner = place % 24
    high, low = found["z"] // 2, found["z"] % 2

    def owner(side):
        return (((high * 4 + found["y"]) * 2 + side) * 2 + low) * 4 + found["x"]

    feature_in = owner(inner // 12) * 12 + inner % 12
    row_out = owner(inner % 12 // 6) * 6 + inner % 6 + inner // 12 * DH
    return feature_in, row_out


def body(tiles, tissue, project_in, project_out, grad_layer):
    zh, y, core, zl, x = [lax.axis_index(name) for name in AXES]
    z = zh * 2 + zl
    tokens = 8 * SIDE
    contract_last = (((1,), (1,)), ((), ()))
    contract_first = (((0,), (0,)), ((), ()))

    halves = project_in.reshape(12, 3, 2, HALF)
    first, second = halves[:, :, 0].reshape(12, 3 * HALF), halves[:, :, 1].reshape(12, 3 * HALF)
    out_first, out_second = project_out[:, :DH], project_out[:, DH:]

    def shard(of_in, of_out):
        return jnp.concatenate([of_in, of_out.reshape(6, 2, HALF).transpose(1, 0, 2).reshape(12, HALF)], axis=1)

    shard_first, shard_second = shard(first, out_first), shard(second, out_second)
    mine = jnp.where(core == 0, shard_first, shard_second)
    other = swap_cores(jnp.where(core == 0, shard_second, shard_first))
    pair_in = by_core(core, mine[:, : 3 * HALF], other[:, : 3 * HALF], 0)
    mine_out, other_out = mine[:, 3 * HALF :].reshape(2, 6, HALF), other[:, 3 * HALF :].reshape(2, 6, HALF)
    pair_out = by_core(core, mine_out, other_out, 1).reshape(24, HALF)
    block = jnp.concatenate([pair_in, pair_out], axis=1)
    for stage in range(3):
        block = jnp.concatenate(gather_stage(block, stage), axis=0)
    weights_in, weights_out = block[:, : 3 * HALF], block[:, 3 * HALF :]

    flat_tiles = tiles.reshape(tokens, D).astype(f32)
    normed, inverse = normalize(flat_tiles)
    live = tissue.reshape(tokens, 1).astype(f32)
    grad_flat = grad_layer.reshape(tokens, D).astype(f32)
    tissue_lanes = jnp.broadcast_to(live.astype(bf16), (tokens, LANE))
    own_hidden = jnp.concatenate([normed.astype(bf16), tissue_lanes], axis=1).reshape(8, SIDE, D + LANE)
    own_grad = jnp.concatenate([(grad_flat * live).astype(bf16), tissue_lanes], axis=1).reshape(8, SIDE, D + LANE)
    sent = jnp.where(
        core == 1,
        jnp.concatenate([own_hidden[2:], own_grad[5:]], axis=0),
        jnp.concatenate([own_hidden[:6], own_grad[:3]], axis=0),
    )
    got = row_neighbour(sent)
    a = jnp.where(
        core == 0, jnp.concatenate([got[:6], own_hidden], axis=0), jnp.concatenate([own_hidden, got[:6]], axis=0)
    )
    b = jnp.where(
        core == 0, jnp.concatenate([got[6:], own_grad], axis=0), jnp.concatenate([own_grad, got[6:]], axis=0)
    )

    def columns_of(a_part, b_part):
        return jnp.concatenate([a_part.reshape(84, D + LANE), b_part.reshape(33, D + LANE)], axis=0)

    left = col_neighbour(columns_of(a[:, 10:], b[:, 13:]), 1)
    right = col_neighbour(columns_of(a[:, :6], b[:, :3]), -1)
    left_a, left_b = left[:84].reshape(14, 6, D + LANE), left[84:].reshape(11, 3, D + LANE)
    right_a, right_b = right[:84].reshape(14, 6, D + LANE), right[84:].reshape(11, 3, D + LANE)
    gap_a, gap_b = jnp.zeros((14, 2, D + LANE), bf16), jnp.zeros((11, 2, D + LANE), bf16)
    wide_a = jnp.concatenate(
        [a, left_a[:, 3:], right_a[:, :3], gap_a, left_a[:, :3], right_a[:, 3:], gap_a], axis=1
    ).reshape(14 * KEY_COLS, D + LANE)
    wide_b = jnp.concatenate([b, left_b, right_b, gap_b], axis=1).reshape(11 * QUERY_COLS, D + LANE)
    wide = jnp.concatenate([wide_a, wide_b], axis=0)
    wide_other = swap_cores(wide)
    all_a = by_core(core, wide[: 14 * KEY_COLS], wide_other[: 14 * KEY_COLS], 0)
    all_b = by_core(core, wide[14 * KEY_COLS :, :D], wide_other[14 * KEY_COLS :, :D], 0)
    alive_map = all_a[:, D].reshape(KEY_ROWS, KEY_COLS).astype(f32)

    feature_in, row_out = feature_places(core, x, y, z)
    order_in = (jnp.arange(D, dtype=jnp.int32)[:, None] == feature_in[None, :]).astype(bf16)
    order_out = (jnp.arange(2 * DH, dtype=jnp.int32)[:, None] == row_out[None, :]).astype(bf16)
    hidden = jnp.dot(all_a[:, :D], order_in, preferred_element_type=f32).astype(bf16)

    column_base = (zl * 4 + x) * SIDE
    j = jnp.arange(KEY_COLS, dtype=jnp.int32)
    key_col = jnp.select(
        [j < 16, j < 19, j < 22, j < 24, j < 27, j < 30],
        [j, j - 19, j - 3, j - 4000, j - 30, j - 8],
        -4000,
    )
    key_col = key_col + column_base
    col_start = jnp.clip(key_col[:QUERY_COLS] - 3, 0, GRID - WINDOW)[:, None]
    col_in = jnp.logical_and(key_col[None, :] >= col_start, key_col[None, :] < col_start + WINDOW)
    columns = jnp.tile(jnp.where(col_in, open_score, outside_score).astype(f32), (1, 8))
    alive = jnp.where(alive_map > 0, open_score, masked_score).astype(f32)
    alive = jnp.concatenate([alive[i : i + 21] for i in range(8)], axis=1)
    alive = jnp.concatenate([alive, alive[:3]], axis=0)
    row_base = ((zh * 4 + y) * SIDE).reshape(1)

    packed = jnp.dot(hidden, weights_in, preferred_element_type=f32).astype(bf16)
    natural = jnp.dot(order_out, weights_out, preferred_element_type=f32).astype(bf16)
    half_out = jnp.concatenate([natural[:DH], natural[DH:]], axis=1)
    mine_rows = lax.dynamic_slice_in_dim(half_out, core * HALF, HALF, axis=0)
    other_rows = swap_cores(lax.dynamic_slice_in_dim(half_out, (1 - core) * HALF, HALF, axis=0))
    rows_out = by_core(core, mine_rows, other_rows, 1)
    grad_attention = lax.dot_general(all_b, rows_out, contract_last, preferred_element_type=f32).astype(bf16)

    attention, grad_packed = attend(row_base, packed, grad_attention, alive, columns)

    hidden_own = hidden.reshape(KEY_ROWS, KEY_COLS, D)[6:22, :SIDE].reshape(SIDE * SIDE, D)
    grad_own = all_b.reshape(QUERY_ROWS, QUERY_COLS, D)[3:19, :SIDE].reshape(SIDE * SIDE, D)
    grad_own = lax.dynamic_slice_in_dim(grad_own, core * DH, DH, axis=1)
    attention_all = by_core(core, attention, swap_cores(attention), 1)
    grad_out = lax.dot_general(attention_all, grad_own, contract_first, preferred_element_type=f32).astype(bf16)
    grad_out = jnp.concatenate([grad_out[:, :HALF], grad_out[:, HALF:]], axis=0)
    grad_out = lax.dot_general(order_out, grad_out, contract_first, preferred_element_type=f32).astype(bf16)
    chunks = []
    for k in range(4):
        part = slice(k * 384, (k + 1) * 384)
        grad_in = lax.dot_general(
            hidden_own[:, part], grad_packed, contract_first, preferred_element_type=f32
        ).astype(bf16)
        chunks.append(jnp.concatenate([grad_in, grad_out[part]], axis=1))
    total = scatter_stage(chunks, 2)
    for stage in (1, 0):
        total = total.astype(bf16)
        size = total.shape[0] // 4
        total = scatter_stage([total[k * size : (k + 1) * size] for k in range(4)], stage)

    sums_in = total[:, : 3 * HALF].reshape(2, 12, 3 * HALF)
    sums_out = total[:, 3 * HALF :].reshape(2, 2, 6, HALF).transpose(1, 0, 2, 3).reshape(2, 12, HALF)
    sums = jnp.concatenate([sums_in, sums_out], axis=2)
    kept = jnp.where(core == 0, sums[0], sums[1])
    gotten = swap_cores(jnp.where(core == 0, sums[1], sums[0]))
    grad_project_in = by_core(
        core, kept[:, : 3 * HALF].reshape(12, 3, 1, HALF), gotten[:, : 3 * HALF].reshape(12, 3, 1, HALF), 2
    ).reshape(12, 3 * DH)
    kept_out = kept[:, 3 * HALF :].reshape(2, 6, HALF).transpose(1, 0, 2).reshape(6, DH)
    gotten_out = gotten[:, 3 * HALF :].reshape(2, 6, HALF).transpose(1, 0, 2).reshape(6, DH)
    grad_project_out = by_core(core, kept_out, gotten_out, 1)

    projected = jnp.dot(attention_all, half_out, preferred_element_type=f32)
    projected_mine = lax.dynamic_slice_in_dim(projected, core * tokens, tokens, axis=0)
    projected_other = swap_cores(lax.dynamic_slice_in_dim(projected, (1 - core) * tokens, tokens, axis=0))
    projected = by_core(core, projected_mine, projected_other, 1)
    layer_out = (flat_tiles + projected * live).astype(bf16).reshape(8, SIDE, D)

    grad_hidden = lax.dot_general(grad_packed, weights_in, contract_last, preferred_element_type=f32).astype(bf16)
    grad_hidden = lax.dot_general(grad_hidden, order_in, contract_last, preferred_element_type=f32)
    grad_hidden_mine = lax.dynamic_slice_in_dim(grad_hidden, core * tokens, tokens, axis=0)
    grad_hidden_other = swap_cores(
        lax.dynamic_slice_in_dim(grad_hidden, (1 - core) * tokens, tokens, axis=0).astype(bf16)
    )
    grad_hidden = grad_hidden_mine + grad_hidden_other.astype(f32)
    grad_norm = inverse * (
        grad_hidden
        - jnp.mean(grad_hidden, axis=-1, keepdims=True)
        - normed * jnp.mean(grad_hidden * normed, axis=-1, keepdims=True)
    )
    grad_tiles = (grad_flat + grad_norm).astype(bf16).reshape(8, SIDE, D)
    return (layer_out, grad_tiles, grad_project_in, grad_project_out)


def solution(mesh):
    fine = Mesh(mesh.devices.reshape(2, 4, 2, 2, 4), AXES)
    grid = P(("zh", "y", "c"), ("zl", "x"), None)
    rows = P(AXES, None)
    return jax.shard_map(
        body,
        mesh=fine,
        in_specs=(grid, P(("zh", "y", "c"), ("zl", "x")), rows, rows, grid),
        out_specs=(grid, grid, rows, rows),
        check_vma=False,
    )
```

```python
import jax
import jax.numpy as jnp
from jax import lax
from jax.experimental import pallas as pl
from jax.experimental.pallas import tpu as pltpu
from jax.sharding import Mesh, PartitionSpec as P

HEAD_DIM = 64
WINDOW = 7
D = 1536
DH = 768
HALF = DH // 2
GRID = 128
SIDE = 16
KEY_ROWS = 28
KEY_COLS = 32
QUERY_ROWS = 22
QUERY_COLS = 24
LANE = 128

AXES = ("zh", "y", "c", "zl", "x")
STAGES_IN = (("z", "y", "x"), ("x", "z", "y"))
STAGES_OUT = (("x", "y", "z"), ("y", "x", "z"))

epsilon = 1e-05
masked_score = -1e30
outside_score = -3e30
open_score = 3e38

f32 = jnp.float32
bf16 = jnp.bfloat16


def device(x, y, z, c):
    return (((z // 2 * 4 + y) * 2 + c) * 2 + z % 2) * 4 + x


def stage_pairs(axes, shift):
    pairs = []
    for x in range(4):
        for y in range(4):
            for z in range(4):
                for c in range(2):
                    place = {"x": x, "y": y, "z": z}
                    place[axes[c]] = (place[axes[c]] + shift) % 4
                    pairs.append((device(x, y, z, c), device(place["x"], place["y"], place["z"], c)))
    return pairs


def shifted(value, axes, shift):
    return lax.ppermute(value, AXES, stage_pairs(axes, shift))


def swap_cores(value):
    return lax.ppermute(value, "c", [(0, 1), (1, 0)])


def row_neighbour(value):
    pairs = [(r, r + 1 if r % 2 else r - 1) for r in range(16)]
    return lax.ppermute(value, ("zh", "y", "c"), [(a, b) for a, b in pairs if 0 <= b < 16])


def col_neighbour(value, step):
    pairs = [(i, i + step) for i in range(8)]
    return lax.ppermute(value, ("zl", "x"), [(a, b) for a, b in pairs if 0 <= b < 8])


def gather_stage(block, axes):
    far = shifted(block, axes, 2)
    near = shifted(block, axes, 1)
    back = shifted(block, axes, 3)
    return [block, near, far, back]


def scatter_stage(chunks, axes):
    far = shifted(chunks[2], axes, 2)
    near = shifted(chunks[1], axes, 3)
    back = shifted(chunks[3], axes, 1)
    return (chunks[0].astype(f32) + near.astype(f32)) + (far.astype(f32) + back.astype(f32))


def axes_of(stages, stage):
    return (stages[0][stage], stages[1][stage])


def scattered(chunks, stages):
    total = scatter_stage(chunks, axes_of(stages, 2))
    for stage in (1, 0):
        total = total.astype(bf16)
        size = total.shape[0] // 4
        total = scatter_stage([total[k * size : (k + 1) * size] for k in range(4)], axes_of(stages, stage))
    return total


def by_core(core, mine, other, axis):
    return jnp.where(
        core == 0,
        jnp.concatenate([mine, other], axis=axis),
        jnp.concatenate([other, mine], axis=axis),
    )


def normalize(values):
    center = values - jnp.mean(values, axis=-1, keepdims=True)
    inverse = lax.rsqrt(jnp.mean(center * center, axis=-1, keepdims=True) + epsilon)
    return (center * inverse, inverse)


def layer_kernel(
    place_ref, mine_ref, other_ref, w0, w1, w2, w3, gmine_ref, gother_ref, rmine_ref, rother_ref, alive_ref, col_ref,
    attn_out, grads_out, c0, c1, c2, c3,
    packed, hidden, grad_attn, dk, dv, attn, dq,
):
    base, core = place_ref[0], place_ref[1]
    width = 2 * QUERY_COLS
    span = 8 * KEY_COLS
    half = KEY_ROWS // 2 * KEY_COLS
    half_q = QUERY_ROWS // 2 * QUERY_COLS
    contract = (((1,), (1,)), ((), ()))
    over = (((0,), (0,)), ((), ()))
    chunks = (w0, w1, w2, w3)
    part = D // 4

    dk[...] = jnp.zeros_like(dk)
    dv[...] = jnp.zeros_like(dv)

    for source, side in ((mine_ref, core), (other_ref, 1 - core)):
        own_at = pl.multiple_of((1 - side) * 6 * KEY_COLS, KEY_COLS)
        for r in range(8):
            to = pl.ds(pl.multiple_of((side * 8 + r) * SIDE, SIDE), SIDE)
            hidden[to, :] = source[pl.ds(own_at + r * KEY_COLS, SIDE), :]

        def project(t, carry, source=source, side=side):
            rows = pl.ds(pl.multiple_of(t * 112, 112), 112)
            to = pl.ds(pl.multiple_of(side * half + t * 112, 112), 112)
            total = jnp.dot(source[rows, :part], w0[...], preferred_element_type=f32)
            for k in range(1, 4):
                total += jnp.dot(source[rows, k * part : (k + 1) * part], chunks[k][...], preferred_element_type=f32)
            packed[to, :] = total.astype(bf16)
            return carry

        lax.fori_loop(0, 4, project, 0)

    mine_lanes = pl.ds(pl.multiple_of(core * DH, DH), DH)
    other_lanes = pl.ds(pl.multiple_of((1 - core) * DH, DH), DH)
    for source, side in ((gmine_ref, core), (gother_ref, 1 - core)):
        to = pl.ds(pl.multiple_of(side * half_q, 8), half_q)
        total = lax.dot_general(source[:, mine_lanes], rmine_ref[...], contract, preferred_element_type=f32)
        total += lax.dot_general(source[:, other_lanes], rother_ref[...], contract, preferred_element_type=f32)
        grad_attn[to, :] = total.astype(bf16).astype(f32)

    key_line = lax.broadcasted_iota(jnp.int32, (1, span), 1) // KEY_COLS
    low = lax.broadcasted_iota(jnp.int32, (width, LANE), 1) < HEAD_DIM
    low2 = jnp.concatenate([low, jnp.logical_not(low)], axis=0)
    upper = lax.broadcasted_iota(jnp.int32, (8, LANE), 0) < 4

    def block(i, carry):
        row = base - 3 + 2 * i
        start = jnp.clip(row - 3, 0, GRID - 8)
        local = start - (base - 6)
        alive = alive_ref[pl.ds(local, 1), :]
        key_row = key_line + start
        caps = []
        for step in range(2):
            first = jnp.clip(row + step - 3, 0, GRID - WINDOW)
            inside = jnp.logical_and(key_row >= first, key_row < first + WINDOW)
            caps.append(jnp.minimum(col_ref[...], jnp.where(inside, alive, outside_score)))
        cap = jnp.concatenate(caps + caps, axis=0)
        keys_at = pl.ds(pl.multiple_of(local * KEY_COLS, KEY_COLS), span)
        query_at = pl.multiple_of((3 + 2 * i) * KEY_COLS, KEY_COLS)
        block_at = pl.ds(pl.multiple_of(i * width, width), width)
        groups = range(3)
        lanes = [pl.ds(g * LANE, LANE) for g in groups]
        key = [packed[keys_at, pl.ds(HALF + g * LANE, LANE)] for g in groups]
        value = [packed[keys_at, pl.ds(2 * HALF + g * LANE, LANE)] for g in groups]
        query2, grad2f = [], []
        for g in groups:
            lines = packed[pl.ds(query_at, 2 * KEY_COLS), lanes[g]].astype(f32) * HEAD_DIM ** (-0.5)
            pieces = []
            for step in range(2):
                line = lines[step * KEY_COLS : (step + 1) * KEY_COLS]
                pieces += [line[:SIDE], jnp.where(upper, line[16:24], pltpu.roll(line[24:32], 4, 0))]
            query2.append(jnp.where(low2, jnp.concatenate(pieces + pieces, axis=0), 0.0).astype(bf16))
            grad = grad_attn[block_at, lanes[g]]
            grad2f.append(jnp.where(low2, jnp.concatenate([grad, grad], axis=0), 0.0))
        grad2 = [g.astype(bf16) for g in grad2f]
        raw = [lax.dot_general(query2[g], key[g], contract, preferred_element_type=f32) for g in groups]
        grad_prob = [lax.dot_general(grad2[g], value[g], contract, preferred_element_type=f32) for g in groups]
        prob = []
        for g in groups:
            scores = jnp.minimum(raw[g], cap)
            expon = jnp.exp(scores - jnp.max(scores, axis=1, keepdims=True))
            prob.append(expon * (1.0 / jnp.sum(expon, axis=1, keepdims=True)))
        weights = [p.astype(bf16) for p in prob]
        mixed = [jnp.dot(weights[g], value[g], preferred_element_type=f32).astype(bf16).astype(f32) for g in groups]
        value_sum = [lax.dot_general(weights[g], grad2[g], over, preferred_element_type=f32) for g in groups]
        delta = [jnp.sum(grad2f[g] * mixed[g], axis=1, keepdims=True) for g in groups]
        grad_score = [(prob[g] * (grad_prob[g] - delta[g])).astype(bf16) for g in groups]
        grad_q = [jnp.dot(grad_score[g], key[g], preferred_element_type=f32) for g in groups]
        key_sum = [lax.dot_general(grad_score[g], query2[g], over, preferred_element_type=f32) for g in groups]
        for g in groups:
            attn[block_at, lanes[g]] = jnp.where(low, mixed[g][:width], mixed[g][width:])
            dq[block_at, lanes[g]] = jnp.where(low, grad_q[g][:width], grad_q[g][width:])
            dv[keys_at, lanes[g]] += value_sum[g]
            dk[keys_at, lanes[g]] += key_sum[g]
        return carry

    lax.fori_loop(0, QUERY_ROWS // 2, block, 0)
    for r in range(SIDE):
        own = pl.ds(r * SIDE, SIDE)
        at_query = pl.ds((r + 3) * QUERY_COLS, SIDE)
        at_key = pl.ds((r + 6) * KEY_COLS, SIDE)
        attn_out[own, :] = attn[at_query, :].astype(bf16)
        grads_out[own, :HALF] = (dq[at_query, :] * HEAD_DIM ** (-0.5)).astype(bf16)
        grads_out[own, HALF : 2 * HALF] = dk[at_key, :].astype(bf16)
        grads_out[own, 2 * HALF :] = dv[at_key, :].astype(bf16)
    for k, chunk in enumerate((c0, c1, c2, c3)):
        chunk[...] = lax.dot_general(
            hidden[:, k * part : (k + 1) * part], grads_out[...], over, preferred_element_type=f32
        ).astype(bf16)


def layer(place, *arrays):
    vmem = pl.BlockSpec(memory_space=pltpu.VMEM)
    keys, queries = KEY_ROWS * KEY_COLS, QUERY_ROWS * QUERY_COLS
    return pl.pallas_call(
        layer_kernel,
        out_shape=(
            jax.ShapeDtypeStruct((SIDE * SIDE, HALF), bf16),
            jax.ShapeDtypeStruct((SIDE * SIDE, 3 * HALF), bf16),
        )
        + (jax.ShapeDtypeStruct((D // 4, 3 * HALF), bf16),) * 4,
        in_specs=[pl.BlockSpec(memory_space=pltpu.SMEM)] + [vmem] * len(arrays),
        out_specs=(vmem,) * 6,
        scratch_shapes=[
            pltpu.VMEM((keys, 3 * HALF), bf16),
            pltpu.VMEM((SIDE * SIDE, D), bf16),
            pltpu.VMEM((queries, HALF), f32),
            pltpu.VMEM((keys, HALF), f32),
            pltpu.VMEM((keys, HALF), f32),
            pltpu.VMEM((queries, HALF), f32),
            pltpu.VMEM((queries, HALF), f32),
        ],
        compiler_params=pltpu.CompilerParams(vmem_limit_bytes=48 * 1024 * 1024),
        cost_estimate=pl.CostEstimate(flops=8 * 10**9, bytes_accessed=12 * 10**6, transcendentals=10**6),
    )(place, *arrays)


def found_places(core, here, stages):
    place = jnp.arange(D, dtype=jnp.int32)
    step = [(place // 24) % 4, (place // 96) % 4, place // 384]
    found = {}
    for name in ("x", "y", "z"):
        mine = [lax.rem(here[name] - step[stages[c].index(name)] + 4, 4) for c in range(2)]
        found[name] = jnp.where(core == 0, mine[0], mine[1])
    return found, place % 24


def owner(found, side):
    return (((found["z"] // 2 * 4 + found["y"]) * 2 + side) * 2 + found["z"] % 2) * 4 + found["x"]


def order_matrices(core, x, y, z):
    here = {"x": x, "y": y, "z": z}
    found, inner = found_places(core, here, STAGES_IN)
    feature = owner(found, inner // 12) * 12 + inner % 12
    order_in = (jnp.arange(D + LANE, dtype=jnp.int32)[:, None] == feature[None, :]).astype(bf16)
    found, inner = found_places(core, here, STAGES_OUT)
    row = owner(found, inner % 12 // 6) * 6 + inner % 6 + inner // 12 * DH
    order_out = (jnp.arange(2 * DH, dtype=jnp.int32)[:, None] == row[None, :]).astype(bf16)
    return order_in, order_out


def body(tiles, tissue, project_in, project_out, grad_layer):
    zh, y, core, zl, x = [lax.axis_index(name) for name in AXES]
    z = zh * 2 + zl
    tokens = 8 * SIDE
    contract_last = (((1,), (1,)), ((), ()))
    contract_first = (((0,), (0,)), ((), ()))

    halves = project_in.reshape(12, 3, 2, HALF)
    first, second = halves[:, :, 0].reshape(12, 3 * HALF), halves[:, :, 1].reshape(12, 3 * HALF)

    def shard(of_in, of_out):
        return jnp.concatenate([of_in, of_out.reshape(6, 2, HALF).transpose(1, 0, 2).reshape(12, HALF)], axis=1)

    shard_first, shard_second = shard(first, project_out[:, :DH]), shard(second, project_out[:, DH:])
    mine = jnp.where(core == 0, shard_first, shard_second)
    other = swap_cores(jnp.where(core == 0, shard_second, shard_first))
    block_in = by_core(core, mine[:, : 3 * HALF], other[:, : 3 * HALF], 0)
    mine_out, other_out = mine[:, 3 * HALF :].reshape(2, 6, HALF), other[:, 3 * HALF :].reshape(2, 6, HALF)
    block_out = by_core(core, mine_out, other_out, 1).reshape(24, HALF)

    flat_tiles = tiles.reshape(tokens, D).astype(f32)
    normed, inverse = normalize(flat_tiles)
    live = tissue.reshape(tokens, 1).astype(f32)
    grad_flat = grad_layer.reshape(tokens, D).astype(f32)
    tissue_lanes = jnp.broadcast_to(live.astype(bf16), (tokens, LANE))
    own_hidden = jnp.concatenate([normed.astype(bf16), tissue_lanes], axis=1).reshape(8, SIDE, D + LANE)
    own_grad = jnp.concatenate([(grad_flat * live).astype(bf16), tissue_lanes], axis=1).reshape(8, SIDE, D + LANE)
    sent = jnp.where(
        core == 1,
        jnp.concatenate([own_hidden[2:], own_grad[5:]], axis=0),
        jnp.concatenate([own_hidden[:6], own_grad[:3]], axis=0),
    )

    got_in = gather_stage(block_in, axes_of(STAGES_IN, 0))
    got_out = gather_stage(block_out, axes_of(STAGES_OUT, 0))
    got = row_neighbour(sent)
    block_in, block_out, got = lax.optimization_barrier(
        (jnp.concatenate(got_in, axis=0), jnp.concatenate(got_out, axis=0), got)
    )

    got_in = gather_stage(block_in, axes_of(STAGES_IN, 1))
    got_out = gather_stage(block_out, axes_of(STAGES_OUT, 1))
    a = jnp.where(
        core == 0, jnp.concatenate([got[:6], own_hidden], axis=0), jnp.concatenate([own_hidden, got[:6]], axis=0)
    )
    b = jnp.where(
        core == 0, jnp.concatenate([got[6:], own_grad], axis=0), jnp.concatenate([own_grad, got[6:]], axis=0)
    )

    def columns_of(a_part, b_part):
        return jnp.concatenate([a_part.reshape(112, D + LANE), b_part.reshape(44, D + LANE)], axis=0)

    left = col_neighbour(columns_of(jnp.concatenate([a[:, 12:], a[:, 8:12]], axis=1), b[:, 12:]), 1)
    right = col_neighbour(columns_of(a[:, :8], b[:, :4]), -1)
    block_in, block_out, left, right = lax.optimization_barrier(
        (jnp.concatenate(got_in, axis=0), jnp.concatenate(got_out, axis=0), left, right)
    )

    got_out = gather_stage(block_out, axes_of(STAGES_OUT, 2))
    weights_in = gather_stage(block_in, axes_of(STAGES_IN, 2))
    wide_a = jnp.concatenate([a, left[:112].reshape(14, 8, D + LANE), right[:112].reshape(14, 8, D + LANE)], axis=1)
    wide_a = wide_a.reshape(14 * KEY_COLS, D + LANE)
    wide_b = jnp.concatenate([b, left[112:].reshape(11, 4, D + LANE), right[112:].reshape(11, 4, D + LANE)], axis=1)
    wide_b = wide_b.reshape(11 * QUERY_COLS, D + LANE)
    other_a, other_b = swap_cores(wide_a), swap_cores(wide_b)
    order_in, order_out = order_matrices(core, x, y, z)
    hidden_mine = jnp.dot(wide_a, order_in, preferred_element_type=f32).astype(bf16)
    hidden_other = jnp.dot(other_a, order_in, preferred_element_type=f32).astype(bf16)

    alive_map = by_core(core, wide_a[:, D], other_a[:, D], 0).reshape(KEY_ROWS, KEY_COLS).astype(f32)
    j = jnp.arange(KEY_COLS, dtype=jnp.int32)
    key_col = jnp.select([j < 16, j < 20, j < 24], [j, j - 20, j - 28], j - 8) + (zl * 4 + x) * SIDE
    query_col = jnp.concatenate([key_col[:20], key_col[24:28]])
    col_start = jnp.clip(query_col - 3, 0, GRID - WINDOW)[:, None]
    col_in = jnp.logical_and(key_col[None, :] >= col_start, key_col[None, :] < col_start + WINDOW)
    columns = jnp.tile(jnp.where(col_in, open_score, outside_score).astype(f32), (1, 8))
    alive = jnp.where(alive_map > 0, open_score, masked_score).astype(f32)
    alive = jnp.concatenate([alive[i : i + 21] for i in range(8)], axis=1)
    alive = jnp.concatenate([alive, alive[:3]], axis=0)
    place = jnp.stack([(zh * 4 + y) * SIDE, core]).astype(jnp.int32)

    natural = jnp.dot(order_out, jnp.concatenate(got_out, axis=0), preferred_element_type=f32).astype(bf16)
    half_out = jnp.concatenate([natural[:DH], natural[DH:]], axis=1)
    mine_rows = lax.dynamic_slice_in_dim(half_out, core * HALF, HALF, axis=0)
    other_rows = swap_cores(lax.dynamic_slice_in_dim(half_out, (1 - core) * HALF, HALF, axis=0))

    attention, grad_packed, *chunks_in = layer(
        place, hidden_mine, hidden_other, *weights_in, wide_b, other_b, mine_rows, other_rows, alive, columns
    )
    total_in = scattered(chunks_in, STAGES_IN)

    grad_mine = lax.dynamic_slice_in_dim(own_grad.reshape(tokens, D + LANE), core * DH, DH, axis=1)
    grad_other = lax.dynamic_slice(
        other_b.reshape(11, QUERY_COLS, D + LANE), (3 * core, 0, core * DH), (8, SIDE, DH)
    ).reshape(tokens, DH)
    grad_own = by_core(core, grad_mine, grad_other, 0)
    attention_all = by_core(core, attention, swap_cores(attention), 1)
    grad_out = lax.dot_general(attention_all, grad_own, contract_first, preferred_element_type=f32).astype(bf16)
    grad_out = jnp.concatenate([grad_out[:, :HALF], grad_out[:, HALF:]], axis=0)
    grad_out = lax.dot_general(order_out, grad_out, contract_first, preferred_element_type=f32).astype(bf16)
    total_out = scattered([grad_out[k * 384 : (k + 1) * 384] for k in range(4)], STAGES_OUT)

    sums_in = total_in.reshape(2, 12, 3 * HALF)
    sums_out = total_out.reshape(2, 2, 6, HALF).transpose(1, 0, 2, 3).reshape(2, 12, HALF)
    sums = jnp.concatenate([sums_in, sums_out], axis=2)
    kept = jnp.where(core == 0, sums[0], sums[1])
    gotten = swap_cores(jnp.where(core == 0, sums[1], sums[0]))
    grad_project_in = by_core(
        core, kept[:, : 3 * HALF].reshape(12, 3, 1, HALF), gotten[:, : 3 * HALF].reshape(12, 3, 1, HALF), 2
    ).reshape(12, 3 * DH)
    kept_out = kept[:, 3 * HALF :].reshape(2, 6, HALF).transpose(1, 0, 2).reshape(6, DH)
    gotten_out = gotten[:, 3 * HALF :].reshape(2, 6, HALF).transpose(1, 0, 2).reshape(6, DH)
    grad_project_out = by_core(core, kept_out, gotten_out, 1)

    projected = jnp.dot(attention_all, half_out, preferred_element_type=f32)
    projected_mine = lax.dynamic_slice_in_dim(projected, core * tokens, tokens, axis=0)
    projected_other = swap_cores(lax.dynamic_slice_in_dim(projected, (1 - core) * tokens, tokens, axis=0))
    projected = by_core(core, projected_mine, projected_other, 1)
    layer_out = (flat_tiles + projected * live).astype(bf16).reshape(8, SIDE, D)

    grad_hidden = jnp.concatenate(
        [lax.dot_general(grad_packed, w, contract_last, preferred_element_type=f32).astype(bf16) for w in weights_in],
        axis=1,
    )
    grad_hidden = lax.dot_general(grad_hidden, order_in, contract_last, preferred_element_type=f32)[:, :D]
    grad_hidden_mine = lax.dynamic_slice_in_dim(grad_hidden, core * tokens, tokens, axis=0)
    grad_hidden_other = swap_cores(
        lax.dynamic_slice_in_dim(grad_hidden, (1 - core) * tokens, tokens, axis=0).astype(bf16)
    )
    grad_hidden = grad_hidden_mine + grad_hidden_other.astype(f32)
    grad_norm = inverse * (
        grad_hidden
        - jnp.mean(grad_hidden, axis=-1, keepdims=True)
        - normed * jnp.mean(grad_hidden * normed, axis=-1, keepdims=True)
    )
    grad_tiles = (grad_flat + grad_norm).astype(bf16).reshape(8, SIDE, D)
    return (layer_out, grad_tiles, grad_project_in, grad_project_out)


def solution(mesh):
    fine = Mesh(mesh.devices.reshape(2, 4, 2, 2, 4), AXES)
    grid = P(("zh", "y", "c"), ("zl", "x"), None)
    rows = P(AXES, None)
    return jax.shard_map(
        body,
        mesh=fine,
        in_specs=(grid, P(("zh", "y", "c"), ("zl", "x")), rows, rows, grid),
        out_specs=(grid, grid, rows, rows),
        check_vma=False,
    )
```

```python
import jax
import jax.numpy as jnp
from jax import lax
from jax.experimental import pallas as pl
from jax.experimental.pallas import tpu as pltpu
from jax.sharding import Mesh, PartitionSpec as P

HEAD_DIM = 64
WINDOW = 7
D = 1536
DH = 768
HALF = DH // 2
GRID = 128
SIDE = 16
KEY_ROWS = 28
KEY_COLS = 32
QUERY_ROWS = 22
QUERY_COLS = 24
LANE = 128
WIDE = D + LANE

AXES = ("zh", "y", "c", "zl", "x")
STAGES = (("y", "z", "x"), ("z", "x", "y"))

epsilon = 1e-05
masked_score = -1e30
outside_score = -3e30
open_score = 3e38

f32 = jnp.float32
bf16 = jnp.bfloat16


def device(x, y, z, c):
    return (((z // 2 * 4 + y) * 2 + c) * 2 + z % 2) * 4 + x


def stage_pairs(axes, shift):
    pairs = []
    for x in range(4):
        for y in range(4):
            for z in range(4):
                for c in range(2):
                    place = {"x": x, "y": y, "z": z}
                    place[axes[c]] = (place[axes[c]] + shift) % 4
                    pairs.append((device(x, y, z, c), device(place["x"], place["y"], place["z"], c)))
    return pairs


def shifted(value, axes, shift):
    return lax.ppermute(value, AXES, stage_pairs(axes, shift))


def swap_cores(value):
    return lax.ppermute(value, "c", [(0, 1), (1, 0)])


def row_neighbour(value):
    pairs = [(r, r + 1 if r % 2 else r - 1) for r in range(16)]
    return lax.ppermute(value, ("zh", "y", "c"), [(a, b) for a, b in pairs if 0 <= b < 16])


def col_neighbour(value, step):
    pairs = [(i, i + step) for i in range(8)]
    return lax.ppermute(value, ("zl", "x"), [(a, b) for a, b in pairs if 0 <= b < 8])


def gather_stage(block, stage):
    axes = (STAGES[0][stage], STAGES[1][stage])
    far = shifted(block, axes, 2)
    near = shifted(block, axes, 1)
    back = shifted(block, axes, 3)
    return [block, near, far, back]


def scatter_stage(chunks, stage):
    axes = (STAGES[0][stage], STAGES[1][stage])
    far = shifted(chunks[2], axes, 2)
    near = shifted(chunks[1], axes, 3)
    back = shifted(chunks[3], axes, 1)
    return (chunks[0].astype(f32) + near.astype(f32)) + (far.astype(f32) + back.astype(f32))


def by_core(core, mine, other, axis):
    return jnp.where(
        core == 0,
        jnp.concatenate([mine, other], axis=axis),
        jnp.concatenate([other, mine], axis=axis),
    )


def on_chip(kernel, place, arrays, outs, scratch=(), megabytes=14):
    vmem = pl.BlockSpec(memory_space=pltpu.VMEM)
    return pl.pallas_call(
        kernel,
        out_shape=tuple(jax.ShapeDtypeStruct(shape, kind) for shape, kind in outs),
        in_specs=[pl.BlockSpec(memory_space=pltpu.SMEM)] + [vmem] * len(arrays),
        out_specs=(vmem,) * len(outs),
        scratch_shapes=[pltpu.VMEM(shape, kind) for shape, kind in scratch],
        compiler_params=pltpu.CompilerParams(vmem_limit_bytes=megabytes * 1024 * 1024),
        cost_estimate=pl.CostEstimate(flops=1000, bytes_accessed=1000, transcendentals=0),
    )(place, *arrays)


def normalize(values):
    center = values - jnp.mean(values, axis=-1, keepdims=True)
    inverse = lax.rsqrt(jnp.mean(center * center, axis=-1, keepdims=True) + epsilon)
    return (center * inverse, inverse)


def prepare_kernel(place_ref, tiles_ref, grad_ref, live_ref, hidden_out, grad_out, sent_out):
    core = place_ref[1]
    for r in range(8):
        at = pl.ds(r * SIDE, SIDE)
        normed, inverse = normalize(tiles_ref[at, :].astype(f32))
        live = live_ref[at, :]
        lanes = live.astype(bf16)
        hidden_out[at, :D] = normed.astype(bf16)
        hidden_out[at, D:] = lanes
        grad_out[at, :D] = (grad_ref[at, :].astype(f32) * live[:, :1]).astype(bf16)
        grad_out[at, D:] = lanes
    sent_out[:96, :] = hidden_out[pl.ds(pl.multiple_of(core * 32, 16), 96), :]
    sent_out[96:, :] = grad_out[pl.ds(pl.multiple_of(core * 80, 16), 48), :]


def columns_kernel(place_ref, hidden_ref, grad_ref, got_ref, a_out, b_out, right_out, left_out):
    core = place_ref[1]
    a_out[pl.ds(pl.multiple_of(core * 128, 32), 96), :] = got_ref[:96, :]
    a_out[pl.ds(pl.multiple_of((1 - core) * 96, 32), 128), :] = hidden_ref[...]
    b_out[pl.ds(pl.multiple_of(core * 128, 16), 48), :] = got_ref[96:, :]
    b_out[pl.ds(pl.multiple_of((1 - core) * 48, 16), 128), :] = grad_ref[...]
    b_out[176:, :] = jnp.zeros((SIDE, WIDE), bf16)
    upper = lax.broadcasted_iota(jnp.int32, (8, WIDE), 0) < 4
    for m in range(7):
        lines = a_out[32 * m : 32 * m + 32, :].astype(f32)
        right = [pltpu.roll(lines[16 * i + 8 : 16 * i + 16], 4, 0) for i in range(2)]
        right_out[16 * m : 16 * m + 16, :] = jnp.concatenate(right, axis=0).astype(bf16)
        left_out[16 * m : 16 * m + 16, :] = jnp.concatenate([lines[:8], lines[16:24]], axis=0).astype(bf16)
    for m in range(3):
        lines = b_out[64 * m : 64 * m + 64, :].astype(f32)
        right, left = [], []
        for i in (0, 32):
            right.append(jnp.where(upper, pltpu.roll(lines[i + 8 : i + 16], 4, 0), lines[i + 24 : i + 32]))
            left.append(jnp.where(upper, lines[i : i + 8], pltpu.roll(lines[i + 16 : i + 24], 4, 0)))
        at = slice(112 + 16 * m, 128 + 16 * m)
        right_out[at, :] = jnp.concatenate(right, axis=0).astype(bf16)
        left_out[at, :] = jnp.concatenate(left, axis=0).astype(bf16)


def widen_kernel(place_ref, a_ref, b_ref, left_ref, right_ref, a_out, b_out):
    upper = lax.broadcasted_iota(jnp.int32, (8, WIDE), 0) < 4
    for m in range(7):
        left = left_ref[16 * m : 16 * m + 16, :].astype(f32)
        right = right_ref[16 * m : 16 * m + 16, :].astype(f32)
        for i in range(2):
            at = KEY_COLS * (2 * m + i)
            a_out[at : at + SIDE, :] = a_ref[SIDE * (2 * m + i) : SIDE * (2 * m + i + 1), :]
            both = [left[8 * i : 8 * i + 8], right[8 * i : 8 * i + 8]]
            a_out[at + SIDE : at + KEY_COLS, :] = jnp.concatenate(both, axis=0).astype(bf16)
    for m in range(3):
        left = left_ref[112 + 16 * m : 128 + 16 * m, :].astype(f32)
        right = right_ref[112 + 16 * m : 128 + 16 * m, :].astype(f32)
        for i in range(2):
            lines = b_ref[64 * m + 32 * i : 64 * m + 32 * i + 32, :].astype(f32)
            left8, right8 = left[8 * i : 8 * i + 8], right[8 * i : 8 * i + 8]
            pieces = [
                lines[:SIDE],
                jnp.where(upper, left8, pltpu.roll(right8, 4, 0)),
                lines[SIDE:],
                jnp.where(upper, pltpu.roll(left8, 4, 0), right8),
            ]
            at = 2 * QUERY_COLS * (2 * m + i)
            b_out[at : at + 2 * QUERY_COLS, :] = jnp.concatenate(pieces, axis=0).astype(bf16)


def one_hot(hit):
    return jnp.where(hit, 1.0, 0.0).astype(bf16)


def permute_kernel(place_ref, tokens_ref, feature_ref, out):
    def part(n, carry):
        lanes = pl.ds(pl.multiple_of(n * 256, 256), 256)
        feature = lax.broadcasted_iota(jnp.int32, (D, 256), 0)
        order = one_hot(feature == feature_ref[:, lanes])
        out[:, lanes] = jnp.dot(tokens_ref[:, :D], order, preferred_element_type=f32).astype(bf16)
        return carry

    lax.fori_loop(0, D // 256, part, 0)


def out_rows_kernel(place_ref, r0, r1, r2, r3, row_ref, half_out, sent_out):
    core = place_ref[1]

    def part(n, carry):
        first = pl.multiple_of(n * 128, 128)
        for h in range(2):
            row = lax.broadcasted_iota(jnp.int32, (128, D // 4), 0) + (first + h * DH)
            total = jnp.zeros((128, HALF), f32)
            for k, ref in enumerate((r0, r1, r2, r3)):
                order = one_hot(row == row_ref[:, k * 384 : (k + 1) * 384])
                total += jnp.dot(order, ref[...], preferred_element_type=f32)
            half_out[pl.ds(first, 128), h * HALF : (h + 1) * HALF] = total.astype(bf16)
        return carry

    lax.fori_loop(0, DH // 128, part, 0)
    sent_out[...] = half_out[pl.ds(pl.multiple_of((1 - core) * HALF, HALF), HALF), :]


def out_grads_kernel(place_ref, mine_ref, other_ref, grad_ref, row_ref, c0, c1, c2, c3, grads):
    core = place_ref[1]
    over = (((0,), (0,)), ((), ()))
    for attn, side in ((mine_ref, core), (other_ref, 1 - core)):
        for h in range(2):
            to = pl.ds(pl.multiple_of(h * DH + side * HALF, HALF), HALF)
            grads[to, :] = lax.dot_general(
                attn[...], grad_ref[:, h * HALF : (h + 1) * HALF], over, preferred_element_type=f32
            ).astype(bf16)
    lane = lax.broadcasted_iota(jnp.int32, (LANE, LANE), 1).astype(f32)
    for k, chunk in enumerate((c0, c1, c2, c3)):

        def part(n, carry, k=k, chunk=chunk):
            first = pl.multiple_of(n * LANE, LANE)
            row = row_ref[:, pl.ds(k * 384 + first, LANE)].astype(f32)
            row = jnp.transpose(jnp.broadcast_to(row, (LANE, LANE)))
            order = jnp.concatenate([one_hot(lane + m * LANE == row) for m in range(2 * DH // LANE)], axis=1)
            chunk[pl.ds(first, LANE), :] = jnp.dot(order, grads[...], preferred_element_type=f32).astype(bf16)
            return carry

        lax.fori_loop(0, 3, part, 0)


def grad_hidden_kernel(place_ref, grads_ref, w0, w1, w2, w3, feature_ref, mine_out, sent_out, rel):
    core = place_ref[1]
    contract = (((1,), (1,)), ((), ()))
    for k, ref in enumerate((w0, w1, w2, w3)):
        rel[:, k * 384 : (k + 1) * 384] = lax.dot_general(
            grads_ref[...], ref[...], contract, preferred_element_type=f32
        ).astype(bf16)

    def part(n, carry):
        first = pl.multiple_of(n * 256, 256)
        feature = lax.broadcasted_iota(jnp.int32, (256, D), 0) + first
        order = one_hot(feature == feature_ref[...])
        lanes = pl.ds(first, 256)
        for side, out in ((core, mine_out), (1 - core, sent_out)):
            rows = rel[pl.ds(pl.multiple_of(side * 128, 128), 128), :]
            out[:, lanes] = lax.dot_general(rows, order, contract, preferred_element_type=f32).astype(bf16)
        return carry

    lax.fori_loop(0, D // 256, part, 0)


def project_kernel(place_ref, mine_ref, other_ref, half_ref, mine_out, sent_out):
    core = place_ref[1]
    for side, out in ((core, mine_out), (1 - core, sent_out)):
        rows = pl.ds(pl.multiple_of(side * 128, 128), 128)
        total = jnp.dot(
            mine_ref[rows, :],
            half_ref[pl.ds(pl.multiple_of(core * HALF, HALF), HALF), :],
            preferred_element_type=f32,
        )
        total += jnp.dot(
            other_ref[rows, :],
            half_ref[pl.ds(pl.multiple_of((1 - core) * HALF, HALF), HALF), :],
            preferred_element_type=f32,
        )
        out[...] = total


def finish_kernel(
    place_ref, tiles_ref, grad_ref, live_ref, pmine_ref, pother_ref, gmine_ref, gother_ref, layer_out, tiles_out
):
    first = place_ref[1] == 0
    for r in range(8):
        at = pl.ds(r * SIDE, SIDE)
        tiles = tiles_ref[at, :].astype(f32)
        normed, inverse = normalize(tiles)
        live = live_ref[at, :][:, :1]
        mine, other = pmine_ref[at, :], pother_ref[at, :]
        low, high = jnp.where(first, mine, other), jnp.where(first, other, mine)
        layer_out[at, :DH] = (tiles[:, :DH] + low * live).astype(bf16)
        layer_out[at, DH:] = (tiles[:, DH:] + high * live).astype(bf16)
        grad_hidden = gmine_ref[at, :].astype(f32) + gother_ref[at, :].astype(f32)
        grad_norm = inverse * (
            grad_hidden
            - jnp.mean(grad_hidden, axis=-1, keepdims=True)
            - normed * jnp.mean(grad_hidden * normed, axis=-1, keepdims=True)
        )
        tiles_out[at, :] = (grad_ref[at, :].astype(f32) + grad_norm).astype(bf16)


def layer_kernel(
    place_ref, mine_ref, other_ref, w0, w1, w2, w3, amine_ref, aother_ref, gmine_ref, gother_ref, rmine_ref, rother_ref,
    attn_out, grads_out, c0, c1, c2, c3, grad_own,
    packed, hidden, grad_attn, dk, dv, attn, dq, tissue, lines_f32,
):
    base, core, column = place_ref[0], place_ref[1], place_ref[2]
    width = 2 * QUERY_COLS
    span = 8 * KEY_COLS
    half = KEY_ROWS // 2 * KEY_COLS
    half_q = QUERY_ROWS // 2 * QUERY_COLS
    contract = (((1,), (1,)), ((), ()))
    over = (((0,), (0,)), ((), ()))
    chunks = (w0, w1, w2, w3)
    part = D // 4

    dk[...] = jnp.zeros_like(dk)
    dv[...] = jnp.zeros_like(dv)

    for source, side in ((mine_ref, core), (other_ref, 1 - core)):
        own_at = pl.multiple_of((1 - side) * 6 * KEY_COLS, KEY_COLS)
        for r in range(8):
            to = pl.ds(pl.multiple_of((side * 8 + r) * SIDE, SIDE), SIDE)
            hidden[to, :] = source[pl.ds(own_at + r * KEY_COLS, SIDE), :]

        def project(t, carry, source=source, side=side):
            rows = pl.ds(pl.multiple_of(t * 112, 112), 112)
            to = pl.ds(pl.multiple_of(side * half + t * 112, 112), 112)
            total = jnp.dot(source[rows, :part], w0[...], preferred_element_type=f32)
            for k in range(1, 4):
                total += jnp.dot(
                    source[rows, k * part : (k + 1) * part], chunks[k][...], preferred_element_type=f32
                )
            packed[to, :] = total.astype(bf16)
            return carry

        lax.fori_loop(0, 4, project, 0)

    mine_lanes = pl.ds(pl.multiple_of(core * DH, DH), DH)
    other_lanes = pl.ds(pl.multiple_of((1 - core) * DH, DH), DH)
    rmine = rmine_ref[pl.ds(pl.multiple_of(core * HALF, HALF), HALF), :]
    for source, side in ((gmine_ref, core), (gother_ref, 1 - core)):
        to = pl.ds(pl.multiple_of(side * half_q, 8), half_q)
        total = lax.dot_general(source[:, mine_lanes], rmine, contract, preferred_element_type=f32)
        total += lax.dot_general(source[:, other_lanes], rother_ref[...], contract, preferred_element_type=f32)
        grad_attn[to, :] = total[:half_q].astype(bf16).astype(f32)

    for source, side in ((gmine_ref, core), (gother_ref, 1 - core)):
        lines_f32[...] = source[:, mine_lanes].astype(f32)
        for r in range(8):
            own = lines_f32[pl.ds(pl.multiple_of((1 - side) * 72 + 24 * r, 8), SIDE), :]
            grad_own[pl.ds(pl.multiple_of((side * 8 + r) * SIDE, SIDE), SIDE), :] = own.astype(bf16)

    for source, side in ((amine_ref, core), (aother_ref, 1 - core)):
        tissue[pl.ds(pl.multiple_of(side * half, 64), half), :] = source[:, D:].astype(f32)
    alive_line = jnp.concatenate(
        [jnp.transpose(tissue[m * LANE : (m + 1) * LANE, :])[:8] for m in range(7)] + [jnp.zeros((8, LANE), f32)], axis=1
    )
    alive_line = jnp.where(alive_line > 0, open_score, masked_score)
    spot = lax.broadcasted_iota(jnp.int32, (QUERY_COLS, span), 1) % KEY_COLS
    key_col = jnp.where(spot < 16, spot, jnp.where(spot < 20, spot - 20, jnp.where(spot < 24, spot - 28, spot - 8)))
    spot = lax.broadcasted_iota(jnp.int32, (QUERY_COLS, span), 0)
    query_col = jnp.where(spot < 16, spot, jnp.where(spot < 20, spot - 20, spot - 4))
    col_start = jnp.clip(query_col + column - 3, 0, GRID - WINDOW)
    key_col = key_col + column
    col_in = jnp.logical_and(key_col >= col_start, key_col < col_start + WINDOW)
    col_cap = jnp.where(col_in, open_score, outside_score)

    key_line = lax.broadcasted_iota(jnp.int32, (1, span), 1) // KEY_COLS
    low = lax.broadcasted_iota(jnp.int32, (width, LANE), 1) < HEAD_DIM
    low2 = jnp.concatenate([low, jnp.logical_not(low)], axis=0)
    upper = lax.broadcasted_iota(jnp.int32, (8, LANE), 0) < 4

    def block(i, carry):
        row = base - 3 + 2 * i
        start = jnp.clip(row - 3, 0, GRID - 8)
        local = start - (base - 6)
        alive = pltpu.roll(alive_line, lax.rem((32 - local) * KEY_COLS, 32 * KEY_COLS), 1)[:1, :span]
        key_row = key_line + start
        caps = []
        for step in range(2):
            first = jnp.clip(row + step - 3, 0, GRID - WINDOW)
            inside = jnp.logical_and(key_row >= first, key_row < first + WINDOW)
            caps.append(jnp.minimum(col_cap, jnp.where(inside, alive, outside_score)))
        cap = jnp.concatenate(caps + caps, axis=0)
        keys_at = pl.ds(pl.multiple_of(local * KEY_COLS, KEY_COLS), span)
        query_at = pl.multiple_of((3 + 2 * i) * KEY_COLS, KEY_COLS)
        block_at = pl.ds(pl.multiple_of(i * width, width), width)
        groups = range(3)
        lanes = [pl.ds(g * LANE, LANE) for g in groups]
        key = [packed[keys_at, pl.ds(HALF + g * LANE, LANE)] for g in groups]
        value = [packed[keys_at, pl.ds(2 * HALF + g * LANE, LANE)] for g in groups]
        query2, grad2f = [], []
        for g in groups:
            lines = packed[pl.ds(query_at, 2 * KEY_COLS), lanes[g]].astype(f32) * HEAD_DIM ** (-0.5)
            pieces = []
            for step in range(2):
                line = lines[step * KEY_COLS : (step + 1) * KEY_COLS]
                pieces += [line[:SIDE], jnp.where(upper, line[16:24], pltpu.roll(line[24:32], 4, 0))]
            query2.append(jnp.where(low2, jnp.concatenate(pieces + pieces, axis=0), 0.0).astype(bf16))
            grad = grad_attn[block_at, lanes[g]]
            grad2f.append(jnp.where(low2, jnp.concatenate([grad, grad], axis=0), 0.0))
        grad2 = [g.astype(bf16) for g in grad2f]
        raw = [lax.dot_general(query2[g], key[g], contract, preferred_element_type=f32) for g in groups]
        grad_prob = [lax.dot_general(grad2[g], value[g], contract, preferred_element_type=f32) for g in groups]
        prob = []
        for g in groups:
            scores = jnp.minimum(raw[g], cap)
            expon = jnp.exp(scores - jnp.max(scores, axis=1, keepdims=True))
            prob.append(expon * (1.0 / jnp.sum(expon, axis=1, keepdims=True)))
        weights = [p.astype(bf16) for p in prob]
        mixed = [jnp.dot(weights[g], value[g], preferred_element_type=f32).astype(bf16).astype(f32) for g in groups]
        value_sum = [lax.dot_general(weights[g], grad2[g], over, preferred_element_type=f32) for g in groups]
        delta = [jnp.sum(grad2f[g] * mixed[g], axis=1, keepdims=True) for g in groups]
        grad_score = [(prob[g] * (grad_prob[g] - delta[g])).astype(bf16) for g in groups]
        grad_q = [jnp.dot(grad_score[g], key[g], preferred_element_type=f32) for g in groups]
        key_sum = [lax.dot_general(grad_score[g], query2[g], over, preferred_element_type=f32) for g in groups]
        for g in groups:
            attn[block_at, lanes[g]] = jnp.where(low, mixed[g][:width], mixed[g][width:])
            dq[block_at, lanes[g]] = jnp.where(low, grad_q[g][:width], grad_q[g][width:])
            dv[keys_at, lanes[g]] += value_sum[g]
            dk[keys_at, lanes[g]] += key_sum[g]
        return carry

    lax.fori_loop(0, QUERY_ROWS // 2, block, 0)
    for r in range(SIDE):
        own = pl.ds(r * SIDE, SIDE)
        at_query = pl.ds((r + 3) * QUERY_COLS, SIDE)
        at_key = pl.ds((r + 6) * KEY_COLS, SIDE)
        attn_out[own, :] = attn[at_query, :].astype(bf16)
        grads_out[own, :HALF] = (dq[at_query, :] * HEAD_DIM ** (-0.5)).astype(bf16)
        grads_out[own, HALF : 2 * HALF] = dk[at_key, :].astype(bf16)
        grads_out[own, 2 * HALF :] = dv[at_key, :].astype(bf16)
    for k, chunk in enumerate((c0, c1, c2, c3)):
        chunk[...] = lax.dot_general(
            hidden[:, k * part : (k + 1) * part], grads_out[...], over, preferred_element_type=f32
        ).astype(bf16)


def layer(place, *arrays):
    keys, queries = KEY_ROWS * KEY_COLS, QUERY_ROWS * QUERY_COLS
    return on_chip(
        layer_kernel,
        place,
        arrays,
        [((SIDE * SIDE, HALF), bf16), ((SIDE * SIDE, 3 * HALF), bf16)] + [((D // 4, 3 * HALF), bf16)] * 4 + [((SIDE * SIDE, DH), bf16)],
        [
            ((keys, 3 * HALF), bf16),
            ((SIDE * SIDE, D), bf16),
            ((queries, HALF), f32),
            ((keys, HALF), f32),
            ((keys, HALF), f32),
            ((queries, HALF), f32),
            ((queries, HALF), f32),
            ((keys, LANE), f32),
            ((288, DH), f32),
        ],
        30,
    )


def found_places(core, here, place):
    step = [(place // 24) % 4, (place // 96) % 4, place // 384]
    found = {}
    for name in ("x", "y", "z"):
        mine = [lax.rem(here[name] - step[STAGES[c].index(name)] + 4, 4) for c in range(2)]
        found[name] = jnp.where(core == 0, mine[0], mine[1])
    return found


def orders(core, here, place):
    found, inner = found_places(core, here, place), place % 24

    def owner(side):
        return (((found["z"] // 2 * 4 + found["y"]) * 2 + side) * 2 + found["z"] % 2) * 4 + found["x"]

    feature = owner(inner // 12) * 12 + inner % 12
    row = owner(inner % 12 // 6) * 6 + inner % 6 + inner // 12 * DH
    return feature, row


def body(tiles, tissue, project_in, project_out, grad_layer):
    zh, y, core, zl, x = [lax.axis_index(name) for name in AXES]
    z = zh * 2 + zl
    tokens = 8 * SIDE
    place = jnp.stack([(zh * 4 + y) * SIDE, core, (zl * 4 + x) * SIDE]).astype(jnp.int32)

    halves = project_in.reshape(12, 3, 2, HALF)
    first, second = halves[:, :, 0].reshape(12, 3 * HALF), halves[:, :, 1].reshape(12, 3 * HALF)

    def shard(of_in, of_out):
        return jnp.concatenate([of_in, of_out.reshape(6, 2, HALF).transpose(1, 0, 2).reshape(12, HALF)], axis=1)

    shard_first, shard_second = shard(first, project_out[:, :DH]), shard(second, project_out[:, DH:])
    mine = jnp.where(core == 0, shard_first, shard_second)
    theirs = jnp.where(core == 0, shard_second, shard_first)
    flat_tiles, flat_grad = tiles.reshape(tokens, D), grad_layer.reshape(tokens, D)
    live = jnp.broadcast_to(tissue.reshape(tokens, 1).astype(f32), (tokens, LANE))
    own_hidden, own_grad, sent = on_chip(
        prepare_kernel,
        place,
        [flat_tiles, flat_grad, live],
        [((tokens, WIDE), bf16), ((tokens, WIDE), bf16), ((144, WIDE), bf16)],
    )
    here = {"x": x, "y": y, "z": z}
    feature_line, row_line = orders(core, here, lax.broadcasted_iota(jnp.int32, (1, D), 1))

    other, got = swap_cores(theirs), row_neighbour(sent)
    other, got, feature_line, row_line = lax.optimization_barrier((other, got, feature_line, row_line))
    block_in = by_core(core, mine[:, : 3 * HALF], other[:, : 3 * HALF], 0)
    mine_out, other_out = mine[:, 3 * HALF :].reshape(2, 6, HALF), other[:, 3 * HALF :].reshape(2, 6, HALF)
    block_out = by_core(core, mine_out, other_out, 1).reshape(24, HALF)
    block = jnp.concatenate([block_in, block_out], axis=1)
    a, b, to_right, to_left = on_chip(
        columns_kernel,
        place,
        [own_hidden, own_grad, got],
        [((224, WIDE), bf16), ((192, WIDE), bf16), ((160, WIDE), bf16), ((160, WIDE), bf16)],
    )
    block, to_right, to_left = lax.optimization_barrier((block, to_right, to_left))

    parts = gather_stage(block, 0)
    left, right = col_neighbour(to_right, 1), col_neighbour(to_left, -1)
    *parts, left, right = lax.optimization_barrier((*parts, left, right))
    wide_a, wide_b = on_chip(
        widen_kernel, place, [a, b, left, right], [((14 * KEY_COLS, WIDE), bf16), ((12 * QUERY_COLS, WIDE), bf16)]
    )
    block, wide_a, wide_b = lax.optimization_barrier((jnp.concatenate(parts, axis=0), wide_a, wide_b))

    parts = gather_stage(block, 1)
    other_a, other_b = swap_cores(wide_a), swap_cores(wide_b)
    *parts, other_a, other_b = lax.optimization_barrier((*parts, other_a, other_b))
    block_out = jnp.concatenate([part[:, 3 * HALF :] for part in parts], axis=0)
    block_in = jnp.concatenate([part[:, : 3 * HALF] for part in parts], axis=0)
    block_out, block_in = lax.optimization_barrier((block_out, block_in))

    rows_out = gather_stage(block_out, 2)
    weights = gather_stage(block_in, 2)
    permuted = [((14 * KEY_COLS, D), bf16)]
    (hidden_mine,) = on_chip(permute_kernel, place, [wide_a, feature_line], permuted)
    (hidden_other,) = on_chip(permute_kernel, place, [other_a, feature_line], permuted)

    half_out, sent_rows = on_chip(
        out_rows_kernel, place, rows_out + [row_line], [((DH, DH), bf16), ((HALF, DH), bf16)]
    )
    other_rows = swap_cores(sent_rows)

    attention, grad_packed, *chunks_in, grad_own = layer(
        place, hidden_mine, hidden_other, *weights, wide_a, other_a, wide_b, other_b, half_out, other_rows
    )
    total_in = scatter_stage(chunks_in, 2)

    attention_other = swap_cores(attention)
    hidden_kept, hidden_sent = on_chip(
        grad_hidden_kernel,
        place,
        [grad_packed, *weights, feature_line],
        [((tokens, D), bf16)] * 2,
        [((2 * tokens, D), bf16)],
    )
    attention_other, hidden_kept, hidden_sent = lax.optimization_barrier((attention_other, hidden_kept, hidden_sent))
    chunks_out = on_chip(
        out_grads_kernel,
        place,
        [attention, attention_other, grad_own, row_line],
        [((D // 4, HALF), bf16)] * 4,
        [((2 * DH, HALF), bf16)],
    )
    projected, projected_sent = on_chip(
        project_kernel, place, [attention, attention_other, half_out], [((tokens, DH), f32)] * 2
    )
    total = jnp.concatenate([total_in, scatter_stage(chunks_out, 2)], axis=1).astype(bf16)
    total, hidden_kept, hidden_sent, projected, projected_sent = lax.optimization_barrier(
        (total, hidden_kept, hidden_sent, projected, projected_sent)
    )
    total = scatter_stage([total[k * 96 : (k + 1) * 96] for k in range(4)], 1).astype(bf16)
    layer_out, grad_tiles = on_chip(
        finish_kernel,
        place,
        [flat_tiles, flat_grad, live, projected, swap_cores(projected_sent), hidden_kept, swap_cores(hidden_sent)],
        [((tokens, D), bf16)] * 2,
    )
    total, layer_out, grad_tiles = lax.optimization_barrier((total, layer_out, grad_tiles))
    total = scatter_stage([total[k * 24 : (k + 1) * 24] for k in range(4)], 0)

    sums_in = total[:, : 3 * HALF].reshape(2, 12, 3 * HALF)
    sums_out = total[:, 3 * HALF :].reshape(2, 2, 6, HALF).transpose(1, 0, 2, 3).reshape(2, 12, HALF)
    sums = jnp.concatenate([sums_in, sums_out], axis=2)
    kept = jnp.where(core == 0, sums[0], sums[1])
    gotten = swap_cores(jnp.where(core == 0, sums[1], sums[0]))
    grad_project_in = by_core(
        core, kept[:, : 3 * HALF].reshape(12, 3, 1, HALF), gotten[:, : 3 * HALF].reshape(12, 3, 1, HALF), 2
    ).reshape(12, 3 * DH)
    kept_out = kept[:, 3 * HALF :].reshape(2, 6, HALF).transpose(1, 0, 2).reshape(6, DH)
    gotten_out = gotten[:, 3 * HALF :].reshape(2, 6, HALF).transpose(1, 0, 2).reshape(6, DH)
    grad_project_out = by_core(core, kept_out, gotten_out, 1)

    return (
        layer_out.reshape(8, SIDE, D),
        grad_tiles.reshape(8, SIDE, D),
        grad_project_in,
        grad_project_out,
    )


def solution(mesh):
    fine = Mesh(mesh.devices.reshape(2, 4, 2, 2, 4), AXES)
    grid = P(("zh", "y", "c"), ("zl", "x"), None)
    rows = P(AXES, None)
    return jax.shard_map(
        body,
        mesh=fine,
        in_specs=(grid, P(("zh", "y", "c"), ("zl", "x")), rows, rows, grid),
        out_specs=(grid, grid, rows, rows),
        check_vma=False,
    )
```

```python
import jax
import jax.numpy as jnp
from jax import lax
from jax.experimental import pallas as pl
from jax.experimental.pallas import tpu as pltpu
from jax.sharding import Mesh, PartitionSpec as P

HEAD_DIM = 64
WINDOW = 7
D = 1536
DH = 768
HALF = DH // 2
GRID = 128
SIDE = 16
KEY_ROWS = 28
KEY_COLS = 32
QUERY_ROWS = 22
QUERY_COLS = 24
LANE = 128
WIDE = D + LANE

AXES = ("zh", "y", "c", "zl", "x")
STAGES = (("z", "y", "x"), ("x", "z", "y"))

epsilon = 1e-05
masked_score = -1e30
outside_score = -3e30
open_score = 3e38

f32 = jnp.float32
bf16 = jnp.bfloat16


def device(x, y, z, c):
    return (((z // 2 * 4 + y) * 2 + c) * 2 + z % 2) * 4 + x


def stage_pairs(axes, shift):
    pairs = []
    for x in range(4):
        for y in range(4):
            for z in range(4):
                for c in range(2):
                    place = {"x": x, "y": y, "z": z}
                    place[axes[c]] = (place[axes[c]] + shift) % 4
                    pairs.append((device(x, y, z, c), device(place["x"], place["y"], place["z"], c)))
    return pairs


def shifted(value, axes, shift):
    return lax.ppermute(value, AXES, stage_pairs(axes, shift))


def swap_cores(value):
    return lax.ppermute(value, "c", [(0, 1), (1, 0)])


def row_neighbour(value):
    pairs = [(r, r + 1 if r % 2 else r - 1) for r in range(16)]
    return lax.ppermute(value, ("zh", "y", "c"), [(a, b) for a, b in pairs if 0 <= b < 16])


def col_neighbour(value, step):
    pairs = [(i, i + step) for i in range(8)]
    return lax.ppermute(value, ("zl", "x"), [(a, b) for a, b in pairs if 0 <= b < 8])


def gather_stage(block, stage):
    axes = (STAGES[0][stage], STAGES[1][stage])
    far = shifted(block, axes, 2)
    near = shifted(block, axes, 1)
    back = shifted(block, axes, 3)
    return [block, near, far, back]


def gather_ring(block):
    axes = (STAGES[0][2], STAGES[1][2])
    return shifted(block, axes, 1), shifted(block, axes, 3)


def relay_ring(near, back):
    axes = (STAGES[0][2], STAGES[1][2])
    return shifted(near[:192], axes, 1), shifted(back[192:], axes, 3)


def scatter_stage(chunks, stage):
    axes = (STAGES[0][stage], STAGES[1][stage])
    far = shifted(chunks[2], axes, 2)
    near = shifted(chunks[1], axes, 3)
    back = shifted(chunks[3], axes, 1)
    return (chunks[0].astype(f32) + near.astype(f32)) + (far.astype(f32) + back.astype(f32))


def by_core(core, mine, other, axis):
    return jnp.where(
        core == 0,
        jnp.concatenate([mine, other], axis=axis),
        jnp.concatenate([other, mine], axis=axis),
    )


def on_chip(kernel, place, arrays, outs, scratch=(), megabytes=14):
    vmem = pl.BlockSpec(memory_space=pltpu.VMEM)
    return pl.pallas_call(
        kernel,
        out_shape=tuple(jax.ShapeDtypeStruct(shape, kind) for shape, kind in outs),
        in_specs=[pl.BlockSpec(memory_space=pltpu.SMEM)] + [vmem] * len(arrays),
        out_specs=(vmem,) * len(outs),
        scratch_shapes=[pltpu.VMEM(shape, kind) for shape, kind in scratch],
        compiler_params=pltpu.CompilerParams(vmem_limit_bytes=megabytes * 1024 * 1024),
        cost_estimate=pl.CostEstimate(flops=1000, bytes_accessed=1000, transcendentals=0),
    )(place, *arrays)


def normalize(values):
    center = values - jnp.mean(values, axis=-1, keepdims=True)
    inverse = lax.rsqrt(jnp.mean(center * center, axis=-1, keepdims=True) + epsilon)
    return (center * inverse, inverse)


def prepare_kernel(place_ref, tiles_ref, grad_ref, live_ref, hidden_out, grad_out, sent_out):
    core = place_ref[1]
    for r in range(8):
        at = pl.ds(r * SIDE, SIDE)
        normed, inverse = normalize(tiles_ref[at, :].astype(f32))
        live = live_ref[at, :]
        lanes = live.astype(bf16)
        hidden_out[at, :D] = normed.astype(bf16)
        hidden_out[at, D:] = lanes
        grad_out[at, :D] = (grad_ref[at, :].astype(f32) * live[:, :1]).astype(bf16)
        grad_out[at, D:] = lanes
    sent_out[:96, :] = hidden_out[pl.ds(pl.multiple_of(core * 32, 16), 96), :]
    sent_out[96:, :] = grad_out[pl.ds(pl.multiple_of(core * 80, 16), 48), :]


def columns_kernel(place_ref, hidden_ref, grad_ref, got_ref, a_out, b_out, right_out, left_out):
    core = place_ref[1]
    a_out[pl.ds(pl.multiple_of(core * 128, 32), 96), :] = got_ref[:96, :]
    a_out[pl.ds(pl.multiple_of((1 - core) * 96, 32), 128), :] = hidden_ref[...]
    b_out[pl.ds(pl.multiple_of(core * 128, 16), 48), :] = got_ref[96:, :]
    b_out[pl.ds(pl.multiple_of((1 - core) * 48, 16), 128), :] = grad_ref[...]
    b_out[176:, :] = jnp.zeros((SIDE, WIDE), bf16)
    upper = lax.broadcasted_iota(jnp.int32, (8, WIDE), 0) < 4
    for m in range(7):
        lines = a_out[32 * m : 32 * m + 32, :].astype(f32)
        right = [pltpu.roll(lines[16 * i + 8 : 16 * i + 16], 4, 0) for i in range(2)]
        right_out[16 * m : 16 * m + 16, :] = jnp.concatenate(right, axis=0).astype(bf16)
        left_out[16 * m : 16 * m + 16, :] = jnp.concatenate([lines[:8], lines[16:24]], axis=0).astype(bf16)
    for m in range(3):
        lines = b_out[64 * m : 64 * m + 64, :].astype(f32)
        right, left = [], []
        for i in (0, 32):
            right.append(jnp.where(upper, pltpu.roll(lines[i + 8 : i + 16], 4, 0), lines[i + 24 : i + 32]))
            left.append(jnp.where(upper, lines[i : i + 8], pltpu.roll(lines[i + 16 : i + 24], 4, 0)))
        at = slice(112 + 16 * m, 128 + 16 * m)
        right_out[at, :] = jnp.concatenate(right, axis=0).astype(bf16)
        left_out[at, :] = jnp.concatenate(left, axis=0).astype(bf16)


def widen_kernel(place_ref, a_ref, b_ref, left_ref, right_ref, a_out, b_out):
    upper = lax.broadcasted_iota(jnp.int32, (8, WIDE), 0) < 4
    for m in range(7):
        left = left_ref[16 * m : 16 * m + 16, :].astype(f32)
        right = right_ref[16 * m : 16 * m + 16, :].astype(f32)
        for i in range(2):
            at = KEY_COLS * (2 * m + i)
            a_out[at : at + SIDE, :] = a_ref[SIDE * (2 * m + i) : SIDE * (2 * m + i + 1), :]
            both = [left[8 * i : 8 * i + 8], right[8 * i : 8 * i + 8]]
            a_out[at + SIDE : at + KEY_COLS, :] = jnp.concatenate(both, axis=0).astype(bf16)
    for m in range(3):
        left = left_ref[112 + 16 * m : 128 + 16 * m, :].astype(f32)
        right = right_ref[112 + 16 * m : 128 + 16 * m, :].astype(f32)
        for i in range(2):
            lines = b_ref[64 * m + 32 * i : 64 * m + 32 * i + 32, :].astype(f32)
            left8, right8 = left[8 * i : 8 * i + 8], right[8 * i : 8 * i + 8]
            pieces = [
                lines[:SIDE],
                jnp.where(upper, left8, pltpu.roll(right8, 4, 0)),
                lines[SIDE:],
                jnp.where(upper, pltpu.roll(left8, 4, 0), right8),
            ]
            at = 2 * QUERY_COLS * (2 * m + i)
            b_out[at : at + 2 * QUERY_COLS, :] = jnp.concatenate(pieces, axis=0).astype(bf16)


def one_hot(hit):
    return jnp.where(hit, 1.0, 0.0).astype(bf16)


def permute_kernel(place_ref, tokens_ref, feature_ref, out):
    def part(n, carry):
        lanes = pl.ds(pl.multiple_of(n * 256, 256), 256)
        feature = lax.broadcasted_iota(jnp.int32, (D, 256), 0)
        order = one_hot(feature == feature_ref[:, lanes])
        out[:, lanes] = jnp.dot(tokens_ref[:, :D], order, preferred_element_type=f32).astype(bf16)
        return carry

    lax.fori_loop(0, D // 256, part, 0)


def out_rows_product(row_ref, part, h, first, chunk):
    row = lax.broadcasted_iota(jnp.int32, (128, D // 4), 0) + (first + h * DH)
    order = one_hot(row == row_ref[:, part * 384 : (part + 1) * 384])
    return jnp.dot(order, chunk, preferred_element_type=f32)


def near_rows_kernel(place_ref, r0, r1, r3, row_ref, sums_out):
    def part(n, carry):
        first = pl.multiple_of(n * 128, 128)
        for h in range(2):
            total = out_rows_product(row_ref, 0, h, first, r0[:, 3 * HALF :])
            total += out_rows_product(row_ref, 1, h, first, r1[:, 3 * HALF :])
            total += out_rows_product(row_ref, 3, h, first, r3[:, 3 * HALF :])
            sums_out[pl.ds(first, 128), h * HALF : (h + 1) * HALF] = total
        return carry

    lax.fori_loop(0, DH // 128, part, 0)


def out_rows_kernel(place_ref, sums_ref, r2_top, r2_low, row_ref, half_out, sent_out):
    core = place_ref[1]
    far = jnp.concatenate([r2_top[:, 3 * HALF :], r2_low[:, 3 * HALF :]], axis=0)

    def part(n, carry):
        first = pl.multiple_of(n * 128, 128)
        for h in range(2):
            lanes = slice(h * HALF, (h + 1) * HALF)
            total = sums_ref[pl.ds(first, 128), lanes] + out_rows_product(row_ref, 2, h, first, far)
            half_out[pl.ds(first, 128), lanes] = total.astype(bf16)
        return carry

    lax.fori_loop(0, DH // 128, part, 0)
    sent_out[...] = half_out[pl.ds(pl.multiple_of((1 - core) * HALF, HALF), HALF), :]


def packed_kernel(place_ref, mine_ref, other_ref, w0, w1, w2_top, w2_low, w3, packed, hidden, w2):
    core = place_ref[1]
    half = KEY_ROWS // 2 * KEY_COLS
    part = D // 4
    w2[:192, :] = w2_top[:, : 3 * HALF]
    w2[192:, :] = w2_low[:, : 3 * HALF]
    for source, side in ((mine_ref, core), (other_ref, 1 - core)):
        own_at = pl.multiple_of((1 - side) * 6 * KEY_COLS, KEY_COLS)
        for r in range(8):
            to = pl.ds(pl.multiple_of((side * 8 + r) * SIDE, SIDE), SIDE)
            hidden[to, :] = source[pl.ds(own_at + r * KEY_COLS, SIDE), :]

        def project(t, carry, source=source, side=side):
            rows = pl.ds(pl.multiple_of(t * 112, 112), 112)
            to = pl.ds(pl.multiple_of(side * half + t * 112, 112), 112)
            total = jnp.dot(source[rows, :part], w0[:, : 3 * HALF], preferred_element_type=f32)
            for k, ref in ((1, w1), (2, w2), (3, w3)):
                total += jnp.dot(
                    source[rows, k * part : (k + 1) * part], ref[:, : 3 * HALF], preferred_element_type=f32
                )
            packed[to, :] = total.astype(bf16)
            return carry

        lax.fori_loop(0, 4, project, 0)


def out_grads_kernel(place_ref, mine_ref, other_ref, grad_ref, row_ref, c0, c1, c2, c3):
    core = place_ref[1]
    over = (((0,), (0,)), ((), ()))
    part = D // 4
    inner = lax.broadcasted_iota(jnp.int32, (part, HALF), 0) % 24
    for k, chunk in enumerate((c0, c1, c2, c3)):
        row = row_ref[:, k * part : (k + 1) * part]
        row = jnp.where(row < DH, row, row - DH)
        picked = jnp.zeros((2 * LANE, part), f32)
        for attn, side in ((mine_ref, core), (other_ref, 1 - core)):
            order = one_hot(lax.broadcasted_iota(jnp.int32, (HALF, part), 0) + side * HALF == row)
            picked += jnp.dot(attn[...], order, preferred_element_type=f32)
        picked = picked.astype(bf16)
        first = lax.dot_general(picked, grad_ref[:, :HALF], over, preferred_element_type=f32)
        second = lax.dot_general(picked, grad_ref[:, HALF:], over, preferred_element_type=f32)
        chunk[...] = jnp.where(inner < 12, first, second).astype(bf16)


def grad_hidden_kernel(place_ref, grads_ref, w0, w1, w2_top, w2_low, w3, feature_ref, mine_out, sent_out, rel):
    core = place_ref[1]
    contract = (((1,), (1,)), ((), ()))
    far = jnp.concatenate([w2_top[:, : 3 * HALF], w2_low[:, : 3 * HALF]], axis=0)
    for k, chunk in enumerate((w0[:, : 3 * HALF], w1[:, : 3 * HALF], far, w3[:, : 3 * HALF])):
        rel[:, k * 384 : (k + 1) * 384] = lax.dot_general(
            grads_ref[...], chunk, contract, preferred_element_type=f32
        ).astype(bf16)

    def part(n, carry):
        first = pl.multiple_of(n * 256, 256)
        feature = lax.broadcasted_iota(jnp.int32, (256, D), 0) + first
        order = one_hot(feature == feature_ref[...])
        lanes = pl.ds(first, 256)
        for side, out in ((core, mine_out), (1 - core, sent_out)):
            rows = rel[pl.ds(pl.multiple_of(side * 128, 128), 128), :]
            out[:, lanes] = lax.dot_general(rows, order, contract, preferred_element_type=f32).astype(bf16)
        return carry

    lax.fori_loop(0, D // 256, part, 0)


def project_kernel(place_ref, mine_ref, other_ref, half_ref, mine_out, sent_out):
    core = place_ref[1]
    for side, out in ((core, mine_out), (1 - core, sent_out)):
        rows = pl.ds(pl.multiple_of(side * 128, 128), 128)
        total = jnp.dot(
            mine_ref[rows, :],
            half_ref[pl.ds(pl.multiple_of(core * HALF, HALF), HALF), :],
            preferred_element_type=f32,
        )
        total += jnp.dot(
            other_ref[rows, :],
            half_ref[pl.ds(pl.multiple_of((1 - core) * HALF, HALF), HALF), :],
            preferred_element_type=f32,
        )
        out[...] = total


def finish_kernel(
    place_ref, tiles_ref, grad_ref, live_ref, pmine_ref, pother_ref, gmine_ref, gother_ref, layer_out, tiles_out
):
    first = place_ref[1] == 0
    for r in range(8):
        at = pl.ds(r * SIDE, SIDE)
        tiles = tiles_ref[at, :].astype(f32)
        normed, inverse = normalize(tiles)
        live = live_ref[at, :][:, :1]
        mine, other = pmine_ref[at, :], pother_ref[at, :]
        low, high = jnp.where(first, mine, other), jnp.where(first, other, mine)
        layer_out[at, :DH] = (tiles[:, :DH] + low * live).astype(bf16)
        layer_out[at, DH:] = (tiles[:, DH:] + high * live).astype(bf16)
        grad_hidden = gmine_ref[at, :].astype(f32) + gother_ref[at, :].astype(f32)
        grad_norm = inverse * (
            grad_hidden
            - jnp.mean(grad_hidden, axis=-1, keepdims=True)
            - normed * jnp.mean(grad_hidden * normed, axis=-1, keepdims=True)
        )
        tiles_out[at, :] = (grad_ref[at, :].astype(f32) + grad_norm).astype(bf16)


def layer_kernel(
    place_ref, packed, hidden, amine_ref, aother_ref, gmine_ref, gother_ref, rmine_ref, rother_ref,
    attn_out, grads_out, c0, c1, c2, c3, grad_own,
    grad_attn, dk, dv, attn, dq, tissue, lines_f32,
):
    base, core, column = place_ref[0], place_ref[1], place_ref[2]
    width = 2 * QUERY_COLS
    span = 8 * KEY_COLS
    half = KEY_ROWS // 2 * KEY_COLS
    half_q = QUERY_ROWS // 2 * QUERY_COLS
    contract = (((1,), (1,)), ((), ()))
    over = (((0,), (0,)), ((), ()))
    part = D // 4

    dk[...] = jnp.zeros_like(dk)
    dv[...] = jnp.zeros_like(dv)

    mine_lanes = pl.ds(pl.multiple_of(core * DH, DH), DH)
    other_lanes = pl.ds(pl.multiple_of((1 - core) * DH, DH), DH)
    rmine = rmine_ref[pl.ds(pl.multiple_of(core * HALF, HALF), HALF), :]
    for source, side in ((gmine_ref, core), (gother_ref, 1 - core)):
        to = pl.ds(pl.multiple_of(side * half_q, 8), half_q)
        total = lax.dot_general(source[:, mine_lanes], rmine, contract, preferred_element_type=f32)
        total += lax.dot_general(source[:, other_lanes], rother_ref[...], contract, preferred_element_type=f32)
        grad_attn[to, :] = total[:half_q].astype(bf16).astype(f32)

    for source, side in ((gmine_ref, core), (gother_ref, 1 - core)):
        lines_f32[...] = source[:, mine_lanes].astype(f32)
        for r in range(8):
            own = lines_f32[pl.ds(pl.multiple_of((1 - side) * 72 + 24 * r, 8), SIDE), :]
            grad_own[pl.ds(pl.multiple_of((side * 8 + r) * SIDE, SIDE), SIDE), :] = own.astype(bf16)

    for source, side in ((amine_ref, core), (aother_ref, 1 - core)):
        tissue[pl.ds(pl.multiple_of(side * half, 64), half), :] = source[:, D:].astype(f32)
    alive_line = jnp.concatenate(
        [jnp.transpose(tissue[m * LANE : (m + 1) * LANE, :])[:8] for m in range(7)] + [jnp.zeros((8, LANE), f32)], axis=1
    )
    alive_line = jnp.where(alive_line > 0, open_score, masked_score)
    spot = lax.broadcasted_iota(jnp.int32, (QUERY_COLS, span), 1) % KEY_COLS
    key_col = jnp.where(spot < 16, spot, jnp.where(spot < 20, spot - 20, jnp.where(spot < 24, spot - 28, spot - 8)))
    spot = lax.broadcasted_iota(jnp.int32, (QUERY_COLS, span), 0)
    query_col = jnp.where(spot < 16, spot, jnp.where(spot < 20, spot - 20, spot - 4))
    col_start = jnp.clip(query_col + column - 3, 0, GRID - WINDOW)
    key_col = key_col + column
    col_in = jnp.logical_and(key_col >= col_start, key_col < col_start + WINDOW)
    col_cap = jnp.where(col_in, open_score, outside_score)

    key_line = lax.broadcasted_iota(jnp.int32, (1, span), 1) // KEY_COLS
    low = lax.broadcasted_iota(jnp.int32, (width, LANE), 1) < HEAD_DIM
    low2 = jnp.concatenate([low, jnp.logical_not(low)], axis=0)
    upper = lax.broadcasted_iota(jnp.int32, (8, LANE), 0) < 4

    def block(i, carry):
        row = base - 3 + 2 * i
        start = jnp.clip(row - 3, 0, GRID - 8)
        local = start - (base - 6)
        alive = pltpu.roll(alive_line, lax.rem((32 - local) * KEY_COLS, 32 * KEY_COLS), 1)[:1, :span]
        key_row = key_line + start
        caps = []
        for step in range(2):
            first = jnp.clip(row + step - 3, 0, GRID - WINDOW)
            inside = jnp.logical_and(key_row >= first, key_row < first + WINDOW)
            caps.append(jnp.minimum(col_cap, jnp.where(inside, alive, outside_score)))
        cap = jnp.concatenate(caps + caps, axis=0)
        keys_at = pl.ds(pl.multiple_of(local * KEY_COLS, KEY_COLS), span)
        query_at = pl.multiple_of((3 + 2 * i) * KEY_COLS, KEY_COLS)
        block_at = pl.ds(pl.multiple_of(i * width, width), width)
        groups = range(3)
        lanes = [pl.ds(g * LANE, LANE) for g in groups]
        key = [packed[keys_at, pl.ds(HALF + g * LANE, LANE)] for g in groups]
        value = [packed[keys_at, pl.ds(2 * HALF + g * LANE, LANE)] for g in groups]
        query2, grad2f = [], []
        for g in groups:
            lines = packed[pl.ds(query_at, 2 * KEY_COLS), lanes[g]].astype(f32) * HEAD_DIM ** (-0.5)
            pieces = []
            for step in range(2):
                line = lines[step * KEY_COLS : (step + 1) * KEY_COLS]
                pieces += [line[:SIDE], jnp.where(upper, line[16:24], pltpu.roll(line[24:32], 4, 0))]
            query2.append(jnp.where(low2, jnp.concatenate(pieces + pieces, axis=0), 0.0).astype(bf16))
            grad = grad_attn[block_at, lanes[g]]
            grad2f.append(jnp.where(low2, jnp.concatenate([grad, grad], axis=0), 0.0))
        grad2 = [g.astype(bf16) for g in grad2f]
        raw = [lax.dot_general(query2[g], key[g], contract, preferred_element_type=f32) for g in groups]
        grad_prob = [lax.dot_general(grad2[g], value[g], contract, preferred_element_type=f32) for g in groups]
        prob = []
        for g in groups:
            scores = jnp.minimum(raw[g], cap)
            expon = jnp.exp(scores - jnp.max(scores, axis=1, keepdims=True))
            prob.append(expon * (1.0 / jnp.sum(expon, axis=1, keepdims=True)))
        weights = [p.astype(bf16) for p in prob]
        mixed = [jnp.dot(weights[g], value[g], preferred_element_type=f32).astype(bf16).astype(f32) for g in groups]
        value_sum = [lax.dot_general(weights[g], grad2[g], over, preferred_element_type=f32) for g in groups]
        delta = [jnp.sum(grad2f[g] * mixed[g], axis=1, keepdims=True) for g in groups]
        grad_score = [(prob[g] * (grad_prob[g] - delta[g])).astype(bf16) for g in groups]
        grad_q = [jnp.dot(grad_score[g], key[g], preferred_element_type=f32) for g in groups]
        key_sum = [lax.dot_general(grad_score[g], query2[g], over, preferred_element_type=f32) for g in groups]
        for g in groups:
            attn[block_at, lanes[g]] = jnp.where(low, mixed[g][:width], mixed[g][width:])
            dq[block_at, lanes[g]] = jnp.where(low, grad_q[g][:width], grad_q[g][width:])
            dv[keys_at, lanes[g]] += value_sum[g]
            dk[keys_at, lanes[g]] += key_sum[g]
        return carry

    lax.fori_loop(0, QUERY_ROWS // 2, block, 0)
    for r in range(SIDE):
        own = pl.ds(r * SIDE, SIDE)
        at_query = pl.ds((r + 3) * QUERY_COLS, SIDE)
        at_key = pl.ds((r + 6) * KEY_COLS, SIDE)
        attn_out[own, :] = attn[at_query, :].astype(bf16)
        grads_out[own, :HALF] = (dq[at_query, :] * HEAD_DIM ** (-0.5)).astype(bf16)
        grads_out[own, HALF : 2 * HALF] = dk[at_key, :].astype(bf16)
        grads_out[own, 2 * HALF :] = dv[at_key, :].astype(bf16)
    for k, chunk in enumerate((c0, c1, c2, c3)):
        chunk[...] = lax.dot_general(
            hidden[:, k * part : (k + 1) * part], grads_out[...], over, preferred_element_type=f32
        ).astype(bf16)


def layer(place, *arrays):
    keys, queries = KEY_ROWS * KEY_COLS, QUERY_ROWS * QUERY_COLS
    return on_chip(
        layer_kernel,
        place,
        arrays,
        [((SIDE * SIDE, HALF), bf16), ((SIDE * SIDE, 3 * HALF), bf16)] + [((D // 4, 3 * HALF), bf16)] * 4 + [((SIDE * SIDE, DH), bf16)],
        [
            ((queries, HALF), f32),
            ((keys, HALF), f32),
            ((keys, HALF), f32),
            ((queries, HALF), f32),
            ((queries, HALF), f32),
            ((keys, LANE), f32),
            ((288, DH), f32),
        ],
        30,
    )


def found_places(core, here, place):
    step = [(place // 24) % 4, (place // 96) % 4, place // 384]
    found = {}
    for name in ("x", "y", "z"):
        mine = [lax.rem(here[name] - step[STAGES[c].index(name)] + 4, 4) for c in range(2)]
        found[name] = jnp.where(core == 0, mine[0], mine[1])
    return found


def orders(core, here, place):
    found, inner = found_places(core, here, place), place % 24

    def owner(side):
        return (((found["z"] // 2 * 4 + found["y"]) * 2 + side) * 2 + found["z"] % 2) * 4 + found["x"]

    feature = owner(inner // 12) * 12 + inner % 12
    row = owner(inner % 12 // 6) * 6 + inner % 6 + inner // 12 * DH
    return feature, row


def body(tiles, tissue, project_in, project_out, grad_layer):
    zh, y, core, zl, x = [lax.axis_index(name) for name in AXES]
    z = zh * 2 + zl
    tokens = 8 * SIDE
    place = jnp.stack([(zh * 4 + y) * SIDE, core, (zl * 4 + x) * SIDE]).astype(jnp.int32)

    halves = project_in.reshape(12, 3, 2, HALF)
    first, second = halves[:, :, 0].reshape(12, 3 * HALF), halves[:, :, 1].reshape(12, 3 * HALF)

    def shard(of_in, of_out):
        return jnp.concatenate([of_in, of_out.reshape(6, 2, HALF).transpose(1, 0, 2).reshape(12, HALF)], axis=1)

    shard_first, shard_second = shard(first, project_out[:, :DH]), shard(second, project_out[:, DH:])
    mine = jnp.where(core == 0, shard_first, shard_second)
    theirs = jnp.where(core == 0, shard_second, shard_first)
    other = swap_cores(theirs)
    here = {"x": x, "y": y, "z": z}
    feature_line, row_line = orders(core, here, lax.broadcasted_iota(jnp.int32, (1, D), 1))
    flat_tiles, flat_grad = tiles.reshape(tokens, D), grad_layer.reshape(tokens, D)
    live = jnp.broadcast_to(tissue.reshape(tokens, 1).astype(f32), (tokens, LANE))
    own_hidden, own_grad, sent = on_chip(
        prepare_kernel,
        place,
        [flat_tiles, flat_grad, live],
        [((tokens, WIDE), bf16), ((tokens, WIDE), bf16), ((144, WIDE), bf16)],
    )
    block_in = by_core(core, mine[:, : 3 * HALF], other[:, : 3 * HALF], 0)
    mine_out, other_out = mine[:, 3 * HALF :].reshape(2, 6, HALF), other[:, 3 * HALF :].reshape(2, 6, HALF)
    block_out = by_core(core, mine_out, other_out, 1).reshape(24, HALF)
    block = jnp.concatenate([block_in, block_out], axis=1)
    block, sent, feature_line, row_line = lax.optimization_barrier((block, sent, feature_line, row_line))

    parts = gather_stage(block, 0)
    got = row_neighbour(sent)
    *parts, got = lax.optimization_barrier((*parts, got))
    block = jnp.concatenate(parts, axis=0)
    a, b, to_right, to_left = on_chip(
        columns_kernel,
        place,
        [own_hidden, own_grad, got],
        [((224, WIDE), bf16), ((192, WIDE), bf16), ((160, WIDE), bf16), ((160, WIDE), bf16)],
    )
    block, to_right, to_left = lax.optimization_barrier((block, to_right, to_left))

    parts = gather_stage(block, 1)
    left, right = col_neighbour(to_right, 1), col_neighbour(to_left, -1)
    block = lax.optimization_barrier(jnp.concatenate(parts, axis=0))

    near, back = gather_ring(block)
    wide_a, wide_b = on_chip(
        widen_kernel, place, [a, b, left, right], [((14 * KEY_COLS, WIDE), bf16), ((12 * QUERY_COLS, WIDE), bf16)]
    )
    other_a, other_b = swap_cores(wide_a), swap_cores(wide_b)
    permuted = [((14 * KEY_COLS, D), bf16)]
    (hidden_mine,) = on_chip(permute_kernel, place, [wide_a, feature_line], permuted)
    (hidden_other,) = on_chip(permute_kernel, place, [other_a, feature_line], permuted)

    hidden_mine, near, back = lax.optimization_barrier((hidden_mine, near, back))
    weights = [block, near, *relay_ring(near, back), back]
    hidden_other, row_line = lax.optimization_barrier((hidden_other, row_line))
    (near_rows,) = on_chip(near_rows_kernel, place, [block, near, back, row_line], [((DH, DH), f32)])
    half_out, sent_rows = on_chip(
        out_rows_kernel,
        place,
        [near_rows, weights[2], weights[3], row_line],
        [((DH, DH), bf16), ((HALF, DH), bf16)],
    )
    other_rows = swap_cores(sent_rows)
    packed, hidden = on_chip(
        packed_kernel,
        place,
        [hidden_mine, hidden_other, *weights],
        [((KEY_ROWS * KEY_COLS, 3 * HALF), bf16), ((SIDE * SIDE, D), bf16)],
        [((D // 4, 3 * HALF), bf16)],
    )

    attention, grad_packed, *chunks_in, grad_own = layer(
        place, packed, hidden, wide_a, other_a, wide_b, other_b, half_out, other_rows
    )
    axes = (STAGES[0][2], STAGES[1][2])
    far, near, back = shifted(chunks_in[2], axes, 2), shifted(chunks_in[1], axes, 3), shifted(chunks_in[3], axes, 1)

    attention_other = swap_cores(attention)
    hidden_kept, hidden_sent = on_chip(
        grad_hidden_kernel,
        place,
        [grad_packed, *weights, feature_line],
        [((tokens, D), bf16)] * 2,
        [((2 * tokens, D), bf16)],
    )
    attention_other, hidden_kept, hidden_sent = lax.optimization_barrier((attention_other, hidden_kept, hidden_sent))
    chunks_out = on_chip(
        out_grads_kernel,
        place,
        [attention, attention_other, grad_own, row_line],
        [((D // 4, HALF), bf16)] * 4,
    )
    projected, projected_sent = on_chip(
        project_kernel, place, [attention, attention_other, half_out], [((tokens, DH), f32)] * 2
    )
    far_out, near_out = shifted(chunks_out[2], axes, 2), shifted(chunks_out[1], axes, 3)
    total_in, back_out = lax.optimization_barrier((chunks_in[0].astype(f32) + near.astype(f32), chunks_out[3]))
    back_out = shifted(back_out, axes, 1)
    total_in = total_in + (far.astype(f32) + back.astype(f32))
    total_out = (chunks_out[0].astype(f32) + near_out.astype(f32)) + (far_out.astype(f32) + back_out.astype(f32))
    total = jnp.concatenate([total_in, total_out], axis=1).astype(bf16)
    total, hidden_kept, hidden_sent, projected, projected_sent = lax.optimization_barrier(
        (total, hidden_kept, hidden_sent, projected, projected_sent)
    )
    total = scatter_stage([total[k * 96 : (k + 1) * 96] for k in range(4)], 1).astype(bf16)
    layer_out, grad_tiles = on_chip(
        finish_kernel,
        place,
        [flat_tiles, flat_grad, live, projected, swap_cores(projected_sent), hidden_kept, swap_cores(hidden_sent)],
        [((tokens, D), bf16)] * 2,
    )
    total = scatter_stage([total[k * 24 : (k + 1) * 24] for k in range(4)], 0)

    sums_in = total[:, : 3 * HALF].reshape(2, 12, 3 * HALF)
    sums_out = total[:, 3 * HALF :].reshape(2, 2, 6, HALF).transpose(1, 0, 2, 3).reshape(2, 12, HALF)
    sums = jnp.concatenate([sums_in, sums_out], axis=2)
    kept = jnp.where(core == 0, sums[0], sums[1])
    gotten = swap_cores(jnp.where(core == 0, sums[1], sums[0]))
    gotten, layer_out, grad_tiles = lax.optimization_barrier((gotten, layer_out, grad_tiles))
    grad_project_in = by_core(
        core, kept[:, : 3 * HALF].reshape(12, 3, 1, HALF), gotten[:, : 3 * HALF].reshape(12, 3, 1, HALF), 2
    ).reshape(12, 3 * DH)
    kept_out = kept[:, 3 * HALF :].reshape(2, 6, HALF).transpose(1, 0, 2).reshape(6, DH)
    gotten_out = gotten[:, 3 * HALF :].reshape(2, 6, HALF).transpose(1, 0, 2).reshape(6, DH)
    grad_project_out = by_core(core, kept_out, gotten_out, 1)

    return (
        layer_out.reshape(8, SIDE, D),
        grad_tiles.reshape(8, SIDE, D),
        grad_project_in,
        grad_project_out,
    )


def solution(mesh):
    fine = Mesh(mesh.devices.reshape(2, 4, 2, 2, 4), AXES)
    grid = P(("zh", "y", "c"), ("zl", "x"), None)
    rows = P(AXES, None)
    return jax.shard_map(
        body,
        mesh=fine,
        in_specs=(grid, P(("zh", "y", "c"), ("zl", "x")), rows, rows, grid),
        out_specs=(grid, grid, rows, rows),
        check_vma=False,
    )
```

```python
import jax
import jax.numpy as jnp
from jax import lax
from jax.experimental import pallas as pl
from jax.experimental.pallas import tpu as pltpu
from jax.sharding import Mesh, PartitionSpec as P

HEAD_DIM = 64
WINDOW = 7
D = 1536
DH = 768
HALF = DH // 2
GRID = 128
SIDE = 16
KEY_ROWS = 28
KEY_COLS = 32
QUERY_ROWS = 22
QUERY_COLS = 24
LANE = 128
WIDE = D + LANE

AXES = ("zh", "y", "c", "zl", "x")
STAGES = (("z", "y", "x"), ("x", "z", "y"))

epsilon = 1e-05
masked_score = -1e30
outside_score = -3e30
open_score = 3e38

f32 = jnp.float32
bf16 = jnp.bfloat16


def device(x, y, z, c):
    return (((z // 2 * 4 + y) * 2 + c) * 2 + z % 2) * 4 + x


def stage_pairs(axes, shift):
    pairs = []
    for x in range(4):
        for y in range(4):
            for z in range(4):
                for c in range(2):
                    place = {"x": x, "y": y, "z": z}
                    place[axes[c]] = (place[axes[c]] + shift) % 4
                    pairs.append((device(x, y, z, c), device(place["x"], place["y"], place["z"], c)))
    return pairs


def shifted(value, axes, shift):
    return lax.ppermute(value, AXES, stage_pairs(axes, shift))


def swap_cores(value):
    return lax.ppermute(value, "c", [(0, 1), (1, 0)])


def row_neighbour(value):
    pairs = [(r, r + 1 if r % 2 else r - 1) for r in range(16)]
    return lax.ppermute(value, ("zh", "y", "c"), [(a, b) for a, b in pairs if 0 <= b < 16])


def col_neighbour(value, step):
    pairs = [(i, i + step) for i in range(8)]
    return lax.ppermute(value, ("zl", "x"), [(a, b) for a, b in pairs if 0 <= b < 8])


def gather_stage(block, stage):
    axes = (STAGES[0][stage], STAGES[1][stage])
    far = shifted(block, axes, 2)
    near = shifted(block, axes, 1)
    back = shifted(block, axes, 3)
    return [block, near, far, back]


def gather_ring(block):
    axes = (STAGES[0][2], STAGES[1][2])
    return shifted(block, axes, 1), shifted(block, axes, 3)


def relay_ring(near, back):
    axes = (STAGES[0][2], STAGES[1][2])
    return shifted(near[:192], axes, 1), shifted(back[192:], axes, 3)


def scatter_stage(chunks, stage):
    axes = (STAGES[0][stage], STAGES[1][stage])
    far = shifted(chunks[2], axes, 2)
    near = shifted(chunks[1], axes, 3)
    back = shifted(chunks[3], axes, 1)
    return (chunks[0].astype(f32) + near.astype(f32)) + (far.astype(f32) + back.astype(f32))


def by_core(core, mine, other, axis):
    return jnp.where(
        core == 0,
        jnp.concatenate([mine, other], axis=axis),
        jnp.concatenate([other, mine], axis=axis),
    )


def on_chip(kernel, place, arrays, outs, scratch=(), megabytes=14):
    vmem = pl.BlockSpec(memory_space=pltpu.VMEM)
    return pl.pallas_call(
        kernel,
        out_shape=tuple(jax.ShapeDtypeStruct(shape, kind) for shape, kind in outs),
        in_specs=[pl.BlockSpec(memory_space=pltpu.SMEM)] + [vmem] * len(arrays),
        out_specs=(vmem,) * len(outs),
        scratch_shapes=[pltpu.VMEM(shape, kind) for shape, kind in scratch],
        compiler_params=pltpu.CompilerParams(vmem_limit_bytes=megabytes * 1024 * 1024),
        cost_estimate=pl.CostEstimate(flops=1000, bytes_accessed=1000, transcendentals=0),
    )(place, *arrays)


def normalize(values):
    center = values - jnp.mean(values, axis=-1, keepdims=True)
    inverse = lax.rsqrt(jnp.mean(center * center, axis=-1, keepdims=True) + epsilon)
    return (center * inverse, inverse)


def prepare_kernel(place_ref, tiles_ref, grad_ref, live_ref, hidden_out, grad_out, sent_out):
    core = place_ref[1]
    for r in range(8):
        at = pl.ds(r * SIDE, SIDE)
        normed, inverse = normalize(tiles_ref[at, :].astype(f32))
        live = live_ref[at, :]
        lanes = live.astype(bf16)
        hidden_out[at, :D] = normed.astype(bf16)
        hidden_out[at, D:] = lanes
        grad_out[at, :D] = (grad_ref[at, :].astype(f32) * live[:, :1]).astype(bf16)
        grad_out[at, D:] = lanes
    sent_out[:96, :] = hidden_out[pl.ds(pl.multiple_of(core * 32, 16), 96), :]
    sent_out[96:, :] = grad_out[pl.ds(pl.multiple_of(core * 80, 16), 48), :]


def columns_kernel(place_ref, hidden_ref, grad_ref, got_ref, a_out, b_out, right_out, left_out):
    core = place_ref[1]
    a_out[pl.ds(pl.multiple_of(core * 128, 32), 96), :] = got_ref[:96, :]
    a_out[pl.ds(pl.multiple_of((1 - core) * 96, 32), 128), :] = hidden_ref[...]
    b_out[pl.ds(pl.multiple_of(core * 128, 16), 48), :] = got_ref[96:, :]
    b_out[pl.ds(pl.multiple_of((1 - core) * 48, 16), 128), :] = grad_ref[...]
    b_out[176:, :] = jnp.zeros((SIDE, WIDE), bf16)
    upper = lax.broadcasted_iota(jnp.int32, (8, WIDE), 0) < 4
    for m in range(7):
        lines = a_out[32 * m : 32 * m + 32, :].astype(f32)
        right = [pltpu.roll(lines[16 * i + 8 : 16 * i + 16], 4, 0) for i in range(2)]
        right_out[16 * m : 16 * m + 16, :] = jnp.concatenate(right, axis=0).astype(bf16)
        left_out[16 * m : 16 * m + 16, :] = jnp.concatenate([lines[:8], lines[16:24]], axis=0).astype(bf16)
    for m in range(3):
        lines = b_out[64 * m : 64 * m + 64, :].astype(f32)
        right, left = [], []
        for i in (0, 32):
            right.append(jnp.where(upper, pltpu.roll(lines[i + 8 : i + 16], 4, 0), lines[i + 24 : i + 32]))
            left.append(jnp.where(upper, lines[i : i + 8], pltpu.roll(lines[i + 16 : i + 24], 4, 0)))
        at = slice(112 + 16 * m, 128 + 16 * m)
        right_out[at, :] = jnp.concatenate(right, axis=0).astype(bf16)
        left_out[at, :] = jnp.concatenate(left, axis=0).astype(bf16)


def widen_kernel(place_ref, a_ref, b_ref, left_ref, right_ref, a_out, b_out):
    upper = lax.broadcasted_iota(jnp.int32, (8, WIDE), 0) < 4
    for m in range(7):
        left = left_ref[16 * m : 16 * m + 16, :].astype(f32)
        right = right_ref[16 * m : 16 * m + 16, :].astype(f32)
        for i in range(2):
            at = KEY_COLS * (2 * m + i)
            a_out[at : at + SIDE, :] = a_ref[SIDE * (2 * m + i) : SIDE * (2 * m + i + 1), :]
            both = [left[8 * i : 8 * i + 8], right[8 * i : 8 * i + 8]]
            a_out[at + SIDE : at + KEY_COLS, :] = jnp.concatenate(both, axis=0).astype(bf16)
    for m in range(3):
        left = left_ref[112 + 16 * m : 128 + 16 * m, :].astype(f32)
        right = right_ref[112 + 16 * m : 128 + 16 * m, :].astype(f32)
        for i in range(2):
            lines = b_ref[64 * m + 32 * i : 64 * m + 32 * i + 32, :].astype(f32)
            left8, right8 = left[8 * i : 8 * i + 8], right[8 * i : 8 * i + 8]
            pieces = [
                lines[:SIDE],
                jnp.where(upper, left8, pltpu.roll(right8, 4, 0)),
                lines[SIDE:],
                jnp.where(upper, pltpu.roll(left8, 4, 0), right8),
            ]
            at = 2 * QUERY_COLS * (2 * m + i)
            b_out[at : at + 2 * QUERY_COLS, :] = jnp.concatenate(pieces, axis=0).astype(bf16)


def one_hot(hit):
    return jnp.where(hit, 1.0, 0.0).astype(bf16)


def permute_kernel(place_ref, tokens_ref, feature_ref, out):
    def part(n, carry):
        lanes = pl.ds(pl.multiple_of(n * 256, 256), 256)
        feature = lax.broadcasted_iota(jnp.int32, (D, 256), 0)
        order = one_hot(feature == feature_ref[:, lanes])
        out[:, lanes] = jnp.dot(tokens_ref[:, :D], order, preferred_element_type=f32).astype(bf16)
        return carry

    lax.fori_loop(0, D // 256, part, 0)


def out_rows_product(row_ref, part, first, chunk):
    row = row_ref[:, part * 384 : (part + 1) * 384]
    row = jnp.where(row < DH, row, row - DH)
    order = one_hot(lax.broadcasted_iota(jnp.int32, (128, D // 4), 0) + first == row)
    return jnp.dot(order, chunk, preferred_element_type=f32)


def by_half(chunk):
    upper = lax.broadcasted_iota(jnp.int32, chunk.shape, 0) % 24 < 12
    chunk = chunk.astype(f32)
    halves = [jnp.where(upper, chunk, 0.0), jnp.where(upper, 0.0, chunk)]
    return jnp.concatenate(halves, axis=1).astype(bf16)


def near_rows_kernel(place_ref, r0, r1, r3, row_ref, sums_out, halves):
    for i, ref in enumerate((r0, r1, r3)):
        halves[i, :, :] = by_half(ref[:, 3 * HALF :])

    def part(n, carry):
        first = pl.multiple_of(n * 128, 128)
        total = out_rows_product(row_ref, 0, first, halves[0])
        total += out_rows_product(row_ref, 1, first, halves[1])
        total += out_rows_product(row_ref, 3, first, halves[2])
        sums_out[pl.ds(first, 128), :] = total
        return carry

    lax.fori_loop(0, DH // 128, part, 0)


def out_rows_kernel(place_ref, sums_ref, r2_top, r2_low, row_ref, half_out, sent_out, halves):
    core = place_ref[1]
    halves[:192, :] = by_half(r2_top[:, 3 * HALF :])
    halves[192:, :] = by_half(r2_low[:, 3 * HALF :])

    def part(n, carry):
        first = pl.multiple_of(n * 128, 128)
        rows = pl.ds(first, 128)
        half_out[rows, :] = (sums_ref[rows, :] + out_rows_product(row_ref, 2, first, halves[...])).astype(bf16)
        return carry

    lax.fori_loop(0, DH // 128, part, 0)
    sent_out[...] = half_out[pl.ds(pl.multiple_of((1 - core) * HALF, HALF), HALF), :]


def packed_kernel(place_ref, mine_ref, other_ref, w0, w1, w2_top, w2_low, w3, packed, hidden, w2):
    core = place_ref[1]
    half = KEY_ROWS // 2 * KEY_COLS
    part = D // 4
    w2[:192, :] = w2_top[:, : 3 * HALF]
    w2[192:, :] = w2_low[:, : 3 * HALF]
    for source, side in ((mine_ref, core), (other_ref, 1 - core)):
        own_at = pl.multiple_of((1 - side) * 6 * KEY_COLS, KEY_COLS)
        for r in range(8):
            to = pl.ds(pl.multiple_of((side * 8 + r) * SIDE, SIDE), SIDE)
            hidden[to, :] = source[pl.ds(own_at + r * KEY_COLS, SIDE), :]

        def project(t, carry, source=source, side=side):
            rows = pl.ds(pl.multiple_of(t * 224, 224), 224)
            to = pl.ds(pl.multiple_of(side * half + t * 224, 224), 224)
            total = jnp.dot(source[rows, :part], w0[:, : 3 * HALF], preferred_element_type=f32)
            for k, ref in ((1, w1), (2, w2), (3, w3)):
                total += jnp.dot(
                    source[rows, k * part : (k + 1) * part], ref[:, : 3 * HALF], preferred_element_type=f32
                )
            packed[to, :] = total.astype(bf16)
            return carry

        lax.fori_loop(0, 2, project, 0)


def out_grads_kernel(place_ref, mine_ref, other_ref, grad_ref, row_ref, c0, c1, c2, c3):
    core = place_ref[1]
    over = (((0,), (0,)), ((), ()))
    part = D // 4
    inner = lax.broadcasted_iota(jnp.int32, (part, HALF), 0) % 24
    for k, chunk in enumerate((c0, c1, c2, c3)):
        row = row_ref[:, k * part : (k + 1) * part]
        row = jnp.where(row < DH, row, row - DH)
        picked = jnp.zeros((2 * LANE, part), f32)
        for attn, side in ((mine_ref, core), (other_ref, 1 - core)):
            order = one_hot(lax.broadcasted_iota(jnp.int32, (HALF, part), 0) + side * HALF == row)
            picked += jnp.dot(attn[...], order, preferred_element_type=f32)
        picked = picked.astype(bf16)
        first = lax.dot_general(picked, grad_ref[:, :HALF], over, preferred_element_type=f32)
        second = lax.dot_general(picked, grad_ref[:, HALF:], over, preferred_element_type=f32)
        chunk[...] = jnp.where(inner < 12, first, second).astype(bf16)


def grad_hidden_kernel(place_ref, grads_ref, w0, w1, w2_top, w2_low, w3, feature_ref, mine_out, sent_out, rel):
    core = place_ref[1]
    contract = (((1,), (1,)), ((), ()))
    far = jnp.concatenate([w2_top[:, : 3 * HALF], w2_low[:, : 3 * HALF]], axis=0)
    for k, chunk in enumerate((w0[:, : 3 * HALF], w1[:, : 3 * HALF], far, w3[:, : 3 * HALF])):
        rel[:, k * 384 : (k + 1) * 384] = lax.dot_general(
            grads_ref[...], chunk, contract, preferred_element_type=f32
        ).astype(bf16)

    def part(n, carry):
        first = pl.multiple_of(n * 256, 256)
        feature = lax.broadcasted_iota(jnp.int32, (256, D), 0) + first
        order = one_hot(feature == feature_ref[...])
        lanes = pl.ds(first, 256)
        for side, out in ((core, mine_out), (1 - core, sent_out)):
            rows = rel[pl.ds(pl.multiple_of(side * 128, 128), 128), :]
            out[:, lanes] = lax.dot_general(rows, order, contract, preferred_element_type=f32).astype(bf16)
        return carry

    lax.fori_loop(0, D // 256, part, 0)


def project_kernel(place_ref, mine_ref, other_ref, half_ref, mine_out, sent_out):
    core = place_ref[1]
    for side, out in ((core, mine_out), (1 - core, sent_out)):
        rows = pl.ds(pl.multiple_of(side * 128, 128), 128)
        total = jnp.dot(
            mine_ref[rows, :],
            half_ref[pl.ds(pl.multiple_of(core * HALF, HALF), HALF), :],
            preferred_element_type=f32,
        )
        total += jnp.dot(
            other_ref[rows, :],
            half_ref[pl.ds(pl.multiple_of((1 - core) * HALF, HALF), HALF), :],
            preferred_element_type=f32,
        )
        out[...] = total


def finish_kernel(
    place_ref, tiles_ref, grad_ref, live_ref, pmine_ref, pother_ref, gmine_ref, gother_ref, layer_out, tiles_out
):
    first = place_ref[1] == 0
    for r in range(8):
        at = pl.ds(r * SIDE, SIDE)
        tiles = tiles_ref[at, :].astype(f32)
        normed, inverse = normalize(tiles)
        live = live_ref[at, :][:, :1]
        mine, other = pmine_ref[at, :], pother_ref[at, :]
        low, high = jnp.where(first, mine, other), jnp.where(first, other, mine)
        layer_out[at, :DH] = (tiles[:, :DH] + low * live).astype(bf16)
        layer_out[at, DH:] = (tiles[:, DH:] + high * live).astype(bf16)
        grad_hidden = gmine_ref[at, :].astype(f32) + gother_ref[at, :].astype(f32)
        grad_norm = inverse * (
            grad_hidden
            - jnp.mean(grad_hidden, axis=-1, keepdims=True)
            - normed * jnp.mean(grad_hidden * normed, axis=-1, keepdims=True)
        )
        tiles_out[at, :] = (grad_ref[at, :].astype(f32) + grad_norm).astype(bf16)


def layer_kernel(
    place_ref, packed, hidden, amine_ref, aother_ref, gmine_ref, gother_ref, rmine_ref, rother_ref,
    attn_out, grads_out, c0, c1, c2, c3, grad_own,
    grad_attn, dk, dv, attn, dq, tissue, lines_f32,
):
    base, core, column = place_ref[0], place_ref[1], place_ref[2]
    width = 2 * QUERY_COLS
    span = 8 * KEY_COLS
    half = KEY_ROWS // 2 * KEY_COLS
    half_q = QUERY_ROWS // 2 * QUERY_COLS
    contract = (((1,), (1,)), ((), ()))
    over = (((0,), (0,)), ((), ()))
    part = D // 4

    dk[...] = jnp.zeros_like(dk)
    dv[...] = jnp.zeros_like(dv)

    mine_lanes = pl.ds(pl.multiple_of(core * DH, DH), DH)
    other_lanes = pl.ds(pl.multiple_of((1 - core) * DH, DH), DH)
    rmine = rmine_ref[pl.ds(pl.multiple_of(core * HALF, HALF), HALF), :]
    for source, side in ((gmine_ref, core), (gother_ref, 1 - core)):
        to = pl.ds(pl.multiple_of(side * half_q, 8), half_q)
        total = lax.dot_general(source[:, mine_lanes], rmine, contract, preferred_element_type=f32)
        total += lax.dot_general(source[:, other_lanes], rother_ref[...], contract, preferred_element_type=f32)
        grad_attn[to, :] = total[:half_q].astype(bf16).astype(f32)

    for source, side in ((gmine_ref, core), (gother_ref, 1 - core)):
        lines_f32[...] = source[:, mine_lanes].astype(f32)
        for r in range(8):
            own = lines_f32[pl.ds(pl.multiple_of((1 - side) * 72 + 24 * r, 8), SIDE), :]
            grad_own[pl.ds(pl.multiple_of((side * 8 + r) * SIDE, SIDE), SIDE), :] = own.astype(bf16)

    for source, side in ((amine_ref, core), (aother_ref, 1 - core)):
        tissue[pl.ds(pl.multiple_of(side * half, 64), half), :] = source[:, D:].astype(f32)
    alive_line = jnp.concatenate(
        [jnp.transpose(tissue[m * LANE : (m + 1) * LANE, :])[:8] for m in range(7)] + [jnp.zeros((8, LANE), f32)], axis=1
    )
    alive_line = jnp.where(alive_line > 0, open_score, masked_score)
    spot = lax.broadcasted_iota(jnp.int32, (QUERY_COLS, span), 1) % KEY_COLS
    key_col = jnp.where(spot < 16, spot, jnp.where(spot < 20, spot - 20, jnp.where(spot < 24, spot - 28, spot - 8)))
    spot = lax.broadcasted_iota(jnp.int32, (QUERY_COLS, span), 0)
    query_col = jnp.where(spot < 16, spot, jnp.where(spot < 20, spot - 20, spot - 4))
    col_start = jnp.clip(query_col + column - 3, 0, GRID - WINDOW)
    key_col = key_col + column
    col_in = jnp.logical_and(key_col >= col_start, key_col < col_start + WINDOW)
    col_cap = jnp.where(col_in, open_score, outside_score)

    key_line = lax.broadcasted_iota(jnp.int32, (1, span), 1) // KEY_COLS
    low = lax.broadcasted_iota(jnp.int32, (width, LANE), 1) < HEAD_DIM
    low2 = jnp.concatenate([low, jnp.logical_not(low)], axis=0)
    upper = lax.broadcasted_iota(jnp.int32, (8, LANE), 0) < 4

    def block(i, carry):
        row = base - 3 + 2 * i
        start = jnp.clip(row - 3, 0, GRID - 8)
        local = start - (base - 6)
        alive = pltpu.roll(alive_line, lax.rem((32 - local) * KEY_COLS, 32 * KEY_COLS), 1)[:1, :span]
        key_row = key_line + start
        caps = []
        for step in range(2):
            first = jnp.clip(row + step - 3, 0, GRID - WINDOW)
            inside = jnp.logical_and(key_row >= first, key_row < first + WINDOW)
            caps.append(jnp.minimum(col_cap, jnp.where(inside, alive, outside_score)))
        cap = jnp.concatenate(caps + caps, axis=0)
        keys_at = pl.ds(pl.multiple_of(local * KEY_COLS, KEY_COLS), span)
        query_at = pl.multiple_of((3 + 2 * i) * KEY_COLS, KEY_COLS)
        block_at = pl.ds(pl.multiple_of(i * width, width), width)
        groups = range(3)
        lanes = [pl.ds(g * LANE, LANE) for g in groups]
        key = [packed[keys_at, pl.ds(HALF + g * LANE, LANE)] for g in groups]
        value = [packed[keys_at, pl.ds(2 * HALF + g * LANE, LANE)] for g in groups]
        query2, grad2f = [], []
        for g in groups:
            lines = packed[pl.ds(query_at, 2 * KEY_COLS), lanes[g]].astype(f32) * HEAD_DIM ** (-0.5)
            pieces = []
            for step in range(2):
                line = lines[step * KEY_COLS : (step + 1) * KEY_COLS]
                pieces += [line[:SIDE], jnp.where(upper, line[16:24], pltpu.roll(line[24:32], 4, 0))]
            query2.append(jnp.where(low2, jnp.concatenate(pieces + pieces, axis=0), 0.0).astype(bf16))
            grad = grad_attn[block_at, lanes[g]]
            grad2f.append(jnp.where(low2, jnp.concatenate([grad, grad], axis=0), 0.0))
        grad2 = [g.astype(bf16) for g in grad2f]
        raw = [lax.dot_general(query2[g], key[g], contract, preferred_element_type=f32) for g in groups]
        grad_prob = [lax.dot_general(grad2[g], value[g], contract, preferred_element_type=f32) for g in groups]
        prob = []
        for g in groups:
            scores = jnp.minimum(raw[g], cap)
            expon = jnp.exp(scores - jnp.max(scores, axis=1, keepdims=True))
            prob.append(expon * (1.0 / jnp.sum(expon, axis=1, keepdims=True)))
        weights = [p.astype(bf16) for p in prob]
        mixed = [jnp.dot(weights[g], value[g], preferred_element_type=f32).astype(bf16).astype(f32) for g in groups]
        value_sum = [lax.dot_general(weights[g], grad2[g], over, preferred_element_type=f32) for g in groups]
        delta = [jnp.sum(grad2f[g] * mixed[g], axis=1, keepdims=True) for g in groups]
        grad_score = [(prob[g] * (grad_prob[g] - delta[g])).astype(bf16) for g in groups]
        grad_q = [jnp.dot(grad_score[g], key[g], preferred_element_type=f32) for g in groups]
        key_sum = [lax.dot_general(grad_score[g], query2[g], over, preferred_element_type=f32) for g in groups]
        for g in groups:
            attn[block_at, lanes[g]] = jnp.where(low, mixed[g][:width], mixed[g][width:])
            dq[block_at, lanes[g]] = jnp.where(low, grad_q[g][:width], grad_q[g][width:])
            dv[keys_at, lanes[g]] += value_sum[g]
            dk[keys_at, lanes[g]] += key_sum[g]
        return carry

    lax.fori_loop(0, QUERY_ROWS // 2, block, 0, unroll=True)
    for r in range(SIDE):
        own = pl.ds(r * SIDE, SIDE)
        at_query = pl.ds((r + 3) * QUERY_COLS, SIDE)
        at_key = pl.ds((r + 6) * KEY_COLS, SIDE)
        attn_out[own, :] = attn[at_query, :].astype(bf16)
        grads_out[own, :HALF] = (dq[at_query, :] * HEAD_DIM ** (-0.5)).astype(bf16)
        grads_out[own, HALF : 2 * HALF] = dk[at_key, :].astype(bf16)
        grads_out[own, 2 * HALF :] = dv[at_key, :].astype(bf16)
    for k, chunk in enumerate((c0, c1, c2, c3)):
        chunk[...] = lax.dot_general(
            hidden[:, k * part : (k + 1) * part], grads_out[...], over, preferred_element_type=f32
        ).astype(bf16)


def layer(place, *arrays):
    keys, queries = KEY_ROWS * KEY_COLS, QUERY_ROWS * QUERY_COLS
    return on_chip(
        layer_kernel,
        place,
        arrays,
        [((SIDE * SIDE, HALF), bf16), ((SIDE * SIDE, 3 * HALF), bf16)] + [((D // 4, 3 * HALF), bf16)] * 4 + [((SIDE * SIDE, DH), bf16)],
        [
            ((queries, HALF), f32),
            ((keys, HALF), f32),
            ((keys, HALF), f32),
            ((queries, HALF), f32),
            ((queries, HALF), f32),
            ((keys, LANE), f32),
            ((288, DH), f32),
        ],
        30,
    )


def found_places(core, here, place):
    step = [(place // 24) % 4, (place // 96) % 4, place // 384]
    found = {}
    for name in ("x", "y", "z"):
        mine = [lax.rem(here[name] - step[STAGES[c].index(name)] + 4, 4) for c in range(2)]
        found[name] = jnp.where(core == 0, mine[0], mine[1])
    return found


def orders(core, here, place):
    found, inner = found_places(core, here, place), place % 24

    def owner(side):
        return (((found["z"] // 2 * 4 + found["y"]) * 2 + side) * 2 + found["z"] % 2) * 4 + found["x"]

    feature = owner(inner // 12) * 12 + inner % 12
    row = owner(inner % 12 // 6) * 6 + inner % 6 + inner // 12 * DH
    return feature, row


def body(tiles, tissue, project_in, project_out, grad_layer):
    zh, y, core, zl, x = [lax.axis_index(name) for name in AXES]
    z = zh * 2 + zl
    tokens = 8 * SIDE
    place = jnp.stack([(zh * 4 + y) * SIDE, core, (zl * 4 + x) * SIDE]).astype(jnp.int32)

    halves = project_in.reshape(12, 3, 2, HALF)
    first, second = halves[:, :, 0].reshape(12, 3 * HALF), halves[:, :, 1].reshape(12, 3 * HALF)

    def shard(of_in, of_out):
        return jnp.concatenate([of_in, of_out.reshape(6, 2, HALF).transpose(1, 0, 2).reshape(12, HALF)], axis=1)

    shard_first, shard_second = shard(first, project_out[:, :DH]), shard(second, project_out[:, DH:])
    mine = jnp.where(core == 0, shard_first, shard_second)
    theirs = jnp.where(core == 0, shard_second, shard_first)
    other = swap_cores(theirs)
    here = {"x": x, "y": y, "z": z}
    feature_line, row_line = orders(core, here, lax.broadcasted_iota(jnp.int32, (1, D), 1))
    flat_tiles, flat_grad = tiles.reshape(tokens, D), grad_layer.reshape(tokens, D)
    live = jnp.broadcast_to(tissue.reshape(tokens, 1).astype(f32), (tokens, LANE))
    own_hidden, own_grad, sent = on_chip(
        prepare_kernel,
        place,
        [flat_tiles, flat_grad, live],
        [((tokens, WIDE), bf16), ((tokens, WIDE), bf16), ((144, WIDE), bf16)],
    )
    block_in = by_core(core, mine[:, : 3 * HALF], other[:, : 3 * HALF], 0)
    mine_out, other_out = mine[:, 3 * HALF :].reshape(2, 6, HALF), other[:, 3 * HALF :].reshape(2, 6, HALF)
    block_out = by_core(core, mine_out, other_out, 1).reshape(24, HALF)
    block = jnp.concatenate([block_in, block_out], axis=1)
    block, sent, feature_line, row_line = lax.optimization_barrier((block, sent, feature_line, row_line))

    parts = gather_stage(block, 0)
    got = row_neighbour(sent)
    *parts, got = lax.optimization_barrier((*parts, got))
    block = jnp.concatenate(parts, axis=0)
    a, b, to_right, to_left = on_chip(
        columns_kernel,
        place,
        [own_hidden, own_grad, got],
        [((224, WIDE), bf16), ((192, WIDE), bf16), ((160, WIDE), bf16), ((160, WIDE), bf16)],
    )
    block, to_right, to_left = lax.optimization_barrier((block, to_right, to_left))

    parts = gather_stage(block, 1)
    left, right = col_neighbour(to_right, 1), col_neighbour(to_left, -1)
    block = lax.optimization_barrier(jnp.concatenate(parts, axis=0))

    near, back = gather_ring(block)
    wide_a, wide_b = on_chip(
        widen_kernel, place, [a, b, left, right], [((14 * KEY_COLS, WIDE), bf16), ((12 * QUERY_COLS, WIDE), bf16)]
    )
    other_a, other_b = swap_cores(wide_a), swap_cores(wide_b)
    permuted = [((14 * KEY_COLS, D), bf16)]
    (hidden_mine,) = on_chip(permute_kernel, place, [wide_a, feature_line], permuted)
    (hidden_other,) = on_chip(permute_kernel, place, [other_a, feature_line], permuted)

    hidden_mine, near, back = lax.optimization_barrier((hidden_mine, near, back))
    weights = [block, near, *relay_ring(near, back), back]
    hidden_other, row_line = lax.optimization_barrier((hidden_other, row_line))
    (near_rows,) = on_chip(near_rows_kernel, place, [block, near, back, row_line], [((DH, DH), f32)], [((3, D // 4, DH), bf16)])
    half_out, sent_rows = on_chip(
        out_rows_kernel,
        place,
        [near_rows, weights[2], weights[3], row_line],
        [((DH, DH), bf16), ((HALF, DH), bf16)],
        [((D // 4, DH), bf16)],
    )
    other_rows = swap_cores(sent_rows)
    packed, hidden = on_chip(
        packed_kernel,
        place,
        [hidden_mine, hidden_other, *weights],
        [((KEY_ROWS * KEY_COLS, 3 * HALF), bf16), ((SIDE * SIDE, D), bf16)],
        [((D // 4, 3 * HALF), bf16)],
    )

    attention, grad_packed, *chunks_in, grad_own = layer(
        place, packed, hidden, wide_a, other_a, wide_b, other_b, half_out, other_rows
    )
    axes = (STAGES[0][2], STAGES[1][2])
    far, near, back = shifted(chunks_in[2], axes, 2), shifted(chunks_in[1], axes, 3), shifted(chunks_in[3], axes, 1)

    attention_other = swap_cores(attention)
    hidden_kept, hidden_sent = on_chip(
        grad_hidden_kernel,
        place,
        [grad_packed, *weights, feature_line],
        [((tokens, D), bf16)] * 2,
        [((2 * tokens, D), bf16)],
    )
    attention_other, hidden_kept, hidden_sent = lax.optimization_barrier((attention_other, hidden_kept, hidden_sent))
    chunks_out = on_chip(
        out_grads_kernel,
        place,
        [attention, attention_other, grad_own, row_line],
        [((D // 4, HALF), bf16)] * 4,
    )
    projected, projected_sent = on_chip(
        project_kernel, place, [attention, attention_other, half_out], [((tokens, DH), f32)] * 2
    )
    far_out, near_out = shifted(chunks_out[2], axes, 2), shifted(chunks_out[1], axes, 3)
    total_in, back_out = lax.optimization_barrier((chunks_in[0].astype(f32) + near.astype(f32), chunks_out[3]))
    back_out = shifted(back_out, axes, 1)
    total_in = total_in + (far.astype(f32) + back.astype(f32))
    total_out = (chunks_out[0].astype(f32) + near_out.astype(f32)) + (far_out.astype(f32) + back_out.astype(f32))
    total = jnp.concatenate([total_in, total_out], axis=1).astype(bf16)
    total, hidden_kept, hidden_sent, projected, projected_sent = lax.optimization_barrier(
        (total, hidden_kept, hidden_sent, projected, projected_sent)
    )
    total = scatter_stage([total[k * 96 : (k + 1) * 96] for k in range(4)], 1).astype(bf16)
    layer_out, grad_tiles = on_chip(
        finish_kernel,
        place,
        [flat_tiles, flat_grad, live, projected, swap_cores(projected_sent), hidden_kept, swap_cores(hidden_sent)],
        [((tokens, D), bf16)] * 2,
    )
    total = scatter_stage([total[k * 24 : (k + 1) * 24] for k in range(4)], 0)

    sums_in = total[:, : 3 * HALF].reshape(2, 12, 3 * HALF)
    sums_out = total[:, 3 * HALF :].reshape(2, 2, 6, HALF).transpose(1, 0, 2, 3).reshape(2, 12, HALF)
    sums = jnp.concatenate([sums_in, sums_out], axis=2)
    kept = jnp.where(core == 0, sums[0], sums[1])
    gotten = swap_cores(jnp.where(core == 0, sums[1], sums[0]))
    gotten, layer_out, grad_tiles = lax.optimization_barrier((gotten, layer_out, grad_tiles))
    grad_project_in = by_core(
        core, kept[:, : 3 * HALF].reshape(12, 3, 1, HALF), gotten[:, : 3 * HALF].reshape(12, 3, 1, HALF), 2
    ).reshape(12, 3 * DH)
    kept_out = kept[:, 3 * HALF :].reshape(2, 6, HALF).transpose(1, 0, 2).reshape(6, DH)
    gotten_out = gotten[:, 3 * HALF :].reshape(2, 6, HALF).transpose(1, 0, 2).reshape(6, DH)
    grad_project_out = by_core(core, kept_out, gotten_out, 1)

    return (
        layer_out.reshape(8, SIDE, D),
        grad_tiles.reshape(8, SIDE, D),
        grad_project_in,
        grad_project_out,
    )


def solution(mesh):
    fine = Mesh(mesh.devices.reshape(2, 4, 2, 2, 4), AXES)
    grid = P(("zh", "y", "c"), ("zl", "x"), None)
    rows = P(AXES, None)
    return jax.shard_map(
        body,
        mesh=fine,
        in_specs=(grid, P(("zh", "y", "c"), ("zl", "x")), rows, rows, grid),
        out_specs=(grid, grid, rows, rows),
        check_vma=False,
    )
```

```python
import jax
import jax.numpy as jnp
from jax import lax
from jax.experimental import pallas as pl
from jax.experimental.pallas import tpu as pltpu
from jax.sharding import Mesh, PartitionSpec as P

HEAD_DIM = 64
WINDOW = 7
D = 1536
DH = 768
HALF = DH // 2
GRID = 128
SIDE = 16
KEY_ROWS = 28
KEY_COLS = 32
QUERY_ROWS = 22
QUERY_COLS = 24
LANE = 128
WIDE = D + LANE

AXES = ("zh", "y", "c", "zl", "x")
STAGES = (("z", "y", "x"), ("x", "z", "y"))

epsilon = 1e-05
masked_score = -1e30
outside_score = -3e30
open_score = 3e38

f32 = jnp.float32
bf16 = jnp.bfloat16


def device(x, y, z, c):
    return (((z // 2 * 4 + y) * 2 + c) * 2 + z % 2) * 4 + x


def stage_pairs(axes, shift):
    pairs = []
    for x in range(4):
        for y in range(4):
            for z in range(4):
                for c in range(2):
                    place = {"x": x, "y": y, "z": z}
                    place[axes[c]] = (place[axes[c]] + shift) % 4
                    pairs.append((device(x, y, z, c), device(place["x"], place["y"], place["z"], c)))
    return pairs


def shifted(value, axes, shift):
    return lax.ppermute(value, AXES, stage_pairs(axes, shift))


def swap_cores(value):
    return lax.ppermute(value, "c", [(0, 1), (1, 0)])


def row_neighbour(value):
    pairs = [(r, r + 1 if r % 2 else r - 1) for r in range(16)]
    return lax.ppermute(value, ("zh", "y", "c"), [(a, b) for a, b in pairs if 0 <= b < 16])


def col_neighbour(value, step):
    pairs = [(i, i + step) for i in range(8)]
    return lax.ppermute(value, ("zl", "x"), [(a, b) for a, b in pairs if 0 <= b < 8])


def gather_stage(block, stage):
    axes = (STAGES[0][stage], STAGES[1][stage])
    far = shifted(block, axes, 2)
    near = shifted(block, axes, 1)
    back = shifted(block, axes, 3)
    return [block, near, far, back]


def gather_ring(block):
    axes = (STAGES[0][2], STAGES[1][2])
    return shifted(block, axes, 1), shifted(block, axes, 3)


def relay_ring(near, back):
    axes = (STAGES[0][2], STAGES[1][2])
    return shifted(near[:192], axes, 1), shifted(back[192:], axes, 3)


def scatter_stage(chunks, stage):
    axes = (STAGES[0][stage], STAGES[1][stage])
    far = shifted(chunks[2], axes, 2)
    near = shifted(chunks[1], axes, 3)
    back = shifted(chunks[3], axes, 1)
    return (chunks[0].astype(f32) + near.astype(f32)) + (far.astype(f32) + back.astype(f32))


def by_core(core, mine, other, axis):
    return jnp.where(
        core == 0,
        jnp.concatenate([mine, other], axis=axis),
        jnp.concatenate([other, mine], axis=axis),
    )


def on_chip(kernel, place, arrays, outs, scratch=(), megabytes=14):
    vmem = pl.BlockSpec(memory_space=pltpu.VMEM)
    return pl.pallas_call(
        kernel,
        out_shape=tuple(jax.ShapeDtypeStruct(shape, kind) for shape, kind in outs),
        in_specs=[pl.BlockSpec(memory_space=pltpu.SMEM)] + [vmem] * len(arrays),
        out_specs=(vmem,) * len(outs),
        scratch_shapes=[pltpu.VMEM(shape, kind) for shape, kind in scratch],
        compiler_params=pltpu.CompilerParams(vmem_limit_bytes=megabytes * 1024 * 1024),
        cost_estimate=pl.CostEstimate(flops=1000, bytes_accessed=1000, transcendentals=0),
    )(place, *arrays)


def normalize(values):
    center = values - jnp.mean(values, axis=-1, keepdims=True)
    inverse = lax.rsqrt(jnp.mean(center * center, axis=-1, keepdims=True) + epsilon)
    return (center * inverse, inverse)


def prepare_kernel(place_ref, tiles_ref, grad_ref, live_ref, hidden_out, grad_out, sent_out):
    core = place_ref[1]
    for r in range(8):
        at = pl.ds(r * SIDE, SIDE)
        normed, inverse = normalize(tiles_ref[at, :].astype(f32))
        live = live_ref[at, :]
        lanes = live.astype(bf16)
        hidden_out[at, :D] = normed.astype(bf16)
        hidden_out[at, D:] = lanes
        grad_out[at, :D] = (grad_ref[at, :].astype(f32) * live[:, :1]).astype(bf16)
        grad_out[at, D:] = lanes
    sent_out[:96, :] = hidden_out[pl.ds(pl.multiple_of(core * 32, 16), 96), :]
    sent_out[96:, :] = grad_out[pl.ds(pl.multiple_of(core * 80, 16), 48), :]


def columns_kernel(place_ref, hidden_ref, grad_ref, got_ref, a_out, b_out, right_out, left_out):
    core = place_ref[1]
    a_out[pl.ds(pl.multiple_of(core * 128, 32), 96), :] = got_ref[:96, :]
    a_out[pl.ds(pl.multiple_of((1 - core) * 96, 32), 128), :] = hidden_ref[...]
    b_out[pl.ds(pl.multiple_of(core * 128, 16), 48), :] = got_ref[96:, :]
    b_out[pl.ds(pl.multiple_of((1 - core) * 48, 16), 128), :] = grad_ref[...]
    b_out[176:, :] = jnp.zeros((SIDE, WIDE), bf16)
    upper = lax.broadcasted_iota(jnp.int32, (8, WIDE), 0) < 4
    for m in range(7):
        lines = a_out[32 * m : 32 * m + 32, :].astype(f32)
        right = [pltpu.roll(lines[16 * i + 8 : 16 * i + 16], 4, 0) for i in range(2)]
        right_out[16 * m : 16 * m + 16, :] = jnp.concatenate(right, axis=0).astype(bf16)
        left_out[16 * m : 16 * m + 16, :] = jnp.concatenate([lines[:8], lines[16:24]], axis=0).astype(bf16)
    for m in range(3):
        lines = b_out[64 * m : 64 * m + 64, :].astype(f32)
        right, left = [], []
        for i in (0, 32):
            right.append(jnp.where(upper, pltpu.roll(lines[i + 8 : i + 16], 4, 0), lines[i + 24 : i + 32]))
            left.append(jnp.where(upper, lines[i : i + 8], pltpu.roll(lines[i + 16 : i + 24], 4, 0)))
        at = slice(112 + 16 * m, 128 + 16 * m)
        right_out[at, :] = jnp.concatenate(right, axis=0).astype(bf16)
        left_out[at, :] = jnp.concatenate(left, axis=0).astype(bf16)


def widen_kernel(place_ref, a_ref, b_ref, left_ref, right_ref, a_out, b_out):
    upper = lax.broadcasted_iota(jnp.int32, (8, WIDE), 0) < 4
    for m in range(7):
        left = left_ref[16 * m : 16 * m + 16, :].astype(f32)
        right = right_ref[16 * m : 16 * m + 16, :].astype(f32)
        for i in range(2):
            at = KEY_COLS * (2 * m + i)
            a_out[at : at + SIDE, :] = a_ref[SIDE * (2 * m + i) : SIDE * (2 * m + i + 1), :]
            both = [left[8 * i : 8 * i + 8], right[8 * i : 8 * i + 8]]
            a_out[at + SIDE : at + KEY_COLS, :] = jnp.concatenate(both, axis=0).astype(bf16)
    for m in range(3):
        left = left_ref[112 + 16 * m : 128 + 16 * m, :].astype(f32)
        right = right_ref[112 + 16 * m : 128 + 16 * m, :].astype(f32)
        for i in range(2):
            lines = b_ref[64 * m + 32 * i : 64 * m + 32 * i + 32, :].astype(f32)
            left8, right8 = left[8 * i : 8 * i + 8], right[8 * i : 8 * i + 8]
            pieces = [
                lines[:SIDE],
                jnp.where(upper, left8, pltpu.roll(right8, 4, 0)),
                lines[SIDE:],
                jnp.where(upper, pltpu.roll(left8, 4, 0), right8),
            ]
            at = 2 * QUERY_COLS * (2 * m + i)
            b_out[at : at + 2 * QUERY_COLS, :] = jnp.concatenate(pieces, axis=0).astype(bf16)


def one_hot(hit):
    return jnp.where(hit, 1.0, 0.0).astype(bf16)


def permute_kernel(place_ref, tokens_ref, feature_ref, out):
    def part(n, carry):
        lanes = pl.ds(pl.multiple_of(n * 512, 512), 512)
        feature = lax.broadcasted_iota(jnp.int32, (D, 512), 0)
        order = one_hot(feature == feature_ref[:, lanes])
        out[:, lanes] = jnp.dot(tokens_ref[:, :D], order, preferred_element_type=f32).astype(bf16)
        return carry

    lax.fori_loop(0, D // 512, part, 0)


def out_rows_product(row_ref, part, first, chunk):
    row = row_ref[:, part * 384 : (part + 1) * 384]
    row = jnp.where(row < DH, row, row - DH)
    order = one_hot(lax.broadcasted_iota(jnp.int32, (768, D // 4), 0) + first == row)
    return jnp.dot(order, chunk, preferred_element_type=f32)


def by_half(chunk):
    upper = lax.broadcasted_iota(jnp.int32, chunk.shape, 0) % 24 < 12
    chunk = chunk.astype(f32)
    halves = [jnp.where(upper, chunk, 0.0), jnp.where(upper, 0.0, chunk)]
    return jnp.concatenate(halves, axis=1).astype(bf16)


def near_rows_kernel(place_ref, r0, r1, r3, row_ref, sums_out, halves):
    for i, ref in enumerate((r0, r1, r3)):
        halves[i, :, :] = by_half(ref[:, 3 * HALF :])

    def part(n, carry):
        first = pl.multiple_of(n * 768, 768)
        total = out_rows_product(row_ref, 0, first, halves[0])
        total += out_rows_product(row_ref, 1, first, halves[1])
        total += out_rows_product(row_ref, 3, first, halves[2])
        sums_out[pl.ds(first, 768), :] = total
        return carry

    lax.fori_loop(0, DH // 768, part, 0)


def out_rows_kernel(place_ref, sums_ref, r2_top, r2_low, row_ref, half_out, sent_out, halves):
    core = place_ref[1]
    halves[:192, :] = by_half(r2_top[:, 3 * HALF :])
    halves[192:, :] = by_half(r2_low[:, 3 * HALF :])

    def part(n, carry):
        first = pl.multiple_of(n * 768, 768)
        rows = pl.ds(first, 768)
        half_out[rows, :] = (sums_ref[rows, :] + out_rows_product(row_ref, 2, first, halves[...])).astype(bf16)
        return carry

    lax.fori_loop(0, DH // 768, part, 0)
    sent_out[...] = half_out[pl.ds(pl.multiple_of((1 - core) * HALF, HALF), HALF), :]


def packed_kernel(place_ref, mine_ref, other_ref, w0, w1, w2_top, w2_low, w3, packed, hidden, w2):
    core = place_ref[1]
    half = KEY_ROWS // 2 * KEY_COLS
    part = D // 4
    w2[:part, :] = w0[:, : 3 * HALF]
    w2[part : 2 * part, :] = w1[:, : 3 * HALF]
    w2[2 * part : 2 * part + 192, :] = w2_top[:, : 3 * HALF]
    w2[2 * part + 192 : 3 * part, :] = w2_low[:, : 3 * HALF]
    w2[3 * part :, :] = w3[:, : 3 * HALF]
    for source, side in ((mine_ref, core), (other_ref, 1 - core)):
        own_at = pl.multiple_of((1 - side) * 6 * KEY_COLS, KEY_COLS)
        for r in range(8):
            to = pl.ds(pl.multiple_of((side * 8 + r) * SIDE, SIDE), SIDE)
            hidden[to, :] = source[pl.ds(own_at + r * KEY_COLS, SIDE), :]

        to = pl.ds(pl.multiple_of(side * half, half), half)
        packed[to, :] = jnp.dot(source[...], w2[...], preferred_element_type=f32).astype(bf16)


def out_grads_kernel(place_ref, mine_ref, other_ref, grad_ref, row_ref, c0, c1, c2, c3):
    core = place_ref[1]
    over = (((0,), (0,)), ((), ()))
    part = D // 4
    inner = lax.broadcasted_iota(jnp.int32, (part, HALF), 0) % 24
    for k, chunk in enumerate((c0, c1, c2, c3)):
        row = row_ref[:, k * part : (k + 1) * part]
        row = jnp.where(row < DH, row, row - DH)
        picked = jnp.zeros((2 * LANE, part), f32)
        for attn, side in ((mine_ref, core), (other_ref, 1 - core)):
            order = one_hot(lax.broadcasted_iota(jnp.int32, (HALF, part), 0) + side * HALF == row)
            picked += jnp.dot(attn[...], order, preferred_element_type=f32)
        picked = picked.astype(bf16)
        first = lax.dot_general(picked, grad_ref[:, :HALF], over, preferred_element_type=f32)
        second = lax.dot_general(picked, grad_ref[:, HALF:], over, preferred_element_type=f32)
        chunk[...] = jnp.where(inner < 12, first, second).astype(bf16)


def grad_hidden_kernel(place_ref, grads_ref, w0, w1, w2_top, w2_low, w3, feature_ref, mine_out, sent_out, rel):
    core = place_ref[1]
    contract = (((1,), (1,)), ((), ()))
    far = jnp.concatenate([w2_top[:, : 3 * HALF], w2_low[:, : 3 * HALF]], axis=0)
    for k, chunk in enumerate((w0[:, : 3 * HALF], w1[:, : 3 * HALF], far, w3[:, : 3 * HALF])):
        rel[:, k * 384 : (k + 1) * 384] = lax.dot_general(
            grads_ref[...], chunk, contract, preferred_element_type=f32
        ).astype(bf16)

    def part(n, carry):
        first = pl.multiple_of(n * 256, 256)
        feature = lax.broadcasted_iota(jnp.int32, (256, D), 0) + first
        order = one_hot(feature == feature_ref[...])
        lanes = pl.ds(first, 256)
        both = lax.dot_general(rel[...], order, contract, preferred_element_type=f32)
        mine_out[:, lanes] = jnp.where(core == 0, both[:128], both[128:]).astype(bf16)
        sent_out[:, lanes] = jnp.where(core == 0, both[128:], both[:128]).astype(bf16)
        return carry

    lax.fori_loop(0, D // 256, part, 0)


def project_kernel(place_ref, mine_ref, other_ref, half_ref, mine_out, sent_out):
    core = place_ref[1]
    for side, out in ((core, mine_out), (1 - core, sent_out)):
        rows = pl.ds(pl.multiple_of(side * 128, 128), 128)
        total = jnp.dot(
            mine_ref[rows, :],
            half_ref[pl.ds(pl.multiple_of(core * HALF, HALF), HALF), :],
            preferred_element_type=f32,
        )
        total += jnp.dot(
            other_ref[rows, :],
            half_ref[pl.ds(pl.multiple_of((1 - core) * HALF, HALF), HALF), :],
            preferred_element_type=f32,
        )
        out[...] = total


def finish_kernel(
    place_ref, tiles_ref, grad_ref, live_ref, pmine_ref, pother_ref, gmine_ref, gother_ref, layer_out, tiles_out
):
    first = place_ref[1] == 0
    for r in range(8):
        at = pl.ds(r * SIDE, SIDE)
        tiles = tiles_ref[at, :].astype(f32)
        normed, inverse = normalize(tiles)
        live = live_ref[at, :][:, :1]
        mine, other = pmine_ref[at, :], pother_ref[at, :]
        low, high = jnp.where(first, mine, other), jnp.where(first, other, mine)
        layer_out[at, :DH] = (tiles[:, :DH] + low * live).astype(bf16)
        layer_out[at, DH:] = (tiles[:, DH:] + high * live).astype(bf16)
        grad_hidden = gmine_ref[at, :].astype(f32) + gother_ref[at, :].astype(f32)
        grad_norm = inverse * (
            grad_hidden
            - jnp.mean(grad_hidden, axis=-1, keepdims=True)
            - normed * jnp.mean(grad_hidden * normed, axis=-1, keepdims=True)
        )
        tiles_out[at, :] = (grad_ref[at, :].astype(f32) + grad_norm).astype(bf16)


def layer_kernel(
    place_ref, packed, hidden, amine_ref, aother_ref, gmine_ref, gother_ref, rmine_ref, rother_ref,
    attn_out, grads_out, c0, c1, c2, c3, grad_own,
    grad_attn, dk, dv, attn, dq, tissue, lines_f32,
):
    base, core, column = place_ref[0], place_ref[1], place_ref[2]
    width = 2 * QUERY_COLS
    span = 8 * KEY_COLS
    half = KEY_ROWS // 2 * KEY_COLS
    half_q = QUERY_ROWS // 2 * QUERY_COLS
    contract = (((1,), (1,)), ((), ()))
    over = (((0,), (0,)), ((), ()))
    part = D // 4

    dk[...] = jnp.zeros_like(dk)
    dv[...] = jnp.zeros_like(dv)

    mine_lanes = pl.ds(pl.multiple_of(core * DH, DH), DH)
    other_lanes = pl.ds(pl.multiple_of((1 - core) * DH, DH), DH)
    rmine = rmine_ref[pl.ds(pl.multiple_of(core * HALF, HALF), HALF), :]
    for source, side in ((gmine_ref, core), (gother_ref, 1 - core)):
        to = pl.ds(pl.multiple_of(side * half_q, 8), half_q)
        total = lax.dot_general(source[:, mine_lanes], rmine, contract, preferred_element_type=f32)
        total += lax.dot_general(source[:, other_lanes], rother_ref[...], contract, preferred_element_type=f32)
        grad_attn[to, :] = total[:half_q].astype(bf16).astype(f32)

    for source, side in ((gmine_ref, core), (gother_ref, 1 - core)):
        lines_f32[...] = source[:, mine_lanes].astype(f32)
        for r in range(8):
            own = lines_f32[pl.ds(pl.multiple_of((1 - side) * 72 + 24 * r, 8), SIDE), :]
            grad_own[pl.ds(pl.multiple_of((side * 8 + r) * SIDE, SIDE), SIDE), :] = own.astype(bf16)

    for source, side in ((amine_ref, core), (aother_ref, 1 - core)):
        tissue[pl.ds(pl.multiple_of(side * half, 64), half), :] = source[:, D:].astype(f32)
    alive_line = jnp.concatenate(
        [jnp.transpose(tissue[m * LANE : (m + 1) * LANE, :])[:8] for m in range(7)] + [jnp.zeros((8, LANE), f32)], axis=1
    )
    alive_line = jnp.where(alive_line > 0, open_score, masked_score)
    spot = lax.broadcasted_iota(jnp.int32, (QUERY_COLS, span), 1) % KEY_COLS
    key_col = jnp.where(spot < 16, spot, jnp.where(spot < 20, spot - 20, jnp.where(spot < 24, spot - 28, spot - 8)))
    spot = lax.broadcasted_iota(jnp.int32, (QUERY_COLS, span), 0)
    query_col = jnp.where(spot < 16, spot, jnp.where(spot < 20, spot - 20, spot - 4))
    col_start = jnp.clip(query_col + column - 3, 0, GRID - WINDOW)
    key_col = key_col + column
    col_in = jnp.logical_and(key_col >= col_start, key_col < col_start + WINDOW)
    col_cap = jnp.where(col_in, open_score, outside_score)

    key_line = lax.broadcasted_iota(jnp.int32, (1, span), 1) // KEY_COLS
    low = lax.broadcasted_iota(jnp.int32, (width, LANE), 1) < HEAD_DIM
    low2 = jnp.concatenate([low, jnp.logical_not(low)], axis=0)
    upper = lax.broadcasted_iota(jnp.int32, (8, LANE), 0) < 4

    def block(i, carry):
        row = base - 3 + 2 * i
        start = jnp.clip(row - 3, 0, GRID - 8)
        local = start - (base - 6)
        alive = pltpu.roll(alive_line, lax.rem((32 - local) * KEY_COLS, 32 * KEY_COLS), 1)[:1, :span]
        key_row = key_line + start
        caps = []
        for step in range(2):
            first = jnp.clip(row + step - 3, 0, GRID - WINDOW)
            inside = jnp.logical_and(key_row >= first, key_row < first + WINDOW)
            caps.append(jnp.minimum(col_cap, jnp.where(inside, alive, outside_score)))
        cap = jnp.concatenate(caps + caps, axis=0)
        keys_at = pl.ds(pl.multiple_of(local * KEY_COLS, KEY_COLS), span)
        query_at = pl.multiple_of((3 + 2 * i) * KEY_COLS, KEY_COLS)
        block_at = pl.ds(pl.multiple_of(i * width, width), width)
        groups = range(3)
        lanes = [pl.ds(g * LANE, LANE) for g in groups]
        key = [packed[keys_at, pl.ds(HALF + g * LANE, LANE)] for g in groups]
        value = [packed[keys_at, pl.ds(2 * HALF + g * LANE, LANE)] for g in groups]
        query2, grad2f = [], []
        for g in groups:
            lines = packed[pl.ds(query_at, 2 * KEY_COLS), lanes[g]].astype(f32) * HEAD_DIM ** (-0.5)
            pieces = []
            for step in range(2):
                line = lines[step * KEY_COLS : (step + 1) * KEY_COLS]
                pieces += [line[:SIDE], jnp.where(upper, line[16:24], pltpu.roll(line[24:32], 4, 0))]
            query2.append(jnp.where(low2, jnp.concatenate(pieces + pieces, axis=0), 0.0).astype(bf16))
            grad = grad_attn[block_at, lanes[g]]
            grad2f.append(jnp.where(low2, jnp.concatenate([grad, grad], axis=0), 0.0))
        grad2 = [g.astype(bf16) for g in grad2f]
        raw = [lax.dot_general(query2[g], key[g], contract, preferred_element_type=f32) for g in groups]
        grad_prob = [lax.dot_general(grad2[g], value[g], contract, preferred_element_type=f32) for g in groups]
        prob = []
        for g in groups:
            scores = jnp.minimum(raw[g], cap)
            expon = jnp.exp(scores - jnp.max(scores, axis=1, keepdims=True))
            prob.append(expon * (1.0 / jnp.sum(expon, axis=1, keepdims=True)))
        weights = [p.astype(bf16) for p in prob]
        mixed = [jnp.dot(weights[g], value[g], preferred_element_type=f32).astype(bf16).astype(f32) for g in groups]
        value_sum = [lax.dot_general(weights[g], grad2[g], over, preferred_element_type=f32) for g in groups]
        delta = [jnp.sum(grad2f[g] * mixed[g], axis=1, keepdims=True) for g in groups]
        grad_score = [(prob[g] * (grad_prob[g] - delta[g])).astype(bf16) for g in groups]
        grad_q = [jnp.dot(grad_score[g], key[g], preferred_element_type=f32) for g in groups]
        key_sum = [lax.dot_general(grad_score[g], query2[g], over, preferred_element_type=f32) for g in groups]
        for g in groups:
            attn[block_at, lanes[g]] = jnp.where(low, mixed[g][:width], mixed[g][width:])
            dq[block_at, lanes[g]] = jnp.where(low, grad_q[g][:width], grad_q[g][width:])
            dv[keys_at, lanes[g]] += value_sum[g]
            dk[keys_at, lanes[g]] += key_sum[g]
        return carry

    lax.fori_loop(0, QUERY_ROWS // 2, block, 0, unroll=True)
    for r in range(SIDE):
        own = pl.ds(r * SIDE, SIDE)
        at_query = pl.ds((r + 3) * QUERY_COLS, SIDE)
        at_key = pl.ds((r + 6) * KEY_COLS, SIDE)
        attn_out[own, :] = attn[at_query, :].astype(bf16)
        grads_out[own, :HALF] = (dq[at_query, :] * HEAD_DIM ** (-0.5)).astype(bf16)
        grads_out[own, HALF : 2 * HALF] = dk[at_key, :].astype(bf16)
        grads_out[own, 2 * HALF :] = dv[at_key, :].astype(bf16)
    for k, chunk in enumerate((c0, c1, c2, c3)):
        chunk[...] = lax.dot_general(
            hidden[:, k * part : (k + 1) * part], grads_out[...], over, preferred_element_type=f32
        ).astype(bf16)


def layer(place, *arrays):
    keys, queries = KEY_ROWS * KEY_COLS, QUERY_ROWS * QUERY_COLS
    return on_chip(
        layer_kernel,
        place,
        arrays,
        [((SIDE * SIDE, HALF), bf16), ((SIDE * SIDE, 3 * HALF), bf16)] + [((D // 4, 3 * HALF), bf16)] * 4 + [((SIDE * SIDE, DH), bf16)],
        [
            ((queries, HALF), f32),
            ((keys, HALF), f32),
            ((keys, HALF), f32),
            ((queries, HALF), f32),
            ((queries, HALF), f32),
            ((keys, LANE), f32),
            ((288, DH), f32),
        ],
        30,
    )


def found_places(core, here, place):
    step = [(place // 24) % 4, (place // 96) % 4, place // 384]
    found = {}
    for name in ("x", "y", "z"):
        mine = [lax.rem(here[name] - step[STAGES[c].index(name)] + 4, 4) for c in range(2)]
        found[name] = jnp.where(core == 0, mine[0], mine[1])
    return found


def orders(core, here, place):
    found, inner = found_places(core, here, place), place % 24

    def owner(side):
        return (((found["z"] // 2 * 4 + found["y"]) * 2 + side) * 2 + found["z"] % 2) * 4 + found["x"]

    feature = owner(inner // 12) * 12 + inner % 12
    row = owner(inner % 12 // 6) * 6 + inner % 6 + inner // 12 * DH
    return feature, row


def body(tiles, tissue, project_in, project_out, grad_layer):
    zh, y, core, zl, x = [lax.axis_index(name) for name in AXES]
    z = zh * 2 + zl
    tokens = 8 * SIDE
    place = jnp.stack([(zh * 4 + y) * SIDE, core, (zl * 4 + x) * SIDE]).astype(jnp.int32)

    halves = project_in.reshape(12, 3, 2, HALF)
    first, second = halves[:, :, 0].reshape(12, 3 * HALF), halves[:, :, 1].reshape(12, 3 * HALF)

    def shard(of_in, of_out):
        return jnp.concatenate([of_in, of_out.reshape(6, 2, HALF).transpose(1, 0, 2).reshape(12, HALF)], axis=1)

    shard_first, shard_second = shard(first, project_out[:, :DH]), shard(second, project_out[:, DH:])
    mine = jnp.where(core == 0, shard_first, shard_second)
    theirs = jnp.where(core == 0, shard_second, shard_first)
    other = swap_cores(theirs)
    here = {"x": x, "y": y, "z": z}
    feature_line, row_line = orders(core, here, lax.broadcasted_iota(jnp.int32, (1, D), 1))
    flat_tiles, flat_grad = tiles.reshape(tokens, D), grad_layer.reshape(tokens, D)
    live = jnp.broadcast_to(tissue.reshape(tokens, 1).astype(f32), (tokens, LANE))
    own_hidden, own_grad, sent = on_chip(
        prepare_kernel,
        place,
        [flat_tiles, flat_grad, live],
        [((tokens, WIDE), bf16), ((tokens, WIDE), bf16), ((144, WIDE), bf16)],
    )
    block_in = by_core(core, mine[:, : 3 * HALF], other[:, : 3 * HALF], 0)
    mine_out, other_out = mine[:, 3 * HALF :].reshape(2, 6, HALF), other[:, 3 * HALF :].reshape(2, 6, HALF)
    block_out = by_core(core, mine_out, other_out, 1).reshape(24, HALF)
    block = jnp.concatenate([block_in, block_out], axis=1)
    block, sent, feature_line, row_line = lax.optimization_barrier((block, sent, feature_line, row_line))

    parts = gather_stage(block, 0)
    got = row_neighbour(sent)
    *parts, got = lax.optimization_barrier((*parts, got))
    block = jnp.concatenate(parts, axis=0)
    a, b, to_right, to_left = on_chip(
        columns_kernel,
        place,
        [own_hidden, own_grad, got],
        [((224, WIDE), bf16), ((192, WIDE), bf16), ((160, WIDE), bf16), ((160, WIDE), bf16)],
    )
    block, to_right, to_left = lax.optimization_barrier((block, to_right, to_left))

    parts = gather_stage(block, 1)
    left, right = col_neighbour(to_right, 1), col_neighbour(to_left, -1)
    block = lax.optimization_barrier(jnp.concatenate(parts, axis=0))

    near, back = gather_ring(block)
    wide_a, wide_b = on_chip(
        widen_kernel, place, [a, b, left, right], [((14 * KEY_COLS, WIDE), bf16), ((12 * QUERY_COLS, WIDE), bf16)]
    )
    other_a, other_b = swap_cores(wide_a), swap_cores(wide_b)
    permuted = [((14 * KEY_COLS, D), bf16)]
    (hidden_mine,) = on_chip(permute_kernel, place, [wide_a, feature_line], permuted)
    (hidden_other,) = on_chip(permute_kernel, place, [other_a, feature_line], permuted)

    hidden_mine, near, back = lax.optimization_barrier((hidden_mine, near, back))
    weights = [block, near, *relay_ring(near, back), back]
    hidden_other, row_line = lax.optimization_barrier((hidden_other, row_line))
    (near_rows,) = on_chip(near_rows_kernel, place, [block, near, back, row_line], [((DH, DH), f32)], [((3, D // 4, DH), bf16)])
    half_out, sent_rows = on_chip(
        out_rows_kernel,
        place,
        [near_rows, weights[2], weights[3], row_line],
        [((DH, DH), bf16), ((HALF, DH), bf16)],
        [((D // 4, DH), bf16)],
    )
    other_rows = swap_cores(sent_rows)
    packed, hidden = on_chip(
        packed_kernel,
        place,
        [hidden_mine, hidden_other, *weights],
        [((KEY_ROWS * KEY_COLS, 3 * HALF), bf16), ((SIDE * SIDE, D), bf16)],
        [((D, 3 * HALF), bf16)],
    )

    attention, grad_packed, *chunks_in, grad_own = layer(
        place, packed, hidden, wide_a, other_a, wide_b, other_b, half_out, other_rows
    )
    axes = (STAGES[0][2], STAGES[1][2])
    far, near, back = shifted(chunks_in[2], axes, 2), shifted(chunks_in[1], axes, 3), shifted(chunks_in[3], axes, 1)

    attention_other = swap_cores(attention)
    hidden_kept, hidden_sent = on_chip(
        grad_hidden_kernel,
        place,
        [grad_packed, *weights, feature_line],
        [((tokens, D), bf16)] * 2,
        [((2 * tokens, D), bf16)],
    )
    attention_other, hidden_kept, hidden_sent = lax.optimization_barrier((attention_other, hidden_kept, hidden_sent))
    chunks_out = on_chip(
        out_grads_kernel,
        place,
        [attention, attention_other, grad_own, row_line],
        [((D // 4, HALF), bf16)] * 4,
    )
    projected, projected_sent = on_chip(
        project_kernel, place, [attention, attention_other, half_out], [((tokens, DH), f32)] * 2
    )
    far_out, near_out = shifted(chunks_out[2], axes, 2), shifted(chunks_out[1], axes, 3)
    total_in, back_out = lax.optimization_barrier((chunks_in[0].astype(f32) + near.astype(f32), chunks_out[3]))
    back_out = shifted(back_out, axes, 1)
    total_in = total_in + (far.astype(f32) + back.astype(f32))
    total_out = (chunks_out[0].astype(f32) + near_out.astype(f32)) + (far_out.astype(f32) + back_out.astype(f32))
    total = jnp.concatenate([total_in, total_out], axis=1).astype(bf16)
    total, hidden_kept, hidden_sent, projected, projected_sent = lax.optimization_barrier(
        (total, hidden_kept, hidden_sent, projected, projected_sent)
    )
    total = scatter_stage([total[k * 96 : (k + 1) * 96] for k in range(4)], 1).astype(bf16)
    layer_out, grad_tiles = on_chip(
        finish_kernel,
        place,
        [flat_tiles, flat_grad, live, projected, swap_cores(projected_sent), hidden_kept, swap_cores(hidden_sent)],
        [((tokens, D), bf16)] * 2,
    )
    total = scatter_stage([total[k * 24 : (k + 1) * 24] for k in range(4)], 0)

    sums_in = total[:, : 3 * HALF].reshape(2, 12, 3 * HALF)
    sums_out = total[:, 3 * HALF :].reshape(2, 2, 6, HALF).transpose(1, 0, 2, 3).reshape(2, 12, HALF)
    sums = jnp.concatenate([sums_in, sums_out], axis=2)
    kept = jnp.where(core == 0, sums[0], sums[1])
    gotten = swap_cores(jnp.where(core == 0, sums[1], sums[0]))
    gotten, layer_out, grad_tiles = lax.optimization_barrier((gotten, layer_out, grad_tiles))
    grad_project_in = by_core(
        core, kept[:, : 3 * HALF].reshape(12, 3, 1, HALF), gotten[:, : 3 * HALF].reshape(12, 3, 1, HALF), 2
    ).reshape(12, 3 * DH)
    kept_out = kept[:, 3 * HALF :].reshape(2, 6, HALF).transpose(1, 0, 2).reshape(6, DH)
    gotten_out = gotten[:, 3 * HALF :].reshape(2, 6, HALF).transpose(1, 0, 2).reshape(6, DH)
    grad_project_out = by_core(core, kept_out, gotten_out, 1)

    return (
        layer_out.reshape(8, SIDE, D),
        grad_tiles.reshape(8, SIDE, D),
        grad_project_in,
        grad_project_out,
    )


def solution(mesh):
    fine = Mesh(mesh.devices.reshape(2, 4, 2, 2, 4), AXES)
    grid = P(("zh", "y", "c"), ("zl", "x"), None)
    rows = P(AXES, None)
    return jax.shard_map(
        body,
        mesh=fine,
        in_specs=(grid, P(("zh", "y", "c"), ("zl", "x")), rows, rows, grid),
        out_specs=(grid, grid, rows, rows),
        check_vma=False,
    )
```

```python
import jax
import jax.numpy as jnp
from jax import lax
from jax.experimental import pallas as pl
from jax.experimental.pallas import tpu as pltpu
from jax.sharding import Mesh, PartitionSpec as P

HEAD_DIM = 64
WINDOW = 7
D = 1536
DH = 768
HALF = DH // 2
GRID = 128
SIDE = 16
KEY_ROWS = 28
KEY_COLS = 32
QUERY_ROWS = 22
QUERY_COLS = 24
LANE = 128
WIDE = D + LANE

AXES = ("zh", "y", "c", "zl", "x")
STAGES = (("z", "y", "x"), ("x", "z", "y"))

epsilon = 1e-05
masked_score = -1e30
outside_score = -3e30
open_score = 3e38

f32 = jnp.float32
bf16 = jnp.bfloat16


def device(x, y, z, c):
    return (((z // 2 * 4 + y) * 2 + c) * 2 + z % 2) * 4 + x


def stage_pairs(axes, shift):
    pairs = []
    for x in range(4):
        for y in range(4):
            for z in range(4):
                for c in range(2):
                    place = {"x": x, "y": y, "z": z}
                    place[axes[c]] = (place[axes[c]] + shift) % 4
                    pairs.append((device(x, y, z, c), device(place["x"], place["y"], place["z"], c)))
    return pairs


def shifted(value, axes, shift):
    return lax.ppermute(value, AXES, stage_pairs(axes, shift))


def swap_cores(value):
    return lax.ppermute(value, "c", [(0, 1), (1, 0)])


def row_neighbour(value):
    pairs = [(r, r + 1 if r % 2 else r - 1) for r in range(16)]
    return lax.ppermute(value, ("zh", "y", "c"), [(a, b) for a, b in pairs if 0 <= b < 16])


def col_neighbour(value, step):
    pairs = [(i, i + step) for i in range(8)]
    return lax.ppermute(value, ("zl", "x"), [(a, b) for a, b in pairs if 0 <= b < 8])


def gather_stage(block, stage):
    axes = (STAGES[0][stage], STAGES[1][stage])
    far = shifted(block, axes, 2)
    near = shifted(block, axes, 1)
    back = shifted(block, axes, 3)
    return [block, near, far, back]


def gather_ring(block):
    axes = (STAGES[0][2], STAGES[1][2])
    return shifted(block, axes, 1), shifted(block, axes, 3)


def relay_ring(near, back):
    axes = (STAGES[0][2], STAGES[1][2])
    return shifted(near[:192], axes, 1), shifted(back[192:], axes, 3)


def scatter_stage(chunks, stage):
    axes = (STAGES[0][stage], STAGES[1][stage])
    far = shifted(chunks[2], axes, 2)
    near = shifted(chunks[1], axes, 3)
    back = shifted(chunks[3], axes, 1)
    return (chunks[0].astype(f32) + near.astype(f32)) + (far.astype(f32) + back.astype(f32))


def by_core(core, mine, other, axis):
    return jnp.where(
        core == 0,
        jnp.concatenate([mine, other], axis=axis),
        jnp.concatenate([other, mine], axis=axis),
    )


def on_chip(kernel, place, arrays, outs, scratch=(), megabytes=14):
    vmem = pl.BlockSpec(memory_space=pltpu.VMEM)
    return pl.pallas_call(
        kernel,
        out_shape=tuple(jax.ShapeDtypeStruct(shape, kind) for shape, kind in outs),
        in_specs=[pl.BlockSpec(memory_space=pltpu.SMEM)] + [vmem] * len(arrays),
        out_specs=(vmem,) * len(outs),
        scratch_shapes=[pltpu.VMEM(shape, kind) for shape, kind in scratch],
        compiler_params=pltpu.CompilerParams(vmem_limit_bytes=megabytes * 1024 * 1024),
        cost_estimate=pl.CostEstimate(flops=1000, bytes_accessed=1000, transcendentals=0),
    )(place, *arrays)


def normalize(values):
    center = values - jnp.mean(values, axis=-1, keepdims=True)
    inverse = lax.rsqrt(jnp.mean(center * center, axis=-1, keepdims=True) + epsilon)
    return (center * inverse, inverse)


def prepare_kernel(place_ref, tiles_ref, grad_ref, live_ref, hidden_out, grad_out, sent_out):
    core = place_ref[1]
    for r in range(8):
        at = pl.ds(r * SIDE, SIDE)
        normed, inverse = normalize(tiles_ref[at, :].astype(f32))
        live = live_ref[at, :]
        lanes = live.astype(bf16)
        hidden_out[at, :D] = normed.astype(bf16)
        hidden_out[at, D:] = lanes
        grad_out[at, :D] = (grad_ref[at, :].astype(f32) * live[:, :1]).astype(bf16)
        grad_out[at, D:] = lanes
    sent_out[:96, :] = hidden_out[pl.ds(pl.multiple_of(core * 32, 16), 96), :]
    sent_out[96:, :] = grad_out[pl.ds(pl.multiple_of(core * 80, 16), 48), :]


def columns_kernel(place_ref, hidden_ref, grad_ref, got_ref, a_out, b_out, right_out, left_out):
    core = place_ref[1]
    a_out[pl.ds(pl.multiple_of(core * 128, 32), 96), :] = got_ref[:96, :]
    a_out[pl.ds(pl.multiple_of((1 - core) * 96, 32), 128), :] = hidden_ref[...]
    b_out[pl.ds(pl.multiple_of(core * 128, 16), 48), :] = got_ref[96:, :]
    b_out[pl.ds(pl.multiple_of((1 - core) * 48, 16), 128), :] = grad_ref[...]
    b_out[176:, :] = jnp.zeros((SIDE, WIDE), bf16)
    upper = lax.broadcasted_iota(jnp.int32, (8, WIDE), 0) < 4
    for m in range(7):
        lines = a_out[32 * m : 32 * m + 32, :].astype(f32)
        right = [pltpu.roll(lines[16 * i + 8 : 16 * i + 16], 4, 0) for i in range(2)]
        right_out[16 * m : 16 * m + 16, :] = jnp.concatenate(right, axis=0).astype(bf16)
        left_out[16 * m : 16 * m + 16, :] = jnp.concatenate([lines[:8], lines[16:24]], axis=0).astype(bf16)
    for m in range(3):
        lines = b_out[64 * m : 64 * m + 64, :].astype(f32)
        right, left = [], []
        for i in (0, 32):
            right.append(jnp.where(upper, pltpu.roll(lines[i + 8 : i + 16], 4, 0), lines[i + 24 : i + 32]))
            left.append(jnp.where(upper, lines[i : i + 8], pltpu.roll(lines[i + 16 : i + 24], 4, 0)))
        at = slice(112 + 16 * m, 128 + 16 * m)
        right_out[at, :] = jnp.concatenate(right, axis=0).astype(bf16)
        left_out[at, :] = jnp.concatenate(left, axis=0).astype(bf16)


def widen_kernel(place_ref, a_ref, b_ref, left_ref, right_ref, a_out, b_out):
    upper = lax.broadcasted_iota(jnp.int32, (8, WIDE), 0) < 4
    for m in range(7):
        left = left_ref[16 * m : 16 * m + 16, :].astype(f32)
        right = right_ref[16 * m : 16 * m + 16, :].astype(f32)
        for i in range(2):
            at = KEY_COLS * (2 * m + i)
            a_out[at : at + SIDE, :] = a_ref[SIDE * (2 * m + i) : SIDE * (2 * m + i + 1), :]
            both = [left[8 * i : 8 * i + 8], right[8 * i : 8 * i + 8]]
            a_out[at + SIDE : at + KEY_COLS, :] = jnp.concatenate(both, axis=0).astype(bf16)
    for m in range(3):
        left = left_ref[112 + 16 * m : 128 + 16 * m, :].astype(f32)
        right = right_ref[112 + 16 * m : 128 + 16 * m, :].astype(f32)
        for i in range(2):
            lines = b_ref[64 * m + 32 * i : 64 * m + 32 * i + 32, :].astype(f32)
            left8, right8 = left[8 * i : 8 * i + 8], right[8 * i : 8 * i + 8]
            pieces = [
                lines[:SIDE],
                jnp.where(upper, left8, pltpu.roll(right8, 4, 0)),
                lines[SIDE:],
                jnp.where(upper, pltpu.roll(left8, 4, 0), right8),
            ]
            at = 2 * QUERY_COLS * (2 * m + i)
            b_out[at : at + 2 * QUERY_COLS, :] = jnp.concatenate(pieces, axis=0).astype(bf16)


def one_hot(hit):
    return jnp.where(hit, 1.0, 0.0).astype(bf16)


def permute_kernel(place_ref, tokens_ref, feature_ref, out):
    def part(n, carry):
        lanes = pl.ds(pl.multiple_of(n * 512, 512), 512)
        feature = lax.broadcasted_iota(jnp.int32, (D, 512), 0)
        order = one_hot(feature == feature_ref[:, lanes])
        out[:, lanes] = jnp.dot(tokens_ref[:, :D], order, preferred_element_type=f32).astype(bf16)
        return carry

    lax.fori_loop(0, D // 512, part, 0)


def out_rows_product(row_ref, part, first, chunk):
    row = row_ref[:, part * 384 : (part + 1) * 384]
    row = jnp.where(row < DH, row, row - DH)
    order = one_hot(lax.broadcasted_iota(jnp.int32, (768, D // 4), 0) + first == row)
    return jnp.dot(order, chunk, preferred_element_type=f32)


def by_half(chunk):
    upper = lax.broadcasted_iota(jnp.int32, chunk.shape, 0) % 24 < 12
    chunk = chunk.astype(f32)
    halves = [jnp.where(upper, chunk, 0.0), jnp.where(upper, 0.0, chunk)]
    return jnp.concatenate(halves, axis=1).astype(bf16)


def near_rows_kernel(place_ref, r0, r1, r3, row_ref, sums_out, halves):
    for i, ref in enumerate((r0, r1, r3)):
        halves[i, :, :] = by_half(ref[:, 3 * HALF :])

    def part(n, carry):
        first = pl.multiple_of(n * 768, 768)
        total = out_rows_product(row_ref, 0, first, halves[0])
        total += out_rows_product(row_ref, 1, first, halves[1])
        total += out_rows_product(row_ref, 3, first, halves[2])
        sums_out[pl.ds(first, 768), :] = total
        return carry

    lax.fori_loop(0, DH // 768, part, 0)


def out_rows_kernel(place_ref, sums_ref, r2_top, r2_low, row_ref, half_out, sent_out, halves):
    core = place_ref[1]
    halves[:192, :] = by_half(r2_top[:, 3 * HALF :])
    halves[192:, :] = by_half(r2_low[:, 3 * HALF :])

    def part(n, carry):
        first = pl.multiple_of(n * 768, 768)
        rows = pl.ds(first, 768)
        half_out[rows, :] = (sums_ref[rows, :] + out_rows_product(row_ref, 2, first, halves[...])).astype(bf16)
        return carry

    lax.fori_loop(0, DH // 768, part, 0)
    sent_out[...] = half_out[pl.ds(pl.multiple_of((1 - core) * HALF, HALF), HALF), :]


def packed_kernel(place_ref, mine_ref, other_ref, w0, w1, w2_top, w2_low, w3, packed, hidden, w2):
    core = place_ref[1]
    half = KEY_ROWS // 2 * KEY_COLS
    part = D // 4
    w2[:part, :] = w0[:, : 3 * HALF]
    w2[part : 2 * part, :] = w1[:, : 3 * HALF]
    w2[2 * part : 2 * part + 192, :] = w2_top[:, : 3 * HALF]
    w2[2 * part + 192 : 3 * part, :] = w2_low[:, : 3 * HALF]
    w2[3 * part :, :] = w3[:, : 3 * HALF]
    for source, side in ((mine_ref, core), (other_ref, 1 - core)):
        own_at = pl.multiple_of((1 - side) * 6 * KEY_COLS, KEY_COLS)
        for r in range(8):
            to = pl.ds(pl.multiple_of((side * 8 + r) * SIDE, SIDE), SIDE)
            hidden[to, :] = source[pl.ds(own_at + r * KEY_COLS, SIDE), :]

        to = pl.ds(pl.multiple_of(side * half, half), half)
        packed[to, :] = jnp.dot(source[...], w2[...], preferred_element_type=f32).astype(bf16)


def out_grads_kernel(place_ref, mine_ref, other_ref, grad_ref, row_ref, c0, c1, c2, c3):
    core = place_ref[1]
    over = (((0,), (0,)), ((), ()))
    part = D // 4
    inner = lax.broadcasted_iota(jnp.int32, (part, HALF), 0) % 24
    for k, chunk in enumerate((c0, c1, c2, c3)):
        row = row_ref[:, k * part : (k + 1) * part]
        row = jnp.where(row < DH, row, row - DH)
        picked = jnp.zeros((2 * LANE, part), f32)
        for attn, side in ((mine_ref, core), (other_ref, 1 - core)):
            order = one_hot(lax.broadcasted_iota(jnp.int32, (HALF, part), 0) + side * HALF == row)
            picked += jnp.dot(attn[...], order, preferred_element_type=f32)
        picked = picked.astype(bf16)
        first = lax.dot_general(picked, grad_ref[:, :HALF], over, preferred_element_type=f32)
        second = lax.dot_general(picked, grad_ref[:, HALF:], over, preferred_element_type=f32)
        chunk[...] = jnp.where(inner < 12, first, second).astype(bf16)


def grad_hidden_kernel(place_ref, grads_ref, w0, w1, w2_top, w2_low, w3, feature_ref, mine_out, sent_out, rel):
    core = place_ref[1]
    contract = (((1,), (1,)), ((), ()))
    far = jnp.concatenate([w2_top[:, : 3 * HALF], w2_low[:, : 3 * HALF]], axis=0)
    for k, chunk in enumerate((w0[:, : 3 * HALF], w1[:, : 3 * HALF], far, w3[:, : 3 * HALF])):
        rel[:, k * 384 : (k + 1) * 384] = lax.dot_general(
            grads_ref[...], chunk, contract, preferred_element_type=f32
        ).astype(bf16)

    def part(n, carry):
        first = pl.multiple_of(n * 256, 256)
        feature = lax.broadcasted_iota(jnp.int32, (256, D), 0) + first
        order = one_hot(feature == feature_ref[...])
        lanes = pl.ds(first, 256)
        both = lax.dot_general(rel[...], order, contract, preferred_element_type=f32)
        mine_out[:, lanes] = jnp.where(core == 0, both[:128], both[128:]).astype(bf16)
        sent_out[:, lanes] = jnp.where(core == 0, both[128:], both[:128]).astype(bf16)
        return carry

    lax.fori_loop(0, D // 256, part, 0)


def last_sum_kernel(place_ref, own_ref, near_ref, far_ref, back_ref, kept_out, sent_out):
    first = place_ref[1] == 0
    total = (own_ref[...].astype(f32) + near_ref[...].astype(f32)) + (
        far_ref[...].astype(f32) + back_ref[...].astype(f32)
    )
    left, right = total[:, : 3 * HALF], total[:, 3 * HALF :]
    lefts = (left[:12], left[12:])
    rights = [jnp.concatenate([right[6 * i : 6 * i + 6], right[12 + 6 * i : 18 + 6 * i]], axis=0) for i in range(2)]
    for out, mine in ((kept_out, first), (sent_out, jnp.logical_not(first))):
        out[:, : 3 * HALF] = jnp.where(mine, lefts[0], lefts[1])
        out[:, 3 * HALF :] = jnp.where(mine, rights[0], rights[1])


def unpack_kernel(place_ref, kept_ref, got_ref, in_out, out_out):
    first = place_ref[1] == 0
    kept, got = kept_ref[...], got_ref[...]
    for half, value in enumerate((jnp.where(first, kept, got), jnp.where(first, got, kept))):
        for t in range(3):
            lanes = slice(t * DH + half * HALF, t * DH + half * HALF + HALF)
            in_out[:, lanes] = value[:, t * HALF : (t + 1) * HALF]
        for h in range(2):
            lanes = slice(half * DH + h * HALF, half * DH + h * HALF + HALF)
            out_out[:, lanes] = value[6 * h : 6 * h + 6, 3 * HALF :]


def project_kernel(place_ref, mine_ref, other_ref, half_ref, mine_out, sent_out):
    core = place_ref[1]
    for side, out in ((core, mine_out), (1 - core, sent_out)):
        rows = pl.ds(pl.multiple_of(side * 128, 128), 128)
        total = jnp.dot(
            mine_ref[rows, :],
            half_ref[pl.ds(pl.multiple_of(core * HALF, HALF), HALF), :],
            preferred_element_type=f32,
        )
        total += jnp.dot(
            other_ref[rows, :],
            half_ref[pl.ds(pl.multiple_of((1 - core) * HALF, HALF), HALF), :],
            preferred_element_type=f32,
        )
        out[...] = total


def finish_kernel(
    place_ref, tiles_ref, grad_ref, live_ref, pmine_ref, pother_ref, gmine_ref, gother_ref, layer_out, tiles_out
):
    first = place_ref[1] == 0
    for r in range(8):
        at = pl.ds(r * SIDE, SIDE)
        tiles = tiles_ref[at, :].astype(f32)
        normed, inverse = normalize(tiles)
        live = live_ref[at, :][:, :1]
        mine, other = pmine_ref[at, :], pother_ref[at, :]
        low, high = jnp.where(first, mine, other), jnp.where(first, other, mine)
        layer_out[at, :DH] = (tiles[:, :DH] + low * live).astype(bf16)
        layer_out[at, DH:] = (tiles[:, DH:] + high * live).astype(bf16)
        grad_hidden = gmine_ref[at, :].astype(f32) + gother_ref[at, :].astype(f32)
        grad_norm = inverse * (
            grad_hidden
            - jnp.mean(grad_hidden, axis=-1, keepdims=True)
            - normed * jnp.mean(grad_hidden * normed, axis=-1, keepdims=True)
        )
        tiles_out[at, :] = (grad_ref[at, :].astype(f32) + grad_norm).astype(bf16)


def layer_kernel(
    place_ref, packed, hidden, amine_ref, aother_ref, gmine_ref, gother_ref, rmine_ref, rother_ref,
    attn_out, grads_out, c0, c1, c2, c3, grad_own,
    grad_attn, dk, dv, attn, dq, tissue, lines_f32,
):
    base, core, column = place_ref[0], place_ref[1], place_ref[2]
    width = 2 * QUERY_COLS
    span = 8 * KEY_COLS
    half = KEY_ROWS // 2 * KEY_COLS
    half_q = QUERY_ROWS // 2 * QUERY_COLS
    contract = (((1,), (1,)), ((), ()))
    over = (((0,), (0,)), ((), ()))
    part = D // 4

    dk[...] = jnp.zeros_like(dk)
    dv[...] = jnp.zeros_like(dv)

    mine_lanes = pl.ds(pl.multiple_of(core * DH, DH), DH)
    other_lanes = pl.ds(pl.multiple_of((1 - core) * DH, DH), DH)
    rmine = rmine_ref[pl.ds(pl.multiple_of(core * HALF, HALF), HALF), :]
    for source, side in ((gmine_ref, core), (gother_ref, 1 - core)):
        to = pl.ds(pl.multiple_of(side * half_q, 8), half_q)
        total = lax.dot_general(source[:, mine_lanes], rmine, contract, preferred_element_type=f32)
        total += lax.dot_general(source[:, other_lanes], rother_ref[...], contract, preferred_element_type=f32)
        grad_attn[to, :] = total[:half_q].astype(bf16).astype(f32)

    for source, side in ((gmine_ref, core), (gother_ref, 1 - core)):
        lines_f32[...] = source[:, mine_lanes].astype(f32)
        for r in range(8):
            own = lines_f32[pl.ds(pl.multiple_of((1 - side) * 72 + 24 * r, 8), SIDE), :]
            grad_own[pl.ds(pl.multiple_of((side * 8 + r) * SIDE, SIDE), SIDE), :] = own.astype(bf16)

    for source, side in ((amine_ref, core), (aother_ref, 1 - core)):
        tissue[pl.ds(pl.multiple_of(side * half, 64), half), :] = source[:, D:].astype(f32)
    alive_line = jnp.concatenate(
        [jnp.transpose(tissue[m * LANE : (m + 1) * LANE, :])[:8] for m in range(7)] + [jnp.zeros((8, LANE), f32)], axis=1
    )
    alive_line = jnp.where(alive_line > 0, open_score, masked_score)
    spot = lax.broadcasted_iota(jnp.int32, (QUERY_COLS, span), 1) % KEY_COLS
    key_col = jnp.where(spot < 16, spot, jnp.where(spot < 20, spot - 20, jnp.where(spot < 24, spot - 28, spot - 8)))
    spot = lax.broadcasted_iota(jnp.int32, (QUERY_COLS, span), 0)
    query_col = jnp.where(spot < 16, spot, jnp.where(spot < 20, spot - 20, spot - 4))
    col_start = jnp.clip(query_col + column - 3, 0, GRID - WINDOW)
    key_col = key_col + column
    col_in = jnp.logical_and(key_col >= col_start, key_col < col_start + WINDOW)
    col_cap = jnp.where(col_in, open_score, outside_score)

    key_line = lax.broadcasted_iota(jnp.int32, (1, span), 1) // KEY_COLS
    low = lax.broadcasted_iota(jnp.int32, (width, LANE), 1) < HEAD_DIM
    low2 = jnp.concatenate([low, jnp.logical_not(low)], axis=0)
    upper = lax.broadcasted_iota(jnp.int32, (8, LANE), 0) < 4

    def block(i, carry):
        row = base - 3 + 2 * i
        start = jnp.clip(row - 3, 0, GRID - 8)
        local = start - (base - 6)
        alive = pltpu.roll(alive_line, lax.rem((32 - local) * KEY_COLS, 32 * KEY_COLS), 1)[:1, :span]
        key_row = key_line + start
        caps = []
        for step in range(2):
            first = jnp.clip(row + step - 3, 0, GRID - WINDOW)
            inside = jnp.logical_and(key_row >= first, key_row < first + WINDOW)
            caps.append(jnp.minimum(col_cap, jnp.where(inside, alive, outside_score)))
        cap = jnp.concatenate(caps + caps, axis=0)
        keys_at = pl.ds(pl.multiple_of(local * KEY_COLS, KEY_COLS), span)
        query_at = pl.multiple_of((3 + 2 * i) * KEY_COLS, KEY_COLS)
        block_at = pl.ds(pl.multiple_of(i * width, width), width)
        groups = range(3)
        lanes = [pl.ds(g * LANE, LANE) for g in groups]
        key = [packed[keys_at, pl.ds(HALF + g * LANE, LANE)] for g in groups]
        value = [packed[keys_at, pl.ds(2 * HALF + g * LANE, LANE)] for g in groups]
        query2, grad2f = [], []
        for g in groups:
            lines = packed[pl.ds(query_at, 2 * KEY_COLS), lanes[g]].astype(f32) * HEAD_DIM ** (-0.5)
            pieces = []
            for step in range(2):
                line = lines[step * KEY_COLS : (step + 1) * KEY_COLS]
                pieces += [line[:SIDE], jnp.where(upper, line[16:24], pltpu.roll(line[24:32], 4, 0))]
            query2.append(jnp.where(low2, jnp.concatenate(pieces + pieces, axis=0), 0.0).astype(bf16))
            grad = grad_attn[block_at, lanes[g]]
            grad2f.append(jnp.where(low2, jnp.concatenate([grad, grad], axis=0), 0.0))
        grad2 = [g.astype(bf16) for g in grad2f]
        raw = [lax.dot_general(query2[g], key[g], contract, preferred_element_type=f32) for g in groups]
        grad_prob = [lax.dot_general(grad2[g], value[g], contract, preferred_element_type=f32) for g in groups]
        prob = []
        for g in groups:
            scores = jnp.minimum(raw[g], cap)
            expon = jnp.exp(scores - jnp.max(scores, axis=1, keepdims=True))
            prob.append(expon * (1.0 / jnp.sum(expon, axis=1, keepdims=True)))
        weights = [p.astype(bf16) for p in prob]
        mixed = [jnp.dot(weights[g], value[g], preferred_element_type=f32).astype(bf16).astype(f32) for g in groups]
        value_sum = [lax.dot_general(weights[g], grad2[g], over, preferred_element_type=f32) for g in groups]
        delta = [jnp.sum(grad2f[g] * mixed[g], axis=1, keepdims=True) for g in groups]
        grad_score = [(prob[g] * (grad_prob[g] - delta[g])).astype(bf16) for g in groups]
        grad_q = [jnp.dot(grad_score[g], key[g], preferred_element_type=f32) for g in groups]
        key_sum = [lax.dot_general(grad_score[g], query2[g], over, preferred_element_type=f32) for g in groups]
        for g in groups:
            attn[block_at, lanes[g]] = jnp.where(low, mixed[g][:width], mixed[g][width:])
            dq[block_at, lanes[g]] = jnp.where(low, grad_q[g][:width], grad_q[g][width:])
            dv[keys_at, lanes[g]] += value_sum[g]
            dk[keys_at, lanes[g]] += key_sum[g]
        return carry

    lax.fori_loop(0, QUERY_ROWS // 2, block, 0, unroll=True)
    for r in range(SIDE):
        own = pl.ds(r * SIDE, SIDE)
        at_query = pl.ds((r + 3) * QUERY_COLS, SIDE)
        at_key = pl.ds((r + 6) * KEY_COLS, SIDE)
        attn_out[own, :] = attn[at_query, :].astype(bf16)
        grads_out[own, :HALF] = (dq[at_query, :] * HEAD_DIM ** (-0.5)).astype(bf16)
        grads_out[own, HALF : 2 * HALF] = dk[at_key, :].astype(bf16)
        grads_out[own, 2 * HALF :] = dv[at_key, :].astype(bf16)
    for k, chunk in enumerate((c0, c1, c2, c3)):
        chunk[...] = lax.dot_general(
            hidden[:, k * part : (k + 1) * part], grads_out[...], over, preferred_element_type=f32
        ).astype(bf16)


def layer(place, *arrays):
    keys, queries = KEY_ROWS * KEY_COLS, QUERY_ROWS * QUERY_COLS
    return on_chip(
        layer_kernel,
        place,
        arrays,
        [((SIDE * SIDE, HALF), bf16), ((SIDE * SIDE, 3 * HALF), bf16)] + [((D // 4, 3 * HALF), bf16)] * 4 + [((SIDE * SIDE, DH), bf16)],
        [
            ((queries, HALF), f32),
            ((keys, HALF), f32),
            ((keys, HALF), f32),
            ((queries, HALF), f32),
            ((queries, HALF), f32),
            ((keys, LANE), f32),
            ((288, DH), f32),
        ],
        30,
    )


def found_places(core, here, place):
    step = [(place // 24) % 4, (place // 96) % 4, place // 384]
    found = {}
    for name in ("x", "y", "z"):
        mine = [lax.rem(here[name] - step[STAGES[c].index(name)] + 4, 4) for c in range(2)]
        found[name] = jnp.where(core == 0, mine[0], mine[1])
    return found


def orders(core, here, place):
    found, inner = found_places(core, here, place), place % 24

    def owner(side):
        return (((found["z"] // 2 * 4 + found["y"]) * 2 + side) * 2 + found["z"] % 2) * 4 + found["x"]

    feature = owner(inner // 12) * 12 + inner % 12
    row = owner(inner % 12 // 6) * 6 + inner % 6 + inner // 12 * DH
    return feature, row


def body(tiles, tissue, project_in, project_out, grad_layer):
    zh, y, core, zl, x = [lax.axis_index(name) for name in AXES]
    z = zh * 2 + zl
    tokens = 8 * SIDE
    place = jnp.stack([(zh * 4 + y) * SIDE, core, (zl * 4 + x) * SIDE]).astype(jnp.int32)

    halves = project_in.reshape(12, 3, 2, HALF)
    first, second = halves[:, :, 0].reshape(12, 3 * HALF), halves[:, :, 1].reshape(12, 3 * HALF)

    def shard(of_in, of_out):
        return jnp.concatenate([of_in, of_out.reshape(6, 2, HALF).transpose(1, 0, 2).reshape(12, HALF)], axis=1)

    shard_first, shard_second = shard(first, project_out[:, :DH]), shard(second, project_out[:, DH:])
    mine = jnp.where(core == 0, shard_first, shard_second)
    theirs = jnp.where(core == 0, shard_second, shard_first)
    other = swap_cores(theirs)
    here = {"x": x, "y": y, "z": z}
    feature_line, row_line = orders(core, here, lax.broadcasted_iota(jnp.int32, (1, D), 1))
    flat_tiles, flat_grad = tiles.reshape(tokens, D), grad_layer.reshape(tokens, D)
    live = jnp.broadcast_to(tissue.reshape(tokens, 1).astype(f32), (tokens, LANE))
    own_hidden, own_grad, sent = on_chip(
        prepare_kernel,
        place,
        [flat_tiles, flat_grad, live],
        [((tokens, WIDE), bf16), ((tokens, WIDE), bf16), ((144, WIDE), bf16)],
    )
    block_in = by_core(core, mine[:, : 3 * HALF], other[:, : 3 * HALF], 0)
    mine_out, other_out = mine[:, 3 * HALF :].reshape(2, 6, HALF), other[:, 3 * HALF :].reshape(2, 6, HALF)
    block_out = by_core(core, mine_out, other_out, 1).reshape(24, HALF)
    block = jnp.concatenate([block_in, block_out], axis=1)
    block, sent, feature_line, row_line = lax.optimization_barrier((block, sent, feature_line, row_line))

    parts = gather_stage(block, 0)
    got = row_neighbour(sent)
    *parts, got = lax.optimization_barrier((*parts, got))
    block = jnp.concatenate(parts, axis=0)
    a, b, to_right, to_left = on_chip(
        columns_kernel,
        place,
        [own_hidden, own_grad, got],
        [((224, WIDE), bf16), ((192, WIDE), bf16), ((160, WIDE), bf16), ((160, WIDE), bf16)],
    )
    block, to_right, to_left = lax.optimization_barrier((block, to_right, to_left))

    parts = gather_stage(block, 1)
    left, right = col_neighbour(to_right, 1), col_neighbour(to_left, -1)
    block = lax.optimization_barrier(jnp.concatenate(parts, axis=0))

    near, back = gather_ring(block)
    wide_a, wide_b = on_chip(
        widen_kernel, place, [a, b, left, right], [((14 * KEY_COLS, WIDE), bf16), ((12 * QUERY_COLS, WIDE), bf16)]
    )
    other_a, other_b = swap_cores(wide_a), swap_cores(wide_b)
    permuted = [((14 * KEY_COLS, D), bf16)]
    (hidden_mine,) = on_chip(permute_kernel, place, [wide_a, feature_line], permuted)
    (hidden_other,) = on_chip(permute_kernel, place, [other_a, feature_line], permuted)

    hidden_mine, near, back = lax.optimization_barrier((hidden_mine, near, back))
    weights = [block, near, *relay_ring(near, back), back]
    hidden_other, row_line = lax.optimization_barrier((hidden_other, row_line))
    (near_rows,) = on_chip(near_rows_kernel, place, [block, near, back, row_line], [((DH, DH), f32)], [((3, D // 4, DH), bf16)])
    half_out, sent_rows = on_chip(
        out_rows_kernel,
        place,
        [near_rows, weights[2], weights[3], row_line],
        [((DH, DH), bf16), ((HALF, DH), bf16)],
        [((D // 4, DH), bf16)],
    )
    other_rows = swap_cores(sent_rows)
    packed, hidden = on_chip(
        packed_kernel,
        place,
        [hidden_mine, hidden_other, *weights],
        [((KEY_ROWS * KEY_COLS, 3 * HALF), bf16), ((SIDE * SIDE, D), bf16)],
        [((D, 3 * HALF), bf16)],
    )

    attention, grad_packed, *chunks_in, grad_own = layer(
        place, packed, hidden, wide_a, other_a, wide_b, other_b, half_out, other_rows
    )
    axes = (STAGES[0][2], STAGES[1][2])
    far, near, back = shifted(chunks_in[2], axes, 2), shifted(chunks_in[1], axes, 3), shifted(chunks_in[3], axes, 1)

    attention_other = swap_cores(attention)
    hidden_kept, hidden_sent = on_chip(
        grad_hidden_kernel,
        place,
        [grad_packed, *weights, feature_line],
        [((tokens, D), bf16)] * 2,
        [((2 * tokens, D), bf16)],
    )
    attention_other, hidden_kept, hidden_sent = lax.optimization_barrier((attention_other, hidden_kept, hidden_sent))
    chunks_out = on_chip(
        out_grads_kernel,
        place,
        [attention, attention_other, grad_own, row_line],
        [((D // 4, HALF), bf16)] * 4,
    )
    projected, projected_sent = on_chip(
        project_kernel, place, [attention, attention_other, half_out], [((tokens, DH), f32)] * 2
    )
    far_out, near_out = shifted(chunks_out[2], axes, 2), shifted(chunks_out[1], axes, 3)
    total_in, back_out = lax.optimization_barrier((chunks_in[0].astype(f32) + near.astype(f32), chunks_out[3]))
    back_out = shifted(back_out, axes, 1)
    total_in = total_in + (far.astype(f32) + back.astype(f32))
    total_out = (chunks_out[0].astype(f32) + near_out.astype(f32)) + (far_out.astype(f32) + back_out.astype(f32))
    total = jnp.concatenate([total_in, total_out], axis=1).astype(bf16)
    total, hidden_kept, hidden_sent, projected, projected_sent = lax.optimization_barrier(
        (total, hidden_kept, hidden_sent, projected, projected_sent)
    )
    total = scatter_stage([total[k * 96 : (k + 1) * 96] for k in range(4)], 1).astype(bf16)
    layer_out, grad_tiles = on_chip(
        finish_kernel,
        place,
        [flat_tiles, flat_grad, live, projected, swap_cores(projected_sent), hidden_kept, swap_cores(hidden_sent)],
        [((tokens, D), bf16)] * 2,
    )
    axes = (STAGES[0][0], STAGES[1][0])
    own, to_near, to_far, to_back = [total[k * 24 : (k + 1) * 24] for k in range(4)]
    parts = [own, shifted(to_near, axes, 3), shifted(to_far, axes, 2), shifted(to_back, axes, 1)]
    kept, sent = on_chip(last_sum_kernel, place, parts, [((12, D), f32)] * 2)
    gotten = swap_cores(sent)
    gotten, layer_out, grad_tiles = lax.optimization_barrier((gotten, layer_out, grad_tiles))
    grad_project_in, grad_project_out = on_chip(
        unpack_kernel, place, [kept, gotten], [((12, 3 * DH), f32), ((6, D), f32)]
    )

    return (
        layer_out.reshape(8, SIDE, D),
        grad_tiles.reshape(8, SIDE, D),
        grad_project_in,
        grad_project_out,
    )


def solution(mesh):
    fine = Mesh(mesh.devices.reshape(2, 4, 2, 2, 4), AXES)
    grid = P(("zh", "y", "c"), ("zl", "x"), None)
    rows = P(AXES, None)
    return jax.shard_map(
        body,
        mesh=fine,
        in_specs=(grid, P(("zh", "y", "c"), ("zl", "x")), rows, rows, grid),
        out_specs=(grid, grid, rows, rows),
        check_vma=False,
    )
```
